512 devices in a mesh: flow: 64 (over x, z), trans: 8 (over y, core).
Axes of the slice: x: 4, y: 4, z: 16, core: 2. Of those that a mesh axis runs over, the one named last changes fastest.
Arguments:
- basis_flux: bfloat16 [64, 1024, 1024], P('flow', 'trans'), may hold values from -0.125 to 0.125
- owner_cell: int32 [64, 1024], P('flow', 'trans'), may hold values from 0 to 1023
- clogged: int32 [64, 1024], P('flow', 'trans'), may hold values 0 or 1
- conductance: float32 [64, 1024], P('flow', 'trans'), may hold values from 0.1 to 1
- live_count: int32 [64, 8], P('flow', 'trans'), may hold values from 32 to 128
- coupling: float32 [64, 1024], P('flow'), may hold values from 1.8 to 2
- leakage: float32 [64, 1024], P('flow'), may hold values from 0.02 to 0.08
- source: float32 [64, 1024], P('flow'), may hold values from -6 to 6
Outputs:
- pressure: float32 [64, 1024], P('flow', 'trans')
The draws below stay inside these ranges and needn't reach their ends.
All inputs are finite; a program needn't handle non-finite values. No bound on the sum of `clogged` on one device may be relied on, other than what follows from the above.
Results may differ from the reference program's by a relative error of at most 0.0003.
The reference program's roundings to bfloat16 on the way count: a program that leaves them out, or rounds other values in their place, can miss the bound.
Values may be sent and summed in bfloat16 or wider, within the bound.
A program may use at most 64 MiB of HBM per device.

```python
import math
import jax
import jax.numpy as jnp
from jax import lax

COARSE = 1024
NF = 128
PLANES = 64
SLAB_ALL = 1024
N_TRANS = 8


def draw_basis_flux(key, part):
    key = jax.random.fold_in(key, 11)
    spread = 1.0 / math.sqrt(SLAB_ALL)
    dims = (PLANES, SLAB_ALL, COARSE)
    normal_part = jax.random.normal(key, dims, jnp.float32)
    values = 3.984 * spread * jnp.clip(normal_part / 3.984, -1.0, 1.0)
    return values.astype(jnp.bfloat16)


def place_ends(array, rng, least, high):
    index_at = [jax.random.randint(jax.random.fold_in(rng, axis), (), 0, length) for axis, length in enumerate(array.shape)]
    longest = array.shape.index(max(array.shape))
    next_to = index_at[:longest] + [(index_at[longest] + 1) % array.shape[longest]] + index_at[longest + 1:]
    return array.at[tuple(index_at)].set(least).at[tuple(next_to)].set(high)


def block_levels(rng, shape, cuts, smallest, top_value):
    gain, own = 1.0, jax.random.fold_in(rng, 6)
    for dim, shards_of in cuts:
        steps = jnp.exp(jax.random.uniform(jax.random.fold_in(own, dim), (shards_of,), jnp.float32, smallest / len(cuts), top_value / len(cuts)))
        gain = gain * jnp.repeat(steps, shape[dim] // shards_of).reshape([-1 if axis == dim else 1 for axis in range(len(shape))])
    return gain


def centred(own_key, shape, deviation, reach, pieces=(), held_as=jnp.bfloat16):
    drawn = deviation * jax.random.normal(own_key, shape, jnp.float32)
    if pieces:
        drawn = drawn * block_levels(own_key, shape, pieces, -0.22, 0.18)
    return jnp.clip(drawn, -reach, reach).astype(held_as)


def setup_inputs(seed: int = 0) -> dict:
    seeds = jax.random.split(jax.random.key(seed), 9)
    return {
        "basis_flux": draw_basis_flux(jax.random.fold_in(seeds[8], 71), 0),
        "owner_cell": place_ends(jax.random.randint(seeds[1], (PLANES, SLAB_ALL), 0, COARSE), jax.random.fold_in(seeds[1], 1), 0, COARSE - 1).astype(jnp.int32),
        "clogged": place_ends((jax.random.randint(seeds[2], (PLANES, SLAB_ALL), 0, 4) < 1).astype(jnp.int32), jax.random.fold_in(seeds[2], 1), 0, 1),
        "conductance": jnp.clip(jnp.exp(math.log(1.0) - 2.3025851 * jax.random.uniform(seeds[3], (PLANES, SLAB_ALL), jnp.float32) ** block_levels(seeds[3], (PLANES, SLAB_ALL), ((0, 64), (1, 8)), -0.2, 0.2)), 0.1, 1.0),
        "live_count": place_ends(jax.random.randint(seeds[4], (PLANES, N_TRANS), NF // 4, NF + 1), jax.random.fold_in(seeds[4], 1), NF // 4, NF).astype(jnp.int32),
        "coupling": jnp.clip(jnp.exp(math.log(2.0) - 0.105360542 * jax.random.uniform(seeds[5], (PLANES, COARSE), jnp.float32) ** block_levels(seeds[5], (PLANES, COARSE), ((0, 64),), -0.2, 0.2)), 1.8, 2.0),
        "leakage": jnp.clip(jnp.exp(math.log(0.08) - 1.3862944 * jax.random.uniform(seeds[6], (PLANES, COARSE), jnp.float32) ** block_levels(seeds[6], (PLANES, COARSE), ((0, 64),), -0.2, 0.2)), 0.02, 0.08),
        "source": centred(seeds[7], (PLANES, COARSE), 1.0, 6.0, ((0, 64),), jnp.float32),
    }


def reference(basis_flux, owner_cell, clogged, conductance, live_count, coupling, leakage, source):
    position = jnp.arange(N_TRANS * NF, dtype=jnp.int32)
    slab_index = position // NF
    within = position % NF
    live_rows = (within[None, :] < live_count[:, slab_index]).astype(jnp.float32)
    weights = (conductance * (1 - clogged).astype(jnp.float32) * live_rows).astype(jnp.bfloat16)

    def assemble(packed):
        flux_rows, owners, weight_rows = packed
        scaled = weight_rows.astype(jnp.float32)[:, None] * flux_rows.astype(jnp.float32)
        return jax.ops.segment_sum(scaled, owners, num_segments=COARSE)

    blocks = lax.map(assemble, (basis_flux, owner_cell, weights))
    flux_diag = jnp.diagonal(blocks, axis1=1, axis2=2)
    schur_term = coupling * coupling / (coupling + leakage + flux_diag)
    zero_row = jnp.zeros((1, COARSE), jnp.float32)
    upstream_face = jnp.concatenate([zero_row, coupling[:-1]], axis=0)
    upstream_schur = jnp.concatenate([zero_row, schur_term[:-1]], axis=0)
    diag_total = leakage + coupling + upstream_face - upstream_schur

    def invert(packed):
        flux_block, diag_extra = packed
        system = flux_block + jnp.diag(diag_extra)
        pivots = 1.0 / jnp.diagonal(system)
        first_sweep = 2.0 * jnp.diag(pivots) - pivots[:, None] * system * pivots[None, :]
        left_product = jnp.dot(first_sweep, system, precision=lax.Precision.HIGHEST, preferred_element_type=jnp.float32)
        return 2.0 * first_sweep - jnp.dot(left_product, first_sweep, precision=lax.Precision.HIGHEST, preferred_element_type=jnp.float32)

    inverses = lax.map(invert, (blocks, diag_total))

    def forward(incoming, packed):
        inverse, face_row, source_row = packed
        forward_state = source_row + incoming
        outgoing = face_row * jnp.dot(inverse, forward_state, precision=lax.Precision.HIGHEST, preferred_element_type=jnp.float32)
        return outgoing, forward_state

    unused, levels = lax.scan(forward, jnp.zeros((COARSE,), jnp.float32), (inverses, coupling, source))

    def backward(incoming, packed):
        inverse, face_row, forward_state = packed
        solved = jnp.dot(inverse, forward_state + face_row * incoming, precision=lax.Precision.HIGHEST, preferred_element_type=jnp.float32)
        return solved, solved

    unused_back, pressure = lax.scan(backward, jnp.zeros((COARSE,), jnp.float32), (inverses, coupling, levels), reverse=True)
    return pressure
```

```python
import functools

import jax
import jax.numpy as jnp
from jax import lax
from jax.experimental import pallas as pl
from jax.experimental.pallas import tpu as pltpu
from jax.sharding import PartitionSpec as P

MESH = pl.DeviceIdType.MESH
BF16 = jnp.bfloat16
F32 = jnp.float32
VMEM_LIMIT = 56 * 1024 * 1024


def dot(left, right):
    return jnp.dot(left, right, preferred_element_type=F32)


def split(value):
    high = value.astype(BF16)
    return high, (value - high.astype(F32)).astype(BF16)


def neighbours(plane, planes):
    return jnp.where(plane > 0, 1, 0) + jnp.where(plane < planes - 1, 1, 0)


def setup_kernel(
    planes, chips, rows, order,
    basis, owner, clogged, conductance, live, coupling, leakage,
    near_high, near_low, inverse_diag,
    slabs, packs, picked, block, gain_high, gain_low, square, faces, faces_in, flux_diag,
    slab_send, slab_recv, pack_send, pack_recv, face_send, face_recv,
):
    plane = lax.axis_index("flow")
    me = lax.axis_index("trans")
    parts = 2 * chips
    chip, core = me // 2, lax.rem(me, 2)
    partner = chip * 2 + 1 - core
    step_rows = 256
    steps = order // step_rows

    barrier = pltpu.get_barrier_semaphore()
    for turn in range(1, parts):
        pl.semaphore_signal(
            barrier, inc=1, device_id=(plane, lax.rem(me + turn, parts)), device_id_type=MESH
        )

    @pl.when(plane > 0)
    def _():
        pl.semaphore_signal(barrier, inc=1, device_id=(plane - 1, me), device_id_type=MESH)

    @pl.when(plane < planes - 1)
    def _():
        pl.semaphore_signal(barrier, inc=1, device_id=(plane + 1, me), device_id_type=MESH)

    def slab(index):
        return slabs.at[:, pl.ds(pl.multiple_of(index * rows, rows), rows)]

    position = lax.broadcasted_iota(jnp.int32, (1, rows), 1)
    weight = (
        conductance[...]
        * (1 - clogged[...]).astype(F32)
        * (position < live[...]).astype(F32)
    ).astype(BF16).astype(F32)
    row_id = lax.broadcasted_iota(jnp.int32, (8, rows), 0)
    packs[me] = jnp.where(row_id == 0, weight, owner[...].astype(F32))
    slabs[:, pl.ds(pl.multiple_of(me * rows, rows), rows)] = basis[0].astype(F32).T.astype(BF16)

    pl.semaphore_wait(barrier, parts - 1 + neighbours(plane, planes))

    def slab_copy(index, target, slot):
        return pltpu.make_async_remote_copy(
            slab(index), slab(index), slab_send.at[slot], slab_recv.at[index],
            device_id=(plane, target), device_id_type=MESH,
        )

    def pack_copy(index, target, slot):
        return pltpu.make_async_remote_copy(
            packs.at[index], packs.at[index], pack_send.at[slot], pack_recv.at[index],
            device_id=(plane, target), device_id_type=MESH,
        )

    others = [lax.rem(me + turn, parts) for turn in range(1, parts)]
    for slot, target in enumerate(others):
        pack_copy(me, target, slot).start()
    away = [lax.rem(chip + turn, chips) * 2 + core for turn in (1, chips - 1, *range(2, chips - 1))]
    for slot, target in enumerate(away):
        slab_copy(me, target, slot).start()
    slab_copy(me, partner, chips - 1).start()

    column = lax.broadcasted_iota(jnp.int32, (rows, order), 1).astype(F32)

    def pick(index, carry):
        turned = packs[index].T
        picked[pl.ds(pl.multiple_of(index * rows, rows), rows), :] = jnp.where(
            turned[:, 1:2] == column, turned[:, 0:1], 0.0
        ).astype(BF16)
        return carry

    for source in others:
        pack_copy(source, partner, 0).wait_recv()
    lax.fori_loop(0, parts, pick, 0)

    for slot, source in enumerate(away):
        slab_copy(source, partner, 0).wait_recv()
        slab_copy(source, partner, chips + slot).start()
    slab_copy(partner, partner, 0).wait_recv()
    for source in away:
        slab_copy(source + 1 - 2 * core, partner, 0).wait_recv()

    eye = lax.broadcasted_iota(jnp.int32, (rows, rows), 0) == lax.broadcasted_iota(
        jnp.int32, (rows, rows), 1
    )
    for index in range(order // rows):
        here = pl.ds(index * rows, rows)
        flux_diag[:, here] = jnp.sum(
            jnp.where(eye, dot(slabs[here, :], picked[:, here]), 0.0), axis=0, keepdims=True
        )

    face = coupling[...]
    leak = leakage[...]
    schur = face * face / (face + leak + flux_diag[...])
    faces[0:1, :] = face
    faces[1:2, :] = schur

    def face_copy(target):
        return pltpu.make_async_remote_copy(
            faces, faces_in, face_send, face_recv, device_id=(target, me), device_id_type=MESH
        )

    @pl.when(plane < planes - 1)
    def _():
        face_copy(plane + 1).start()

    def assemble(index, carry):
        here = pl.ds(pl.multiple_of(index * step_rows, step_rows), step_rows)
        block[here, :] = dot(slabs[here, :], picked[...])
        return carry

    lax.fori_loop(0, steps, assemble, 0)

    @pl.when(plane > 0)
    def _():
        face_copy(plane).wait_recv()

    @pl.when(plane == 0)
    def _():
        faces_in[...] = jnp.zeros_like(faces_in)

    diag = flux_diag[...] + (leak + face + faces_in[0:1, :] - faces_in[1:2, :])
    pivots = 1.0 / diag
    inverse_diag[...] = pivots

    across = lax.broadcasted_iota(jnp.int32, (step_rows, order), 1)
    down = lax.broadcasted_iota(jnp.int32, (step_rows, order), 0)

    def scale(index, carry):
        here = pl.ds(pl.multiple_of(index * step_rows, step_rows), step_rows)
        gain = jnp.where(across == down + index * step_rows, 0.0, block[here, :] * pivots)
        block[here, :] = gain
        gain_high[here, :], gain_low[here, :] = split(gain)
        return carry

    lax.fori_loop(0, steps, scale, 0)

    def squared(index, carry):
        here = pl.ds(pl.multiple_of(index * step_rows, step_rows), step_rows)
        high, low = gain_high[here, :], gain_low[here, :]
        value = dot(high, gain_high[...]) + (dot(high, gain_low[...]) + dot(low, gain_high[...]))
        square[here, :] = value.astype(BF16)
        block[here, :] = value - block[here, :]
        return carry

    lax.fori_loop(0, steps, squared, 0)

    def finish(index, carry):
        here = pl.ds(pl.multiple_of(index * step_rows, step_rows), step_rows)
        near = block[here, :] - dot(gain_high[here, :], square[...])
        near_high[here, :], near_low[here, :] = split(near)
        return carry

    lax.fori_loop(0, steps, finish, 0)

    for slot, target in enumerate(others):
        pack_copy(me, target, slot).wait_send()
    for slot, target in enumerate(away):
        slab_copy(me, target, slot).wait_send()
        slab_copy(target, partner, chips + slot).wait_send()
    slab_copy(me, partner, chips - 1).wait_send()

    @pl.when(plane < planes - 1)
    def _():
        face_copy(plane + 1).wait_send()


def chain_kernel(
    planes, rows, order,
    near_high, near_low, inverse_diag, coupling, source,
    pressure,
    level, sent, received, answer, band_in, send_sem, recv_sem, band_send, band_recv,
):
    plane = lax.axis_index("flow")
    me = lax.axis_index("trans")
    core = lax.rem(me, 2)
    partner = me + 1 - 2 * core
    row_id = lax.broadcasted_iota(jnp.int32, (8, order), 0)

    def apply(value):
        scaled = value * inverse_diag[...]
        high, low = split(scaled)
        both = jnp.where(
            row_id == 0, high.astype(F32), jnp.where(row_id == 1, low.astype(F32), 0.0)
        ).astype(BF16)
        gathered = dot(both, near_high[...]) + dot(both, near_low[...])
        return scaled + jnp.sum(gathered, axis=0, keepdims=True)

    barrier = pltpu.get_barrier_semaphore()
    pl.semaphore_signal(barrier, inc=1, device_id=(plane, partner), device_id_type=MESH)

    def step_copy(way, target):
        return pltpu.make_async_remote_copy(
            sent.at[way], received.at[way], send_sem.at[way], recv_sem.at[way],
            device_id=(target, me), device_id_type=MESH,
        )

    band_copy = pltpu.make_async_remote_copy(
        answer.at[:, pl.ds(pl.multiple_of(partner * rows, rows), rows)], band_in,
        band_send, band_recv, device_id=(plane, partner), device_id_type=MESH,
    )

    @pl.when(core == 0)
    def _():
        pl.semaphore_wait(barrier, 1)
        band_copy.wait_recv()
        pressure[...] = band_in[...]

    @pl.when(core == 1)
    def _():
        @pl.when(plane > 0)
        def _():
            pl.semaphore_signal(barrier, inc=1, device_id=(plane - 1, me), device_id_type=MESH)

        @pl.when(plane < planes - 1)
        def _():
            pl.semaphore_signal(barrier, inc=1, device_id=(plane + 1, me), device_id_type=MESH)

        pl.semaphore_wait(barrier, 1 + neighbours(plane, planes))

        level[...] = source[...]

        @pl.when(plane > 0)
        def _():
            step_copy(0, plane).wait_recv()
            level[...] = source[...] + received[0]

        @pl.when(plane < planes - 1)
        def _():
            sent[0] = coupling[...] * apply(level[...])
            step_copy(0, plane + 1).start()
            step_copy(1, plane).wait_recv()
            level[...] = level[...] + coupling[...] * received[1]

        answer[...] = apply(level[...])

        @pl.when(plane > 0)
        def _():
            sent[1] = answer[...]
            step_copy(1, plane - 1).start()

        band_copy.start()
        pressure[...] = answer[:, pl.ds(pl.multiple_of(me * rows, rows), rows)]

        @pl.when(plane < planes - 1)
        def _():
            step_copy(0, plane + 1).wait_send()

        @pl.when(plane > 0)
        def _():
            step_copy(1, plane - 1).wait_send()

        band_copy.wait_send()


def per_device(basis_flux, owner_cell, clogged, conductance, live_count, coupling, leakage, source):
    planes = lax.axis_size("flow")
    parts = lax.axis_size("trans")
    chips = parts // 2
    rows, order = basis_flux.shape[1:]
    vmem = pl.BlockSpec(memory_space=pltpu.VMEM)
    dma = pltpu.SemaphoreType.DMA
    matrix = jax.ShapeDtypeStruct((order, order), BF16)
    near_high, near_low, inverse_diag = pl.pallas_call(
        functools.partial(setup_kernel, planes, chips, rows, order),
        out_shape=(matrix, matrix, jax.ShapeDtypeStruct((1, order), F32)),
        in_specs=[vmem] * 7,
        out_specs=(vmem,) * 3,
        scratch_shapes=[
            pltpu.VMEM((order, parts * rows), BF16),
            pltpu.VMEM((parts, 8, rows), F32),
            pltpu.VMEM((parts * rows, order), BF16),
            pltpu.VMEM((order, order), F32),
            pltpu.VMEM((order, order), BF16),
            pltpu.VMEM((order, order), BF16),
            pltpu.VMEM((order, order), BF16),
            pltpu.VMEM((2, order), F32),
            pltpu.VMEM((2, order), F32),
            pltpu.VMEM((1, order), F32),
            dma((parts,)), dma((parts,)), dma((parts,)), dma((parts,)), dma, dma,
        ],
        compiler_params=pltpu.CompilerParams(
            collective_id=0, has_side_effects=True, vmem_limit_bytes=VMEM_LIMIT
        ),
    )(basis_flux, owner_cell, clogged, conductance, live_count, coupling, leakage)
    return pl.pallas_call(
        functools.partial(chain_kernel, planes, rows, order),
        out_shape=jax.ShapeDtypeStruct((1, rows), F32),
        in_specs=[vmem] * 5,
        out_specs=vmem,
        scratch_shapes=[
            pltpu.VMEM((1, order), F32),
            pltpu.VMEM((2, 1, order), F32),
            pltpu.VMEM((2, 1, order), F32),
            pltpu.VMEM((1, order), F32),
            pltpu.VMEM((1, rows), F32),
            dma((2,)), dma((2,)), dma, dma,
        ],
        compiler_params=pltpu.CompilerParams(
            collective_id=1, has_side_effects=True, vmem_limit_bytes=VMEM_LIMIT
        ),
    )(near_high, near_low, inverse_diag, coupling, source)


def solution(mesh):
    placed = (
        P("flow", "trans", None),
        P("flow", "trans"),
        P("flow", "trans"),
        P("flow", "trans"),
        P("flow", "trans"),
        P("flow", None),
        P("flow", None),
        P("flow", None),
    )
    return jax.shard_map(
        per_device, mesh=mesh, in_specs=placed, out_specs=P("flow", "trans"), check_vma=False
    )
```

```python
import functools

import jax
import jax.numpy as jnp
from jax import lax
from jax.experimental import pallas as pl
from jax.experimental.pallas import tpu as pltpu
from jax.sharding import PartitionSpec as P

MESH = pl.DeviceIdType.MESH
BF16 = jnp.bfloat16
F32 = jnp.float32
VMEM_LIMIT = 56 * 1024 * 1024


def dot(left, right):
    return jnp.dot(left, right, preferred_element_type=F32)


def split(value):
    high = value.astype(BF16)
    return high, (value - high.astype(F32)).astype(BF16)


def neighbours(plane, planes):
    return jnp.where(plane > 0, 1, 0) + jnp.where(plane < planes - 1, 1, 0)


def setup_kernel(
    planes, chips, rows, order,
    basis, owner, clogged, conductance, live, coupling, leakage,
    near_high, near_low, inverse_diag,
    slabs, packs, picked, block, gain_high, gain_low, square, faces, faces_in, flux_diag,
    slab_send, slab_recv, pack_send, pack_recv, face_send, face_recv,
):
    plane = lax.axis_index("flow")
    me = lax.axis_index("trans")
    parts = 2 * chips
    chip, core = me // 2, lax.rem(me, 2)
    partner = chip * 2 + 1 - core
    step_rows = 256
    steps = order // step_rows

    barrier = pltpu.get_barrier_semaphore()
    for turn in range(1, parts):
        pl.semaphore_signal(
            barrier, inc=1, device_id=(plane, lax.rem(me + turn, parts)), device_id_type=MESH
        )

    @pl.when(plane > 0)
    def _():
        pl.semaphore_signal(barrier, inc=1, device_id=(plane - 1, me), device_id_type=MESH)

    @pl.when(plane < planes - 1)
    def _():
        pl.semaphore_signal(barrier, inc=1, device_id=(plane + 1, me), device_id_type=MESH)

    def slab(index):
        return slabs.at[:, pl.ds(pl.multiple_of(index * rows, rows), rows)]

    position = lax.broadcasted_iota(jnp.int32, (1, rows), 1)
    weight = (
        conductance[...]
        * (1 - clogged[...]).astype(F32)
        * (position < live[...]).astype(F32)
    ).astype(BF16).astype(F32)
    row_id = lax.broadcasted_iota(jnp.int32, (8, rows), 0)
    packs[me] = jnp.where(row_id == 0, weight, owner[...].astype(F32))
    slabs[:, pl.ds(pl.multiple_of(me * rows, rows), rows)] = basis[0].astype(F32).T.astype(BF16)

    pl.semaphore_wait(barrier, parts - 1 + neighbours(plane, planes))

    def slab_copy(index, target, slot):
        return pltpu.make_async_remote_copy(
            slab(index), slab(index), slab_send.at[slot], slab_recv.at[index],
            device_id=(plane, target), device_id_type=MESH,
        )

    def pack_copy(index, target, slot):
        return pltpu.make_async_remote_copy(
            packs.at[index], packs.at[index], pack_send.at[slot], pack_recv.at[index],
            device_id=(plane, target), device_id_type=MESH,
        )

    others = [lax.rem(me + turn, parts) for turn in range(1, parts)]
    for slot, target in enumerate(others):
        pack_copy(me, target, slot).start()
    away = [lax.rem(chip + turn, chips) * 2 + core for turn in (1, chips - 1, *range(2, chips - 1))]
    for slot, target in enumerate(away):
        slab_copy(me, target, slot).start()
    slab_copy(me, partner, chips - 1).start()

    column = lax.broadcasted_iota(jnp.int32, (rows, order), 1).astype(F32)

    def pick(index, carry):
        turned = packs[index].T
        picked[pl.ds(pl.multiple_of(index * rows, rows), rows), :] = jnp.where(
            turned[:, 1:2] == column, turned[:, 0:1], 0.0
        ).astype(BF16)
        return carry

    for source in others:
        pack_copy(source, partner, 0).wait_recv()
    lax.fori_loop(0, parts, pick, 0)

    for slot, source in enumerate(away):
        slab_copy(source, partner, 0).wait_recv()
        slab_copy(source, partner, chips + slot).start()
    slab_copy(partner, partner, 0).wait_recv()
    for source in away:
        slab_copy(source + 1 - 2 * core, partner, 0).wait_recv()

    eye = lax.broadcasted_iota(jnp.int32, (rows, rows), 0) == lax.broadcasted_iota(
        jnp.int32, (rows, rows), 1
    )
    for index in range(order // rows):
        here = pl.ds(index * rows, rows)
        flux_diag[:, here] = jnp.sum(
            jnp.where(eye, dot(slabs[here, :], picked[:, here]), 0.0), axis=0, keepdims=True
        )

    face = coupling[...]
    leak = leakage[...]
    schur = face * face / (face + leak + flux_diag[...])
    faces[0:1, :] = face
    faces[1:2, :] = schur

    def face_copy(target):
        return pltpu.make_async_remote_copy(
            faces, faces_in, face_send, face_recv, device_id=(target, me), device_id_type=MESH
        )

    @pl.when(plane < planes - 1)
    def _():
        face_copy(plane + 1).start()

    def assemble(index, carry):
        here = pl.ds(pl.multiple_of(index * step_rows, step_rows), step_rows)
        block[here, :] = dot(slabs[here, :], picked[...])
        return carry

    lax.fori_loop(0, steps, assemble, 0)

    @pl.when(plane > 0)
    def _():
        face_copy(plane).wait_recv()

    @pl.when(plane == 0)
    def _():
        faces_in[...] = jnp.zeros_like(faces_in)

    diag = flux_diag[...] + (leak + face + faces_in[0:1, :] - faces_in[1:2, :])
    pivots = 1.0 / diag
    inverse_diag[...] = pivots

    across = lax.broadcasted_iota(jnp.int32, (step_rows, order), 1)
    down = lax.broadcasted_iota(jnp.int32, (step_rows, order), 0)

    def scale(index, carry):
        here = pl.ds(pl.multiple_of(index * step_rows, step_rows), step_rows)
        gain = jnp.where(across == down + index * step_rows, 0.0, block[here, :] * pivots)
        block[here, :] = gain
        gain_high[here, :], gain_low[here, :] = split(gain)
        return carry

    lax.fori_loop(0, steps, scale, 0)

    def squared(index, carry):
        here = pl.ds(pl.multiple_of(index * step_rows, step_rows), step_rows)
        high, low = gain_high[here, :], gain_low[here, :]
        value = dot(high, gain_high[...]) + (dot(high, gain_low[...]) + dot(low, gain_high[...]))
        square[here, :] = value.astype(BF16)
        block[here, :] = value - block[here, :]
        return carry

    lax.fori_loop(0, steps, squared, 0)

    def finish(index, carry):
        here = pl.ds(pl.multiple_of(index * step_rows, step_rows), step_rows)
        near = block[here, :] - dot(gain_high[here, :], square[...])
        near_high[here, :], near_low[here, :] = split(near)
        return carry

    lax.fori_loop(0, steps, finish, 0)

    for slot, target in enumerate(others):
        pack_copy(me, target, slot).wait_send()
    for slot, target in enumerate(away):
        slab_copy(me, target, slot).wait_send()
        slab_copy(target, partner, chips + slot).wait_send()
    slab_copy(me, partner, chips - 1).wait_send()

    @pl.when(plane < planes - 1)
    def _():
        face_copy(plane + 1).wait_send()


def chain_kernel(
    planes, span, chips, rows, order, depth,
    near_high, near_low, inverse_diag, coupling, source,
    pressure,
    panel_in, panel_out, back_in, back_out, back_held,
    panel_high, panel_low, last_high, last_low, back_high, back_low,
    level, parts_out, level_out, level_in, up_pieces, down_pieces, end_pieces, end_out,
    edge_up, edge_down, swept_in, swept, band_out, band_in,
    panel_send, panel_recv, held_send, held_recv, up_send, up_recv, down_send, down_recv,
    edge_send, edge_recv, level_send, level_recv, sweep_send, sweep_recv,
    end_send, end_recv, band_send, band_recv,
):
    plane = lax.axis_index("flow")
    me = lax.axis_index("trans")
    chip, core = me // 2, lax.rem(me, 2)
    partner = me + 1 - 2 * core
    spans = planes // span
    row, spot = plane // span, lax.rem(plane, span)
    row_start = row * span
    last = span - 1
    width = order // chips
    turns = width // depth
    wide = width // rows
    first_column = pl.multiple_of(chip * width, width)
    face = coupling[...]
    other_chips = [lax.rem(chip + turn, chips) for turn in range(1, chips)]

    def remote(source_ref, target_ref, send, recv, target_plane, target):
        return pltpu.make_async_remote_copy(
            source_ref, target_ref, send, recv,
            device_id=(target_plane, target), device_id_type=MESH,
        )

    def apply(value):
        count = value.shape[0]
        scaled = value * inverse_diag[...]
        high = scaled.astype(BF16).astype(F32)
        both = jnp.concatenate([high, scaled - high], axis=0).astype(BF16)
        by_high = dot(both, near_high[...])
        by_low = dot(high.astype(BF16), near_low[...])
        return scaled + (by_high[:count] + (by_high[count:] + by_low))

    def two_rows(value):
        row_id = lax.broadcasted_iota(jnp.int32, (8, value.shape[1]), 0)
        high = value.astype(BF16).astype(F32)
        return jnp.where(row_id == 0, high, jnp.where(row_id == 1, value - high, 0.0)).astype(BF16)

    def apply_one(value):
        scaled = value * inverse_diag[...]
        both = two_rows(scaled)
        return scaled + jnp.sum(
            dot(both, near_high[...]) + dot(both, near_low[...]), axis=0, keepdims=True
        )

    def by_panel(value, high, low):
        both = two_rows(value)
        return jnp.sum(dot(both, high[...]) + dot(both, low[...]), axis=0, keepdims=True)

    def take(index):
        return pl.ds(pl.multiple_of(index * depth, depth), depth)

    barrier = pltpu.get_barrier_semaphore()

    def greet(target_plane, target):
        pl.semaphore_signal(barrier, inc=1, device_id=(target_plane, target), device_id_type=MESH)

    greet(plane, partner)
    inner = jnp.where(spot > 0, 1, 0) + jnp.where(spot < last, 1, 0)

    @pl.when(core == 0)
    def _():
        @pl.when(spot > 0)
        def _():
            greet(plane - 1, me)

        @pl.when(spot < last)
        def _():
            greet(plane + 1, me)

        pl.semaphore_wait(barrier, 1 + inner)

    at_end = jnp.logical_or(spot == 0, spot == last)

    @pl.when(core == 1)
    def _():
        for other in other_chips:
            greet(plane, other * 2 + 1)

        for place in range(span):
            if place in (0, last):
                meets = spot != place
            else:
                meets = jnp.logical_or(at_end, jnp.abs(spot - place) == 1)
                meets = jnp.logical_and(meets, spot != place)

            @pl.when(meets)
            def _():
                greet(row_start + place, me)

        for step, there in ((span, row < spans - 1), (-span, row > 0)):
            @pl.when(jnp.logical_and(at_end, there))
            def _():
                for other in range(chips):
                    greet(plane + step, other * 2 + 1)

        beside = jnp.logical_or(spot == 1, spot == last - 1)
        along = jnp.where(at_end, last, jnp.where(beside, 3, 4))
        across = jnp.where(row > 0, chips, 0) + jnp.where(row < spans - 1, chips, 0)
        pl.semaphore_wait(barrier, chips + along + jnp.where(at_end, across, 0))

    one_hot_row = lax.broadcasted_iota(jnp.int32, (depth, order), 0)
    one_hot_column = lax.broadcasted_iota(jnp.int32, (depth, order), 1)

    def unit_rows(index):
        return jnp.where(
            one_hot_column == one_hot_row + (chip * width + index * depth), 1.0, 0.0
        )

    def back_copy(index):
        return remote(
            back_out.at[take(index), :], back_in.at[take(index), :],
            panel_send.at[index], panel_recv.at[index], plane - 1, me,
        )

    def held_copy(index):
        return remote(
            back_out.at[take(index), :], back_held.at[take(index), :],
            held_send.at[index], held_recv.at[index], plane, partner,
        )

    band_copy = remote(band_out, band_in, band_send, band_recv, plane, partner)

    @pl.when(core == 0)
    def _():
        def flow(index, carry):
            @pl.when(spot == last)
            def _():
                back_in[take(index), :] = unit_rows(index)

            @pl.when(spot < last)
            def _():
                back_copy(index).wait_recv()

            back_out[take(index), :] = apply(face * back_in[take(index), :])

            @pl.when(spot > 0)
            def _():
                back_copy(index).start()

            held_copy(index).start()
            return carry

        lax.fori_loop(0, turns, flow, 0)

        def drain(index, carry):
            @pl.when(spot > 0)
            def _():
                back_copy(index).wait_send()

            held_copy(index).wait_send()
            return carry

        lax.fori_loop(0, turns, drain, 0)
        band_copy.wait_recv()
        pressure[...] = band_in[...]

    def panel_copy(index):
        return remote(
            panel_out.at[take(index), :], panel_in.at[take(index), :],
            panel_send.at[index], panel_recv.at[index], plane + 1, me,
        )

    def up_copy(target):
        return remote(
            parts_out.at[target], up_pieces.at[chip],
            up_send.at[target], up_recv.at[chip], plane + span, target * 2 + 1,
        )

    def down_copy(target):
        return remote(
            parts_out.at[target], down_pieces.at[chip],
            down_send.at[target], down_recv.at[chip], plane - span, target * 2 + 1,
        )

    def edge_copy(way, ref, place):
        return remote(
            ref, ref, edge_send.at[way, place], edge_recv.at[way], row_start + place, me
        )

    def level_copy(target, slot):
        return remote(
            level_out, level_in.at[chip], level_send.at[slot], level_recv.at[chip],
            plane, target * 2 + 1,
        )

    def end_copy(target, slot):
        return remote(
            end_out.at[target], end_pieces.at[chip], end_send.at[slot], end_recv.at[chip],
            plane, target * 2 + 1,
        )

    sweep_copy = remote(swept, swept_in, sweep_send, sweep_recv, plane - 1, me)

    def cut(value, ref):
        for index in range(chips):
            ref[index] = value[:, index * width : (index + 1) * width]

    @pl.when(core == 1)
    def _():
        def flow(turn, carry):
            index = lax.rem(turn + turns, turns + 1)

            @pl.when(spot == 0)
            def _():
                panel_in[take(index), :] = unit_rows(index)

            @pl.when(spot > 0)
            def _():
                panel_copy(index).wait_recv()

            @pl.when(turn == 0)
            def _():
                @pl.when(spot == 0)
                def _():
                    panel_in[take(index), :] = jnp.zeros((depth, order), F32)

                panel_in[take(index), :] = panel_in[take(index), :] + jnp.where(
                    one_hot_row == 0, source[...], 0.0
                )

            panel_out[take(index), :] = face * apply(panel_in[take(index), :])

            @pl.when(spot < last)
            def _():
                panel_copy(index).start()

            return carry

        lax.fori_loop(0, turns + 1, flow, 0)
        panel_high[...], panel_low[...] = split(panel_in[0:width, :])
        level[...] = panel_in[width : width + 1, :]

        @pl.when(spot == last)
        def _():
            last_high[...], last_low[...] = split(panel_out[0:width, :])

            @pl.when(row > 0)
            def _():
                for target in range(chips):
                    remote(
                        parts_out.at[target], up_pieces.at[target],
                        up_send.at[target], up_recv.at[target], plane, me,
                    ).wait_recv()
                edge_up[...] = (up_pieces[0] + up_pieces[1]) + (up_pieces[2] + up_pieces[3])

            @pl.when(row == 0)
            def _():
                edge_up[...] = jnp.zeros_like(edge_up)

            @pl.when(row < spans - 1)
            def _():
                cut(by_panel(edge_up[...], last_high, last_low), parts_out)
                parts_out[chip] = parts_out[chip] + panel_out[
                    width : width + 1, pl.ds(first_column, width)
                ]
                for target in range(chips):
                    up_copy(target).start()

            @pl.when(row > 0)
            def _():
                for place in range(last - 1, -1, -1):
                    edge_copy(0, edge_up, place).start()

        @pl.when(row > 0)
        def _():
            @pl.when(spot < last)
            def _():
                edge_copy(0, edge_up, 0).wait_recv()

            level_out[...] = by_panel(edge_up[...], panel_high, panel_low)
            for slot, other in enumerate(other_chips):
                level_copy(other, slot).start()
            level_in[chip] = level_out[...]
            for other in other_chips:
                remote(
                    level_out, level_in.at[other], level_send.at[0], level_recv.at[other],
                    plane, me,
                ).wait_recv()
            level[...] = level[...] + ((level_in[0] + level_in[1]) + (level_in[2] + level_in[3]))

        @pl.when(spot < last)
        def _():
            sweep_copy.wait_recv()
            level[...] = level[...] + face * swept_in[...]

        swept[...] = apply_one(level[...])

        @pl.when(spot > 0)
        def _():
            sweep_copy.start()

        def arrived(index, carry):
            held_copy(index).wait_recv()
            return carry

        lax.fori_loop(0, turns, arrived, 0)
        back_high[...], back_low[...] = split(back_held[...])

        @pl.when(jnp.logical_and(spot == last, row < spans - 1))
        def _():
            for target in range(chips):
                up_copy(target).wait_send()

        @pl.when(spot == 0)
        def _():
            @pl.when(row < spans - 1)
            def _():
                for target in range(chips):
                    remote(
                        parts_out.at[target], down_pieces.at[target],
                        down_send.at[target], down_recv.at[target], plane, me,
                    ).wait_recv()
                edge_down[...] = (down_pieces[0] + down_pieces[1]) + (
                    down_pieces[2] + down_pieces[3]
                )

            @pl.when(row == spans - 1)
            def _():
                edge_down[...] = jnp.zeros_like(edge_down)

            @pl.when(row > 0)
            def _():
                cut(by_panel(edge_down[...], back_high, back_low), parts_out)
                parts_out[chip] = parts_out[chip] + swept[:, pl.ds(first_column, width)]
                for target in range(chips):
                    down_copy(target).start()

            @pl.when(row < spans - 1)
            def _():
                for place in range(1, span):
                    edge_copy(1, edge_down, place).start()

        end_pieces[chip] = jnp.zeros((1, width), F32)

        @pl.when(row < spans - 1)
        def _():
            @pl.when(spot > 0)
            def _():
                edge_copy(1, edge_down, 0).wait_recv()

            cut(by_panel(edge_down[...], back_high, back_low), end_out)
            for slot, other in enumerate(other_chips):
                end_copy(other, slot).start()
            end_pieces[chip] = end_out[chip]
            for other in other_chips:
                remote(
                    end_out.at[other], end_pieces.at[other], end_send.at[0], end_recv.at[other],
                    plane, me,
                ).wait_recv()
            end_pieces[chip] = (end_pieces[0] + end_pieces[1]) + (end_pieces[2] + end_pieces[3])

        answer = end_pieces[chip] + swept[:, pl.ds(first_column, width)]
        band_out[...] = answer[:, 0:rows]
        band_copy.start()
        pressure[...] = answer[:, rows:width]

        @pl.when(spot < last)
        def _():
            def drain(index, carry):
                panel_copy(index).wait_send()
                return carry

            lax.fori_loop(0, turns + 1, drain, 0)

        @pl.when(row > 0)
        def _():
            for slot, other in enumerate(other_chips):
                level_copy(other, slot).wait_send()

            @pl.when(spot == last)
            def _():
                for place in range(last):
                    edge_copy(0, edge_up, place).wait_send()

            @pl.when(spot == 0)
            def _():
                for target in range(chips):
                    down_copy(target).wait_send()

        @pl.when(row < spans - 1)
        def _():
            for slot, other in enumerate(other_chips):
                end_copy(other, slot).wait_send()

            @pl.when(spot == 0)
            def _():
                for place in range(1, span):
                    edge_copy(1, edge_down, place).wait_send()

        @pl.when(spot > 0)
        def _():
            sweep_copy.wait_send()

        band_copy.wait_send()


def per_device(basis_flux, owner_cell, clogged, conductance, live_count, coupling, leakage, source):
    planes = lax.axis_size("flow")
    parts = lax.axis_size("trans")
    chips = parts // 2
    rows, order = basis_flux.shape[1:]
    vmem = pl.BlockSpec(memory_space=pltpu.VMEM)
    dma = pltpu.SemaphoreType.DMA
    matrix = jax.ShapeDtypeStruct((order, order), BF16)
    near_high, near_low, inverse_diag = pl.pallas_call(
        functools.partial(setup_kernel, planes, chips, rows, order),
        out_shape=(matrix, matrix, jax.ShapeDtypeStruct((1, order), F32)),
        in_specs=[vmem] * 7,
        out_specs=(vmem,) * 3,
        scratch_shapes=[
            pltpu.VMEM((order, parts * rows), BF16),
            pltpu.VMEM((parts, 8, rows), F32),
            pltpu.VMEM((parts * rows, order), BF16),
            pltpu.VMEM((order, order), F32),
            pltpu.VMEM((order, order), BF16),
            pltpu.VMEM((order, order), BF16),
            pltpu.VMEM((order, order), BF16),
            pltpu.VMEM((2, order), F32),
            pltpu.VMEM((2, order), F32),
            pltpu.VMEM((1, order), F32),
            dma((parts,)), dma((parts,)), dma((parts,)), dma((parts,)), dma, dma,
        ],
        compiler_params=pltpu.CompilerParams(
            collective_id=0, has_side_effects=True, vmem_limit_bytes=VMEM_LIMIT
        ),
    )(basis_flux, owner_cell, clogged, conductance, live_count, coupling, leakage)
    span, depth = planes // 4, 16
    width = order // chips
    turns = width // depth
    row = (1, order)
    piece = (1, width)
    return pl.pallas_call(
        functools.partial(chain_kernel, planes, span, chips, rows, order, depth),
        out_shape=jax.ShapeDtypeStruct((1, rows), F32),
        in_specs=[vmem] * 5,
        out_specs=vmem,
        scratch_shapes=[
            pltpu.VMEM((width + depth, order), F32),
            pltpu.VMEM((width + depth, order), F32),
            pltpu.VMEM((width, order), F32),
            pltpu.VMEM((width, order), F32),
            pltpu.VMEM((width, order), F32),
            *[pltpu.VMEM((width, order), BF16) for _ in range(6)],
            pltpu.VMEM(row, F32),
            pltpu.VMEM((chips, *piece), F32),
            pltpu.VMEM(row, F32),
            pltpu.VMEM((chips, *row), F32),
            *[pltpu.VMEM((chips, *piece), F32) for _ in range(4)],
            pltpu.VMEM(piece, F32),
            pltpu.VMEM(piece, F32),
            pltpu.VMEM(row, F32),
            pltpu.VMEM(row, F32),
            pltpu.VMEM((1, rows), F32),
            pltpu.VMEM((1, rows), F32),
            dma((turns + 1,)), dma((turns + 1,)), dma((turns,)), dma((turns,)),
            dma((chips,)), dma((chips,)), dma((chips,)), dma((chips,)),
            dma((2, span)), dma((2,)), dma((chips,)), dma((chips,)), dma, dma,
            dma((chips,)), dma((chips,)), dma, dma,
        ],
        compiler_params=pltpu.CompilerParams(
            collective_id=1, has_side_effects=True, vmem_limit_bytes=VMEM_LIMIT
        ),
    )(near_high, near_low, inverse_diag, coupling, source)


def solution(mesh):
    placed = (
        P("flow", "trans", None),
        P("flow", "trans"),
        P("flow", "trans"),
        P("flow", "trans"),
        P("flow", "trans"),
        P("flow", None),
        P("flow", None),
        P("flow", None),
    )
    return jax.shard_map(
        per_device, mesh=mesh, in_specs=placed, out_specs=P("flow", "trans"), check_vma=False
    )
```

```python
import functools

import jax
import jax.numpy as jnp
from jax import lax
from jax.experimental import pallas as pl
from jax.experimental.pallas import tpu as pltpu
from jax.sharding import PartitionSpec as P

MESH = pl.DeviceIdType.MESH
BF16 = jnp.bfloat16
F32 = jnp.float32
VMEM_LIMIT = 56 * 1024 * 1024


def dot(left, right):
    return jnp.dot(left, right, preferred_element_type=F32)


def split(value):
    high = value.astype(BF16)
    return high, (value - high.astype(F32)).astype(BF16)


def kernel(
    planes, span, chips, rows, order, depth,
    basis, owner, clogged, conductance, live, coupling, leakage, source,
    pressure,
    near_high, near_low, inverse_diag,
    slabs, packs, picked, block, gain_high, gain_low, square, faces, faces_in, flux_diag,
    panel_in, panel_out, back_in, back_out, back_held, low_in, low_out, low_held,
    panel_high, panel_low, last_high, last_low, back_high, back_low, low_high, low_low,
    level, parts_out, level_out, level_in, up_pieces, down_pieces, end_pieces, end_out,
    edge_up, edge_down, edge_mid, total, swept_in, swept, band_out, band_in,
    slab_send, slab_recv, pack_send, pack_recv, face_send, face_recv,
    panel_send, panel_recv, held_send, held_recv, low_send, low_recv, lowheld_send, lowheld_recv,
    up_send, up_recv, down_send, down_recv,
    edge_send, edge_recv, level_send, level_recv, sweep_send, sweep_recv,
    end_send, end_recv, band_send, band_recv,
):
    plane = lax.axis_index("flow")
    me = lax.axis_index("trans")
    parts = 2 * chips
    chip, core = me // 2, lax.rem(me, 2)
    partner = me + 1 - 2 * core
    spans = planes // span
    row, spot = plane // span, lax.rem(plane, span)
    row_start = row * span
    last = span - 1
    width = order // chips
    turns = width // depth
    middle = span // 2
    up_turns = jnp.where(row > 0, turns + 1, 1)
    down_turns = jnp.where(row < spans - 1, turns, 0)
    first_column = pl.multiple_of(chip * width, width)
    face = coupling[...]
    other_chips = [lax.rem(chip + turn, chips) for turn in range(1, chips)]
    step_rows = 256
    steps = order // step_rows

    barrier = pltpu.get_barrier_semaphore()

    def greet(target_plane, target):
        pl.semaphore_signal(barrier, inc=1, device_id=(target_plane, target), device_id_type=MESH)

    at_end = jnp.logical_or(spot == 0, spot == last)
    for turn in range(1, parts):
        greet(plane, lax.rem(me + turn, parts))

    @pl.when(plane > 0)
    def _():
        greet(plane - 1, me)

    @pl.when(plane < planes - 1)
    def _():
        greet(plane + 1, me)

    @pl.when(core == 1)
    def _():
        for step, there in ((span, row < spans - 1), (-span, row > 0)):
            @pl.when(jnp.logical_and(at_end, there))
            def _():
                for other in range(chips):
                    greet(plane + step, other * 2 + 1)

    def slab(index):
        return slabs.at[:, pl.ds(pl.multiple_of(index * rows, rows), rows)]

    position = lax.broadcasted_iota(jnp.int32, (1, rows), 1)
    weight = (
        conductance[...]
        * (1 - clogged[...]).astype(F32)
        * (position < live[...]).astype(F32)
    ).astype(BF16).astype(F32)
    row_id = lax.broadcasted_iota(jnp.int32, (8, rows), 0)
    packs[me] = jnp.where(row_id == 0, weight, owner[...].astype(F32))
    slabs[:, pl.ds(pl.multiple_of(me * rows, rows), rows)] = basis[0].astype(F32).T.astype(BF16)

    next_to = jnp.where(plane > 0, 1, 0) + jnp.where(plane < planes - 1, 1, 0)
    across = jnp.where(row > 0, chips, 0) + jnp.where(row < spans - 1, chips, 0)
    extra = jnp.where(at_end, across, 0)
    pl.semaphore_wait(barrier, parts - 1 + next_to + jnp.where(core == 1, extra, 0))

    def slab_copy(index, target, slot):
        return pltpu.make_async_remote_copy(
            slab(index), slab(index), slab_send.at[slot], slab_recv.at[index],
            device_id=(plane, target), device_id_type=MESH,
        )

    def pack_copy(index, target, slot):
        return pltpu.make_async_remote_copy(
            packs.at[index], packs.at[index], pack_send.at[slot], pack_recv.at[index],
            device_id=(plane, target), device_id_type=MESH,
        )

    others = [lax.rem(me + turn, parts) for turn in range(1, parts)]
    for slot, target in enumerate(others):
        pack_copy(me, target, slot).start()
    way = 1 - 2 * core
    ahead = lax.rem(chip + way + chips, chips) * 2 + core
    behind = lax.rem(chip - way + chips, chips) * 2 + core
    across_ring = lax.rem(chip + 2, chips) * 2 + core
    slab_copy(me, ahead, 0).start()
    slab_copy(me, behind, 1).start()
    slab_copy(me, partner, 2).start()

    column = lax.broadcasted_iota(jnp.int32, (rows, order), 1).astype(F32)

    def pick(index, carry):
        turned = packs[index].T
        picked[pl.ds(pl.multiple_of(index * rows, rows), rows), :] = jnp.where(
            turned[:, 1:2] == column, turned[:, 0:1], 0.0
        ).astype(BF16)
        return carry

    for other in others:
        pack_copy(other, partner, 0).wait_recv()
    lax.fori_loop(0, parts, pick, 0)

    slab_copy(behind, partner, 0).wait_recv()
    slab_copy(behind, ahead, 3).start()
    slab_copy(behind, partner, 4).start()
    slab_copy(ahead, partner, 0).wait_recv()
    slab_copy(ahead, partner, 5).start()
    slab_copy(across_ring, partner, 0).wait_recv()
    slab_copy(across_ring, partner, 6).start()
    slab_copy(partner, partner, 0).wait_recv()
    flip = 1 - 2 * core
    for source_slab in (behind, ahead, across_ring):
        slab_copy(source_slab + flip, partner, 0).wait_recv()

    eye = lax.broadcasted_iota(jnp.int32, (rows, rows), 0) == lax.broadcasted_iota(
        jnp.int32, (rows, rows), 1
    )
    for index in range(order // rows):
        here = pl.ds(index * rows, rows)
        flux_diag[:, here] = jnp.sum(
            jnp.where(eye, dot(slabs[here, :], picked[:, here]), 0.0), axis=0, keepdims=True
        )

    leak = leakage[...]
    schur = face * face / (face + leak + flux_diag[...])
    faces[0:1, :] = face
    faces[1:2, :] = schur

    def face_copy(target):
        return pltpu.make_async_remote_copy(
            faces, faces_in, face_send, face_recv, device_id=(target, me), device_id_type=MESH
        )

    @pl.when(plane < planes - 1)
    def _():
        face_copy(plane + 1).start()

    def assemble(index, carry):
        here = pl.ds(pl.multiple_of(index * step_rows, step_rows), step_rows)
        block[here, :] = dot(slabs[here, :], picked[...])
        return carry

    lax.fori_loop(0, steps, assemble, 0)

    @pl.when(plane > 0)
    def _():
        face_copy(plane).wait_recv()

    @pl.when(plane == 0)
    def _():
        faces_in[...] = jnp.zeros_like(faces_in)

    diag = flux_diag[...] + (leak + face + faces_in[0:1, :] - faces_in[1:2, :])
    pivots = 1.0 / diag
    inverse_diag[...] = pivots

    across = lax.broadcasted_iota(jnp.int32, (step_rows, order), 1)
    down = lax.broadcasted_iota(jnp.int32, (step_rows, order), 0)

    def scale(index, carry):
        here = pl.ds(pl.multiple_of(index * step_rows, step_rows), step_rows)
        gain = jnp.where(across == down + index * step_rows, 0.0, block[here, :] * pivots)
        block[here, :] = gain
        gain_high[here, :], gain_low[here, :] = split(gain)
        return carry

    lax.fori_loop(0, steps, scale, 0)

    def squared(index, carry):
        here = pl.ds(pl.multiple_of(index * step_rows, step_rows), step_rows)
        high, low = gain_high[here, :], gain_low[here, :]
        value = dot(high, gain_high[...]) + (dot(high, gain_low[...]) + dot(low, gain_high[...]))
        square[here, :] = value.astype(BF16)
        block[here, :] = value - block[here, :]
        return carry

    lax.fori_loop(0, steps, squared, 0)

    def finish(index, carry):
        here = pl.ds(pl.multiple_of(index * step_rows, step_rows), step_rows)
        near = block[here, :] - dot(gain_high[here, :], square[...])
        near_high[here, :], near_low[here, :] = split(near)
        return carry

    lax.fori_loop(0, steps, finish, 0)

    for slot, target in enumerate(others):
        pack_copy(me, target, slot).wait_send()
    slab_copy(me, ahead, 0).wait_send()
    slab_copy(me, behind, 1).wait_send()
    slab_copy(me, partner, 2).wait_send()
    slab_copy(behind, ahead, 3).wait_send()
    slab_copy(behind, partner, 4).wait_send()
    slab_copy(ahead, partner, 5).wait_send()
    slab_copy(across_ring, partner, 6).wait_send()

    @pl.when(plane < planes - 1)
    def _():
        face_copy(plane + 1).wait_send()

    def remote(source_ref, target_ref, send, recv, target_plane, target):
        return pltpu.make_async_remote_copy(
            source_ref, target_ref, send, recv,
            device_id=(target_plane, target), device_id_type=MESH,
        )

    def apply(value):
        count = value.shape[0]
        scaled = value * inverse_diag[...]
        high = scaled.astype(BF16).astype(F32)
        both = jnp.concatenate([high, scaled - high], axis=0).astype(BF16)
        by_high = dot(both, near_high[...])
        by_low = dot(high.astype(BF16), near_low[...])
        return scaled + (by_high[:count] + (by_high[count:] + by_low))

    def two_rows(value):
        row_id = lax.broadcasted_iota(jnp.int32, (8, value.shape[1]), 0)
        high = value.astype(BF16).astype(F32)
        return jnp.where(row_id == 0, high, jnp.where(row_id == 1, value - high, 0.0)).astype(BF16)

    def apply_one(value):
        scaled = value * inverse_diag[...]
        both = two_rows(scaled)
        return scaled + jnp.sum(
            dot(both, near_high[...]) + dot(both, near_low[...]), axis=0, keepdims=True
        )

    def by_panel(value, high, low):
        both = two_rows(value)
        return jnp.sum(dot(both, high[...]) + dot(both, low[...]), axis=0, keepdims=True)

    def take(index):
        return pl.ds(pl.multiple_of(index * depth, depth), depth)

    one_hot_row = lax.broadcasted_iota(jnp.int32, (depth, order), 0)
    one_hot_column = lax.broadcasted_iota(jnp.int32, (depth, order), 1)

    def unit_rows(index):
        return jnp.where(
            one_hot_column == one_hot_row + (chip * width + index * depth), 1.0, 0.0
        )

    def back_copy(index):
        return remote(
            back_out.at[take(index), :], back_in.at[take(index), :],
            panel_send.at[index], panel_recv.at[index], plane - 1, me,
        )

    def held_copy(index):
        return remote(
            back_out.at[take(index), :], back_held.at[take(index), :],
            held_send.at[index], held_recv.at[index], plane, partner,
        )

    band_copy = remote(band_out, band_in, band_send, band_recv, plane, partner)

    def low_copy(index):
        return remote(
            low_out.at[take(index), :], low_in.at[take(index), :],
            low_send.at[index], low_recv.at[index], plane - 1, me,
        )

    def lowheld_copy(index):
        return remote(
            low_out.at[take(index), :], low_held.at[take(index), :],
            lowheld_send.at[index], lowheld_recv.at[index], plane, partner,
        )

    @pl.when(core == 0)
    def _():
        def flow_down(top, came, went, pass_on, keep):
            def flow(index, carry):
                @pl.when(spot == top)
                def _():
                    came[take(index), :] = unit_rows(index)

                @pl.when(spot < top)
                def _():
                    pass_on(index).wait_recv()

                went[take(index), :] = apply(face * came[take(index), :])

                @pl.when(spot > 0)
                def _():
                    pass_on(index).start()

                keep(index).start()
                return carry

            return flow

        def drain(pass_on, keep):
            def wait(index, carry):
                @pl.when(spot > 0)
                def _():
                    pass_on(index).wait_send()

                keep(index).wait_send()
                return carry

            return wait

        @pl.when(spot < middle)
        def _():
            lax.fori_loop(
                0, turns, flow_down(middle - 1, low_in, low_out, low_copy, lowheld_copy), 0
            )

        lax.fori_loop(0, down_turns, flow_down(last, back_in, back_out, back_copy, held_copy), 0)

        @pl.when(spot < middle)
        def _():
            lax.fori_loop(0, turns, drain(low_copy, lowheld_copy), 0)

        lax.fori_loop(0, down_turns, drain(back_copy, held_copy), 0)
        band_copy.wait_recv()
        pressure[...] = band_in[...]

    def panel_copy(index):
        return remote(
            panel_out.at[take(index), :], panel_in.at[take(index), :],
            panel_send.at[index], panel_recv.at[index], plane + 1, me,
        )

    def up_copy(target):
        return remote(
            parts_out.at[target], up_pieces.at[chip],
            up_send.at[target], up_recv.at[chip], plane + span, target * 2 + 1,
        )

    def down_copy(target):
        return remote(
            parts_out.at[target], down_pieces.at[chip],
            down_send.at[target], down_recv.at[chip], plane - span, target * 2 + 1,
        )

    def edge_copy(way, ref, place):
        return remote(
            ref, ref, edge_send.at[way, place], edge_recv.at[way], row_start + place, me
        )

    def level_copy(target, slot):
        return remote(
            level_out, level_in.at[chip], level_send.at[slot], level_recv.at[chip],
            plane, target * 2 + 1,
        )

    def end_copy(target, slot):
        return remote(
            end_out.at[target], end_pieces.at[chip], end_send.at[slot], end_recv.at[chip],
            plane, target * 2 + 1,
        )

    sweep_copy = remote(swept, swept_in, sweep_send, sweep_recv, plane - 1, me)

    def cut(value, ref):
        for index in range(chips):
            ref[index] = value[:, index * width : (index + 1) * width]

    @pl.when(core == 1)
    def _():
        def flow(turn, carry):
            index = lax.rem(turn + turns, turns + 1)

            @pl.when(spot == 0)
            def _():
                panel_in[take(index), :] = unit_rows(index)

            @pl.when(spot > 0)
            def _():
                panel_copy(index).wait_recv()

            @pl.when(turn == 0)
            def _():
                @pl.when(spot == 0)
                def _():
                    panel_in[take(index), :] = jnp.zeros((depth, order), F32)

                panel_in[take(index), :] = panel_in[take(index), :] + jnp.where(
                    one_hot_row == 0, source[...], 0.0
                )

            arrived_rows = panel_in[take(index), :]
            moved = face * apply(arrived_rows)
            panel_out[take(index), :] = moved

            @pl.when(spot < last)
            def _():
                panel_copy(index).start()

            @pl.when(turn > 0)
            def _():
                panel_high[take(index), :], panel_low[take(index), :] = split(arrived_rows)

                @pl.when(spot == last)
                def _():
                    last_high[take(index), :], last_low[take(index), :] = split(moved)

            return carry

        lax.fori_loop(0, up_turns, flow, 0)
        level[...] = panel_in[width : width + 1, :]

        @pl.when(spot == last)
        def _():
            @pl.when(row > 0)
            def _():
                for target in range(chips):
                    remote(
                        parts_out.at[target], up_pieces.at[target],
                        up_send.at[target], up_recv.at[target], plane, me,
                    ).wait_recv()
                edge_up[...] = (up_pieces[0] + up_pieces[1]) + (up_pieces[2] + up_pieces[3])

            @pl.when(row == 0)
            def _():
                edge_up[...] = jnp.zeros_like(edge_up)

            @pl.when(row == 0)
            def _():
                parts_out[...] = jnp.zeros_like(parts_out)

            @pl.when(jnp.logical_and(row > 0, row < spans - 1))
            def _():
                cut(by_panel(edge_up[...], last_high, last_low), parts_out)

            @pl.when(row < spans - 1)
            def _():
                parts_out[chip] = parts_out[chip] + panel_out[
                    width : width + 1, pl.ds(first_column, width)
                ]
                for target in range(chips):
                    up_copy(target).start()

            @pl.when(row > 0)
            def _():
                for place in range(last - 1, -1, -1):
                    edge_copy(0, edge_up, place).start()

        @pl.when(row > 0)
        def _():
            @pl.when(spot < last)
            def _():
                edge_copy(0, edge_up, 0).wait_recv()

            level_out[...] = by_panel(edge_up[...], panel_high, panel_low)
            for slot, other in enumerate(other_chips):
                level_copy(other, slot).start()
            level_in[chip] = level_out[...]
            for other in other_chips:
                remote(
                    level_out, level_in.at[other], level_send.at[0], level_recv.at[other],
                    plane, me,
                ).wait_recv()
            level[...] = level[...] + ((level_in[0] + level_in[1]) + (level_in[2] + level_in[3]))

        @pl.when(jnp.logical_and(spot != last, spot != middle - 1))
        def _():
            sweep_copy.wait_recv()
            level[...] = level[...] + face * swept_in[...]

        swept[...] = apply_one(level[...])

        @pl.when(jnp.logical_and(spot != 0, spot != middle))
        def _():
            sweep_copy.start()

        @pl.when(spot == middle)
        def _():
            edge_mid[...] = swept[:, pl.ds(first_column, width)]
            for place in (0, *range(middle - 1, 0, -1)):
                edge_copy(2, edge_mid, place).start()

        def arrived(keep):
            def wait(index, carry):
                keep(index).wait_recv()
                return carry

            return wait

        total[...] = jnp.zeros_like(total)

        @pl.when(row < spans - 1)
        def _():
            lax.fori_loop(0, turns, arrived(held_copy), 0)
            back_high[...], back_low[...] = split(back_held[...])

        @pl.when(spot < middle)
        def _():
            lax.fori_loop(0, turns, arrived(lowheld_copy), 0)
            low_high[...], low_low[...] = split(low_held[...])
            edge_copy(2, edge_mid, 0).wait_recv()
            total[...] = by_panel(edge_mid[...], low_high, low_low)

        @pl.when(jnp.logical_and(spot == last, row < spans - 1))
        def _():
            for target in range(chips):
                up_copy(target).wait_send()

        @pl.when(row < spans - 1)
        def _():
            @pl.when(spot == 0)
            def _():
                for target in range(chips):
                    remote(
                        parts_out.at[target], down_pieces.at[target],
                        down_send.at[target], down_recv.at[target], plane, me,
                    ).wait_recv()
                edge_down[...] = (down_pieces[0] + down_pieces[1]) + (
                    down_pieces[2] + down_pieces[3]
                )

            @pl.when(spot > 0)
            def _():
                edge_copy(1, edge_down, 0).wait_recv()

            total[...] = total[...] + by_panel(edge_down[...], back_high, back_low)

        @pl.when(spot == 0)
        def _():
            @pl.when(row > 0)
            def _():
                cut(total[...], parts_out)
                parts_out[chip] = parts_out[chip] + swept[:, pl.ds(first_column, width)]
                for target in range(chips):
                    down_copy(target).start()

            @pl.when(row < spans - 1)
            def _():
                for place in range(1, span):
                    edge_copy(1, edge_down, place).start()

        end_pieces[chip] = jnp.zeros((1, width), F32)
        corrected = jnp.logical_or(row < spans - 1, spot < middle)

        @pl.when(corrected)
        def _():
            cut(total[...], end_out)
            for slot, other in enumerate(other_chips):
                end_copy(other, slot).start()
            end_pieces[chip] = end_out[chip]
            for other in other_chips:
                remote(
                    end_out.at[other], end_pieces.at[other], end_send.at[0], end_recv.at[other],
                    plane, me,
                ).wait_recv()
            end_pieces[chip] = (end_pieces[0] + end_pieces[1]) + (end_pieces[2] + end_pieces[3])

        answer = end_pieces[chip] + swept[:, pl.ds(first_column, width)]
        band_out[...] = answer[:, 0:rows]
        band_copy.start()
        pressure[...] = answer[:, rows:width]

        @pl.when(spot < last)
        def _():
            def drain(turn, carry):
                panel_copy(lax.rem(turn + turns, turns + 1)).wait_send()
                return carry

            lax.fori_loop(0, up_turns, drain, 0)

        @pl.when(row > 0)
        def _():
            for slot, other in enumerate(other_chips):
                level_copy(other, slot).wait_send()

            @pl.when(spot == last)
            def _():
                for place in range(last):
                    edge_copy(0, edge_up, place).wait_send()

            @pl.when(spot == 0)
            def _():
                for target in range(chips):
                    down_copy(target).wait_send()

        @pl.when(corrected)
        def _():
            for slot, other in enumerate(other_chips):
                end_copy(other, slot).wait_send()

        @pl.when(jnp.logical_and(row < spans - 1, spot == 0))
        def _():
            for place in range(1, span):
                edge_copy(1, edge_down, place).wait_send()

        @pl.when(spot == middle)
        def _():
            for place in range(middle):
                edge_copy(2, edge_mid, place).wait_send()

        @pl.when(jnp.logical_and(spot != 0, spot != middle))
        def _():
            sweep_copy.wait_send()

        band_copy.wait_send()


def per_device(basis_flux, owner_cell, clogged, conductance, live_count, coupling, leakage, source):
    planes = lax.axis_size("flow")
    parts = lax.axis_size("trans")
    chips = parts // 2
    rows, order = basis_flux.shape[1:]
    span, depth = planes // 4, 16
    width = order // chips
    turns = width // depth
    row = (1, order)
    piece = (1, width)
    vmem = pl.BlockSpec(memory_space=pltpu.VMEM)
    dma = pltpu.SemaphoreType.DMA
    half = pltpu.VMEM((order, order), BF16)
    return pl.pallas_call(
        functools.partial(kernel, planes, span, chips, rows, order, depth),
        out_shape=jax.ShapeDtypeStruct((1, rows), F32),
        in_specs=[vmem] * 8,
        out_specs=vmem,
        scratch_shapes=[
            half, half, pltpu.VMEM(row, F32),
            half,
            pltpu.VMEM((parts, 8, rows), F32),
            half,
            pltpu.VMEM((order, order), F32),
            half, half, half,
            pltpu.VMEM((2, order), F32),
            pltpu.VMEM((2, order), F32),
            pltpu.VMEM(row, F32),
            pltpu.VMEM((width + depth, order), F32),
            pltpu.VMEM((width + depth, order), F32),
            *[pltpu.VMEM((width, order), F32) for _ in range(6)],
            *[pltpu.VMEM((width, order), BF16) for _ in range(8)],
            pltpu.VMEM(row, F32),
            pltpu.VMEM((chips, *piece), F32),
            pltpu.VMEM(row, F32),
            pltpu.VMEM((chips, *row), F32),
            *[pltpu.VMEM((chips, *piece), F32) for _ in range(4)],
            pltpu.VMEM(piece, F32),
            pltpu.VMEM(piece, F32),
            pltpu.VMEM(piece, F32),
            pltpu.VMEM(row, F32),
            pltpu.VMEM(row, F32),
            pltpu.VMEM(row, F32),
            pltpu.VMEM((1, rows), F32),
            pltpu.VMEM((1, rows), F32),
            dma((parts,)), dma((parts,)), dma((parts,)), dma((parts,)), dma, dma,
            dma((turns + 1,)), dma((turns + 1,)), dma((turns,)), dma((turns,)),
            dma((turns,)), dma((turns,)), dma((turns,)), dma((turns,)),
            dma((chips,)), dma((chips,)), dma((chips,)), dma((chips,)),
            dma((3, span)), dma((3,)), dma((chips,)), dma((chips,)), dma, dma,
            dma((chips,)), dma((chips,)), dma, dma,
        ],
        compiler_params=pltpu.CompilerParams(
            collective_id=0, has_side_effects=True, vmem_limit_bytes=VMEM_LIMIT
        ),
    )(basis_flux, owner_cell, clogged, conductance, live_count, coupling, leakage, source)


def solution(mesh):
    placed = (
        P("flow", "trans", None),
        P("flow", "trans"),
        P("flow", "trans"),
        P("flow", "trans"),
        P("flow", "trans"),
        P("flow", None),
        P("flow", None),
        P("flow", None),
    )
    return jax.shard_map(
        per_device, mesh=mesh, in_specs=placed, out_specs=P("flow", "trans"), check_vma=False
    )
```

```python
import functools

import jax
import jax.numpy as jnp
from jax import lax
from jax.experimental import pallas as pl
from jax.experimental.pallas import tpu as pltpu
from jax.sharding import PartitionSpec as P

MESH = pl.DeviceIdType.MESH
BF16 = jnp.bfloat16
F32 = jnp.float32
VMEM_LIMIT = 56 * 1024 * 1024


def dot(left, right):
    return jnp.dot(left, right, preferred_element_type=F32)


def split(value):
    high = value.astype(BF16)
    return high, (value - high.astype(F32)).astype(BF16)


def kernel(
    planes, span, chips, rows, order, depth, tops,
    basis, owner, clogged, conductance, live, coupling, leakage, source,
    pressure,
    near_high, near_low, inverse_diag,
    slabs, packs, picked, block, gain_high, gain_low, square, faces, faces_in, flux_diag,
    panel_in, panel_out, back_in, back_out, back_high, back_low,
    panel_high, panel_low, last_high, last_low,
    level, parts_out, up_pieces, down_pieces, edge_pieces, end_pieces, end_out,
    edge_up, edges, total, swept_in, swept, system_diag,
    slab_send, slab_recv, pack_send, pack_recv, face_send, face_recv,
    panel_send, panel_recv, back_send, back_recv, held_send, held_recv,
    up_send, up_recv, down_send, down_recv,
    edge_send, edge_recv, mid_send, mid_recv, sweep_send, sweep_recv, end_send, end_recv,
):
    plane = lax.axis_index("flow")
    me = lax.axis_index("trans")
    parts = 2 * chips
    chip, core = me // 2, lax.rem(me, 2)
    partner = me + 1 - 2 * core
    spans = planes // span
    row, spot = plane // span, lax.rem(plane, span)
    row_start = row * span
    last = span - 1
    width = order // chips
    turns = width // depth
    bottoms = tuple(top + 1 for top in tops[1:]) + (0,)
    up_turns = jnp.where(row > 0, turns + 1, 1)

    def one_of(places):
        return functools.reduce(jnp.logical_or, [spot == place for place in places])

    first_column = pl.multiple_of(chip * width, width)
    face = coupling[...]
    other_chips = [lax.rem(chip + turn, chips) for turn in range(1, chips)]
    step_rows = 256
    steps = order // step_rows

    barrier = pltpu.get_barrier_semaphore()

    def greet(target_plane, target):
        pl.semaphore_signal(barrier, inc=1, device_id=(target_plane, target), device_id_type=MESH)

    for turn in range(1, parts):
        greet(plane, lax.rem(me + turn, parts))

    @pl.when(plane > 0)
    def _():
        greet(plane - 1, me)

    @pl.when(plane < planes - 1)
    def _():
        greet(plane + 1, me)

    @pl.when(jnp.logical_and(core == 1, jnp.logical_and(row > 0, one_of(tops))))
    def _():
        for other in range(chips):
            greet(row_start - 1, other * 2 + 1)

    def slab(index):
        return slabs.at[:, pl.ds(pl.multiple_of(index * rows, rows), rows)]

    position = lax.broadcasted_iota(jnp.int32, (1, rows), 1)
    weight = (
        conductance[...]
        * (1 - clogged[...]).astype(F32)
        * (position < live[...]).astype(F32)
    ).astype(BF16).astype(F32)
    row_id = lax.broadcasted_iota(jnp.int32, (8, rows), 0)
    packs[me] = jnp.where(row_id == 0, weight, owner[...].astype(F32))
    slabs[:, pl.ds(pl.multiple_of(me * rows, rows), rows)] = basis[0].astype(F32).T.astype(BF16)

    next_to = jnp.where(plane > 0, 1, 0) + jnp.where(plane < planes - 1, 1, 0)
    sends_up = jnp.logical_and(core == 1, jnp.logical_and(spot == last, row < spans - 1))
    extra = jnp.where(sends_up, chips * len(tops), 0)
    pl.semaphore_wait(barrier, parts - 1 + next_to + extra)

    def slab_copy(index, target, slot):
        return pltpu.make_async_remote_copy(
            slab(index), slab(index), slab_send.at[slot], slab_recv.at[index],
            device_id=(plane, target), device_id_type=MESH,
        )

    def pack_copy(index, target, slot):
        return pltpu.make_async_remote_copy(
            packs.at[index], packs.at[index], pack_send.at[slot], pack_recv.at[index],
            device_id=(plane, target), device_id_type=MESH,
        )

    others = [lax.rem(me + turn, parts) for turn in range(1, parts)]
    for slot, target in enumerate(others):
        pack_copy(me, target, slot).start()
    way = 1 - 2 * core
    ahead = lax.rem(chip + way + chips, chips) * 2 + core
    behind = lax.rem(chip - way + chips, chips) * 2 + core
    across_ring = lax.rem(chip + 2, chips) * 2 + core
    slab_copy(me, ahead, 0).start()
    slab_copy(me, behind, 1).start()
    slab_copy(me, partner, 2).start()

    column = lax.broadcasted_iota(jnp.int32, (rows, order), 1).astype(F32)

    def pick(index, carry):
        turned = packs[index].T
        picked[pl.ds(pl.multiple_of(index * rows, rows), rows), :] = jnp.where(
            turned[:, 1:2] == column, turned[:, 0:1], 0.0
        ).astype(BF16)
        return carry

    for other in others:
        pack_copy(other, partner, 0).wait_recv()
    lax.fori_loop(0, parts, pick, 0)

    slab_copy(behind, partner, 0).wait_recv()
    slab_copy(behind, ahead, 3).start()
    slab_copy(behind, partner, 4).start()
    slab_copy(ahead, partner, 0).wait_recv()
    slab_copy(ahead, partner, 5).start()
    slab_copy(across_ring, partner, 0).wait_recv()
    slab_copy(across_ring, partner, 6).start()
    slab_copy(partner, partner, 0).wait_recv()
    flip = 1 - 2 * core
    for source_slab in (behind, ahead, across_ring):
        slab_copy(source_slab + flip, partner, 0).wait_recv()

    eye = lax.broadcasted_iota(jnp.int32, (rows, rows), 0) == lax.broadcasted_iota(
        jnp.int32, (rows, rows), 1
    )
    for index in range(order // rows):
        here = pl.ds(index * rows, rows)
        flux_diag[:, here] = jnp.sum(
            jnp.where(eye, dot(slabs[here, :], picked[:, here]), 0.0), axis=0, keepdims=True
        )

    leak = leakage[...]
    schur = face * face / (face + leak + flux_diag[...])
    faces[0:1, :] = face
    faces[1:2, :] = schur

    def face_copy(target):
        return pltpu.make_async_remote_copy(
            faces, faces_in, face_send, face_recv, device_id=(target, me), device_id_type=MESH
        )

    @pl.when(plane < planes - 1)
    def _():
        face_copy(plane + 1).start()

    def assemble(index, carry):
        here = pl.ds(pl.multiple_of(index * step_rows, step_rows), step_rows)
        block[here, :] = dot(slabs[here, :], picked[...])
        return carry

    lax.fori_loop(0, steps, assemble, 0)

    @pl.when(plane > 0)
    def _():
        face_copy(plane).wait_recv()

    @pl.when(plane == 0)
    def _():
        faces_in[...] = jnp.zeros_like(faces_in)

    diag = flux_diag[...] + (leak + face + faces_in[0:1, :] - faces_in[1:2, :])
    pivots = 1.0 / diag
    inverse_diag[...] = pivots
    system_diag[...] = diag

    across = lax.broadcasted_iota(jnp.int32, (step_rows, order), 1)
    down = lax.broadcasted_iota(jnp.int32, (step_rows, order), 0)

    def scale(index, carry):
        here = pl.ds(pl.multiple_of(index * step_rows, step_rows), step_rows)
        gain = jnp.where(across == down + index * step_rows, 0.0, block[here, :] * pivots)
        block[here, :] = gain
        gain_high[here, :], gain_low[here, :] = split(gain)
        return carry

    lax.fori_loop(0, steps, scale, 0)

    def squared(index, carry):
        here = pl.ds(pl.multiple_of(index * step_rows, step_rows), step_rows)
        high, low = gain_high[here, :], gain_low[here, :]
        value = dot(high, gain_high[...]) + (dot(high, gain_low[...]) + dot(low, gain_high[...]))
        square[here, :] = value.astype(BF16)
        block[here, :] = value - block[here, :]
        return carry

    lax.fori_loop(0, steps, squared, 0)

    def finish(index, carry):
        here = pl.ds(pl.multiple_of(index * step_rows, step_rows), step_rows)
        near = block[here, :] - dot(gain_high[here, :], square[...])
        near_high[here, :], near_low[here, :] = split(near)
        return carry

    lax.fori_loop(0, steps, finish, 0)

    for slot, target in enumerate(others):
        pack_copy(me, target, slot).wait_send()
    slab_copy(me, ahead, 0).wait_send()
    slab_copy(me, behind, 1).wait_send()
    slab_copy(me, partner, 2).wait_send()
    slab_copy(behind, ahead, 3).wait_send()
    slab_copy(behind, partner, 4).wait_send()
    slab_copy(ahead, partner, 5).wait_send()
    slab_copy(across_ring, partner, 6).wait_send()

    @pl.when(plane < planes - 1)
    def _():
        face_copy(plane + 1).wait_send()

    def remote(source_ref, target_ref, send, recv, target_plane, target):
        return pltpu.make_async_remote_copy(
            source_ref, target_ref, send, recv,
            device_id=(target_plane, target), device_id_type=MESH,
        )

    def apply(value):
        count = value.shape[0]
        scaled = value * inverse_diag[...]
        high = scaled.astype(BF16).astype(F32)
        both = jnp.concatenate([high, scaled - high], axis=0).astype(BF16)
        by_high = dot(both, near_high[...])
        by_low = dot(both[:count], near_low[...])
        return scaled + (by_high[:count] + (by_high[count:] + by_low)), both[:count], both[count:]

    def two_rows(value):
        row_id = lax.broadcasted_iota(jnp.int32, (8, value.shape[1]), 0)
        high = value.astype(BF16).astype(F32)
        return jnp.where(row_id == 0, high, jnp.where(row_id == 1, value - high, 0.0)).astype(BF16)

    def apply_one(value):
        scaled = value * inverse_diag[...]
        both = two_rows(scaled)
        return scaled + jnp.sum(
            dot(both, near_high[...]) + dot(both, near_low[...]), axis=0, keepdims=True
        )

    def by_panel(value, high, low):
        both = two_rows(value)
        return jnp.sum(dot(both, high[...]) + dot(both, low[...]), axis=0, keepdims=True)

    def take(index):
        return pl.ds(pl.multiple_of(index * depth, depth), depth)

    one_hot_row = lax.broadcasted_iota(jnp.int32, (depth, order), 0)
    one_hot_column = lax.broadcasted_iota(jnp.int32, (depth, order), 1)

    def unit_rows(index):
        return jnp.where(
            one_hot_column == one_hot_row + (chip * width + index * depth), 1.0, 0.0
        )

    def back_copy(index):
        return remote(
            back_out.at[take(index), :], back_in.at[take(index), :],
            back_send.at[index], back_recv.at[index], plane - 1, me,
        )

    def held_copy(index, half):
        ref = back_low if half else back_high
        return remote(
            ref.at[take(index), :], ref.at[take(index), :],
            held_send.at[half, index], held_recv.at[half, index // turns], plane, partner,
        )

    def stream_turns(stream):
        active = spot <= tops[stream]
        if stream == 0:
            active = jnp.logical_and(active, row < spans - 1)
        return jnp.where(active, turns, 0)

    def end_copy(target):
        return remote(
            end_out.at[target], end_pieces.at[chip], end_send.at[target], end_recv.at[chip],
            plane, target,
        )

    def end_from(source_chip):
        return remote(
            end_out.at[0], end_pieces.at[source_chip], end_send.at[0], end_recv.at[source_chip],
            plane, me,
        )

    @pl.when(core == 0)
    def _():
        def flow_down(stream, top):
            def flow(turn, carry):
                index = stream * turns + turn

                @pl.when(spot == top)
                def _():
                    back_in[take(index), :] = unit_rows(turn)

                @pl.when(spot < top)
                def _():
                    back_copy(index).wait_recv()

                moved = apply(face * back_in[take(index), :])[0]
                back_out[take(index), :] = moved

                @pl.when(spot > 0)
                def _():
                    back_copy(index).start()

                back_high[take(index), :], back_low[take(index), :] = split(moved)
                held_copy(index, 0).start()
                held_copy(index, 1).start()
                return carry

            return flow

        def drain(stream):
            def wait(turn, carry):
                index = stream * turns + turn

                @pl.when(spot > 0)
                def _():
                    back_copy(index).wait_send()

                held_copy(index, 0).wait_send()
                held_copy(index, 1).wait_send()
                return carry

            return wait

        for stream in range(len(tops) - 1, -1, -1):
            lax.fori_loop(0, stream_turns(stream), flow_down(stream, tops[stream]), 0)
        for stream in range(len(tops) - 1, -1, -1):
            lax.fori_loop(0, stream_turns(stream), drain(stream), 0)
        for target in range(chips):
            end_from(target).wait_recv()
        pressure[...] = (end_pieces[0] + end_pieces[1]) + (end_pieces[2] + end_pieces[3])

    def panel_copy(index):
        return remote(
            panel_out.at[take(index), :], panel_in.at[take(index), :],
            panel_send.at[index], panel_recv.at[index], plane + 1, me,
        )

    def up_copy(target, part):
        return remote(
            parts_out.at[target], up_pieces.at[chip],
            up_send.at[part, target], up_recv.at[chip],
            row_start + span + tops[part], target * 2 + 1,
        )

    def down_copy(target, place):
        return remote(
            parts_out.at[target], down_pieces.at[chip],
            down_send.at[place, target], down_recv.at[chip],
            row_start - span + place, target * 2 + 1,
        )

    def edge_copy(place):
        return remote(
            edge_up, edge_up, edge_send.at[place], edge_recv, row_start + place, me
        )

    def mid_copy(stream, target, place):
        return remote(
            parts_out.at[target], edge_pieces.at[stream, chip],
            mid_send.at[place, target], mid_recv.at[stream, chip],
            row_start + place, target * 2 + 1,
        )

    sweep_copy = remote(swept, swept_in, sweep_send, sweep_recv, plane - 1, me)

    def cut(value, ref, count, size):
        for index in range(count):
            ref[index] = value[:, index * size : (index + 1) * size]

    @pl.when(core == 1)
    def _():
        def flow(turn, carry):
            index = lax.rem(turn + turns, turns + 1)

            @pl.when(spot == 0)
            def _():
                panel_in[take(index), :] = unit_rows(index)

            @pl.when(spot > 0)
            def _():
                panel_copy(index).wait_recv()

            @pl.when(turn == 0)
            def _():
                @pl.when(spot == 0)
                def _():
                    panel_in[take(index), :] = jnp.zeros((depth, order), F32)

                panel_in[take(index), :] = panel_in[take(index), :] + jnp.where(
                    one_hot_row == 0, source[...], 0.0
                )

            arrived_rows = panel_in[take(index), :]
            applied, high, low = apply(arrived_rows)
            moved = face * applied
            panel_out[take(index), :] = moved

            @pl.when(spot < last)
            def _():
                panel_copy(index).start()

            @pl.when(turn > 0)
            def _():
                panel_high[take(index), :] = high
                panel_low[take(index), :] = low

                @pl.when(spot == last)
                def _():
                    last_high[take(index), :], last_low[take(index), :] = split(moved)

            return carry

        lax.fori_loop(0, up_turns, flow, 0)
        level[...] = jnp.where(chip == 0, panel_in[width : width + 1, :], 0.0)

        def gather_pieces(pieces, sems):
            for target in range(chips):
                remote(
                    parts_out.at[target], pieces.at[target], end_send.at[0], sems.at[target],
                    plane, me,
                ).wait_recv()
            return (pieces[0] + pieces[1]) + (pieces[2] + pieces[3])

        @pl.when(jnp.logical_and(row > 0, one_of(tops)))
        def _():
            edge_up[...] = gather_pieces(up_pieces, up_recv)

        @pl.when(jnp.logical_and(spot == last, row < spans - 1))
        def _():
            @pl.when(row == 0)
            def _():
                parts_out[...] = jnp.zeros_like(parts_out)

            @pl.when(row > 0)
            def _():
                cut(by_panel(edge_up[...], last_high, last_low), parts_out, chips, width)

            parts_out[chip] = parts_out[chip] + panel_out[
                width : width + 1, pl.ds(first_column, width)
            ]
            for part in range(len(tops)):
                for target in range(chips):
                    up_copy(target, part).start()

        @pl.when(row > 0)
        def _():
            for top, bottom in zip(tops, bottoms):
                @pl.when(spot == top)
                def _():
                    for place in range(top - 1, bottom - 1, -1):
                        edge_copy(place).start()

            @pl.when(jnp.logical_not(one_of(tops)))
            def _():
                edge_copy(0).wait_recv()

            level[...] = level[...] + system_diag[...] * by_panel(
                edge_up[...], panel_high, panel_low
            )

        @pl.when(jnp.logical_not(one_of(tops)))
        def _():
            sweep_copy.wait_recv()
            level[...] = level[...] + face * swept_in[...]

        swept[...] = apply_one(level[...])

        @pl.when(jnp.logical_not(one_of(bottoms)))
        def _():
            sweep_copy.start()

        for stream in range(1, len(tops)):
            @pl.when(spot == bottoms[stream - 1])
            def _():
                cut(swept[...], parts_out, chips, width)

                def send_mid(place, carry):
                    for target in range(chips):
                        mid_copy(stream, target, place).start()
                    return carry

                lax.fori_loop(0, tops[stream] + 1, send_mid, 0)

        def arrived(stream):
            here = pl.ds(stream * width, width)
            for half, ref in enumerate((back_high, back_low)):
                remote(
                    ref.at[here, :], ref.at[here, :],
                    held_send.at[half, 0], held_recv.at[half, stream], plane, me,
                ).wait_recv()

        def by_stream(stream):
            here = slice(stream * width, (stream + 1) * width)
            return by_panel(edges[stream], back_high.at[here, :], back_low.at[here, :])

        total[...] = swept[...]
        for stream in range(len(tops) - 1, -1, -1):
            @pl.when(stream_turns(stream) > 0)
            def _():
                arrived(stream)

        for stream in range(1, len(tops)):
            @pl.when(spot <= tops[stream])
            def _():
                edges[stream] = gather_pieces(edge_pieces.at[stream], mid_recv.at[stream])
                total[...] = total[...] + by_stream(stream)

        @pl.when(row < spans - 1)
        def _():
            edges[0] = gather_pieces(down_pieces, down_recv)
            total[...] = total[...] + by_stream(0)

        @pl.when(jnp.logical_and(spot == 0, row > 0))
        def _():
            cut(total[...], parts_out, chips, width)

            def send_down(place, carry):
                for target in range(chips):
                    down_copy(target, place).start()
                return carry

            lax.fori_loop(0, span, send_down, 0)

        cut(total[...], end_out, parts, rows)
        for target in others:
            end_copy(target).start()
        end_pieces[chip] = end_out[me]
        for other in other_chips:
            end_from(other).wait_recv()
        pressure[...] = (end_pieces[0] + end_pieces[1]) + (end_pieces[2] + end_pieces[3])

        @pl.when(spot < last)
        def _():
            def drain(turn, carry):
                panel_copy(lax.rem(turn + turns, turns + 1)).wait_send()
                return carry

            lax.fori_loop(0, up_turns, drain, 0)

        @pl.when(jnp.logical_and(spot == last, row < spans - 1))
        def _():
            for part in range(len(tops)):
                for target in range(chips):
                    up_copy(target, part).wait_send()

        @pl.when(row > 0)
        def _():
            for top, bottom in zip(tops, bottoms):
                @pl.when(spot == top)
                def _():
                    for place in range(top - 1, bottom - 1, -1):
                        edge_copy(place).wait_send()

        @pl.when(jnp.logical_and(spot == 0, row > 0))
        def _():
            def sent_down(place, carry):
                for target in range(chips):
                    down_copy(target, place).wait_send()
                return carry

            lax.fori_loop(0, span, sent_down, 0)

        for stream in range(1, len(tops)):
            @pl.when(spot == bottoms[stream - 1])
            def _():
                def sent_mid(place, carry):
                    for target in range(chips):
                        mid_copy(stream, target, place).wait_send()
                    return carry

                lax.fori_loop(0, tops[stream] + 1, sent_mid, 0)

        @pl.when(jnp.logical_not(one_of(bottoms)))
        def _():
            sweep_copy.wait_send()

        for target in others:
            end_copy(target).wait_send()


def per_device(basis_flux, owner_cell, clogged, conductance, live_count, coupling, leakage, source):
    planes = lax.axis_size("flow")
    parts = lax.axis_size("trans")
    chips = parts // 2
    rows, order = basis_flux.shape[1:]
    span, depth = planes // 4, 16
    tops = (15, 10, 7, 4)
    streams = len(tops)
    width = order // chips
    turns = width // depth
    row = (1, order)
    piece = (1, width)
    vmem = pl.BlockSpec(memory_space=pltpu.VMEM)
    dma = pltpu.SemaphoreType.DMA
    half = pltpu.VMEM((order, order), BF16)
    return pl.pallas_call(
        functools.partial(kernel, planes, span, chips, rows, order, depth, tops),
        out_shape=jax.ShapeDtypeStruct((1, rows), F32),
        in_specs=[vmem] * 8,
        out_specs=vmem,
        scratch_shapes=[
            half, half, pltpu.VMEM(row, F32),
            half,
            pltpu.VMEM((parts, 8, rows), F32),
            half,
            pltpu.VMEM((order, order), F32),
            half, half, half,
            pltpu.VMEM((2, order), F32),
            pltpu.VMEM((2, order), F32),
            pltpu.VMEM(row, F32),
            pltpu.VMEM((width + depth, order), F32),
            pltpu.VMEM((width + depth, order), F32),
            pltpu.VMEM((streams * width, order), F32),
            pltpu.VMEM((streams * width, order), F32),
            pltpu.VMEM((streams * width, order), BF16),
            pltpu.VMEM((streams * width, order), BF16),
            *[pltpu.VMEM((width, order), BF16) for _ in range(4)],
            pltpu.VMEM(row, F32),
            *[pltpu.VMEM((chips, *piece), F32) for _ in range(3)],
            pltpu.VMEM((streams, chips, *piece), F32),
            pltpu.VMEM((chips, 1, rows), F32),
            pltpu.VMEM((parts, 1, rows), F32),
            pltpu.VMEM(piece, F32),
            pltpu.VMEM((streams, *piece), F32),
            *[pltpu.VMEM(row, F32) for _ in range(4)],
            dma((parts,)), dma((parts,)), dma((parts,)), dma((parts,)), dma, dma,
            dma((turns + 1,)), dma((turns + 1,)),
            dma((streams * turns,)), dma((streams * turns,)),
            dma((2, streams * turns)), dma((2, streams)),
            dma((streams, chips)), dma((chips,)), dma((span, chips)), dma((chips,)),
            dma((span,)), dma, dma((span, chips)), dma((streams, chips)), dma, dma,
            dma((parts,)), dma((chips,)),
        ],
        compiler_params=pltpu.CompilerParams(
            collective_id=0, has_side_effects=True, vmem_limit_bytes=VMEM_LIMIT
        ),
    )(basis_flux, owner_cell, clogged, conductance, live_count, coupling, leakage, source)


def solution(mesh):
    placed = (
        P("flow", "trans", None),
        P("flow", "trans"),
        P("flow", "trans"),
        P("flow", "trans"),
        P("flow", "trans"),
        P("flow", None),
        P("flow", None),
        P("flow", None),
    )
    return jax.shard_map(
        per_device, mesh=mesh, in_specs=placed, out_specs=P("flow", "trans"), check_vma=False
    )
```

```python
import functools

import jax
import jax.numpy as jnp
from jax import lax
from jax.experimental import pallas as pl
from jax.experimental.pallas import tpu as pltpu
from jax.sharding import PartitionSpec as P

MESH = pl.DeviceIdType.MESH
BF16 = jnp.bfloat16
F32 = jnp.float32
VMEM_LIMIT = 56 * 1024 * 1024


def dot(left, right):
    return jnp.dot(left, right, preferred_element_type=F32)


def split(value):
    high = value.astype(BF16)
    return high, (value - high.astype(F32)).astype(BF16)


def kernel(
    planes, span, chips, rows, order, depth, tops,
    basis, owner, clogged, conductance, live, coupling, leakage, source,
    pressure,
    near_high, near_low, inverse_diag,
    slabs, packs, picked, block, gain_high, gain_low, square, faces, faces_in, flux_diag,
    panel_in, panel_out, back_in, back_out, back_high, back_low,
    panel_high, panel_low, last_high, last_low,
    level, parts_out, up_pieces, down_pieces, edge_pieces, end_pieces, end_out,
    edge_up, edges, total, swept_in, swept, system_diag,
    slab_send, slab_recv, pack_send, pack_recv, face_send, face_recv,
    panel_send, panel_recv, back_send, back_recv, held_send, held_recv,
    up_send, up_recv, down_send, down_recv,
    edge_send, edge_recv, mid_send, mid_recv, sweep_send, sweep_recv, end_send, end_recv,
):
    plane = lax.axis_index("flow")
    me = lax.axis_index("trans")
    parts = 2 * chips
    chip, core = me // 2, lax.rem(me, 2)
    partner = me + 1 - 2 * core
    spans = planes // span
    row, spot = plane // span, lax.rem(plane, span)
    row_start = row * span
    last = span - 1
    width = order // chips
    turns = width // depth
    bottoms = tuple(top + 1 for top in tops[1:]) + (0,)
    up_first = jnp.where(row > 0, 0, turns)
    pass_first = jnp.where(jnp.logical_and(row > 0, spot > 0), 0, turns)

    def one_of(places):
        return functools.reduce(jnp.logical_or, [spot == place for place in places])

    first_column = pl.multiple_of(chip * width, width)
    face = coupling[...]
    other_chips = [lax.rem(chip + turn, chips) for turn in range(1, chips)]
    step_rows = 256
    steps = order // step_rows

    barrier = pltpu.get_barrier_semaphore()

    def greet(target_plane, target):
        pl.semaphore_signal(barrier, inc=1, device_id=(target_plane, target), device_id_type=MESH)

    for turn in range(1, parts):
        greet(plane, lax.rem(me + turn, parts))

    @pl.when(plane > 0)
    def _():
        greet(plane - 1, me)

    @pl.when(plane < planes - 1)
    def _():
        greet(plane + 1, me)

    @pl.when(jnp.logical_and(core == 1, jnp.logical_and(row > 0, one_of(tops))))
    def _():
        for other in range(chips):
            greet(row_start - 1, other * 2 + 1)

    def slab(index):
        return slabs.at[:, pl.ds(pl.multiple_of(index * rows, rows), rows)]

    position = lax.broadcasted_iota(jnp.int32, (1, rows), 1)
    weight = (
        conductance[...]
        * (1 - clogged[...]).astype(F32)
        * (position < live[...]).astype(F32)
    ).astype(BF16).astype(F32)
    row_id = lax.broadcasted_iota(jnp.int32, (8, rows), 0)
    packs[me] = jnp.where(row_id == 0, weight, owner[...].astype(F32))
    slabs[:, pl.ds(pl.multiple_of(me * rows, rows), rows)] = basis[0].astype(F32).T.astype(BF16)

    next_to = jnp.where(plane > 0, 1, 0) + jnp.where(plane < planes - 1, 1, 0)
    sends_up = jnp.logical_and(core == 1, jnp.logical_and(spot == last, row < spans - 1))
    extra = jnp.where(sends_up, chips * len(tops), 0)
    pl.semaphore_wait(barrier, parts - 1 + next_to + extra)

    def slab_copy(index, target, slot):
        return pltpu.make_async_remote_copy(
            slab(index), slab(index), slab_send.at[slot], slab_recv.at[index],
            device_id=(plane, target), device_id_type=MESH,
        )

    def pack_copy(index, target, slot):
        return pltpu.make_async_remote_copy(
            packs.at[index], packs.at[index], pack_send.at[slot], pack_recv.at[index],
            device_id=(plane, target), device_id_type=MESH,
        )

    others = [lax.rem(me + turn, parts) for turn in range(1, parts)]
    for slot, target in enumerate(others):
        pack_copy(me, target, slot).start()
    way = 1 - 2 * core
    ahead = lax.rem(chip + way + chips, chips) * 2 + core
    behind = lax.rem(chip - way + chips, chips) * 2 + core
    across_ring = lax.rem(chip + 2, chips) * 2 + core
    slab_copy(me, ahead, 0).start()
    slab_copy(me, behind, 1).start()
    slab_copy(me, partner, 2).start()

    column = lax.broadcasted_iota(jnp.int32, (rows, order), 1).astype(F32)

    def pick(index, carry):
        turned = packs[index].T
        picked[pl.ds(pl.multiple_of(index * rows, rows), rows), :] = jnp.where(
            turned[:, 1:2] == column, turned[:, 0:1], 0.0
        ).astype(BF16)
        return carry

    for other in others:
        pack_copy(other, partner, 0).wait_recv()
    lax.fori_loop(0, parts, pick, 0)

    slab_copy(behind, partner, 0).wait_recv()
    slab_copy(behind, ahead, 3).start()
    slab_copy(behind, partner, 4).start()
    slab_copy(ahead, partner, 0).wait_recv()
    slab_copy(ahead, partner, 5).start()
    slab_copy(across_ring, partner, 0).wait_recv()
    slab_copy(across_ring, partner, 6).start()
    slab_copy(partner, partner, 0).wait_recv()
    flip = 1 - 2 * core
    for source_slab in (behind, ahead, across_ring):
        slab_copy(source_slab + flip, partner, 0).wait_recv()

    eye = lax.broadcasted_iota(jnp.int32, (rows, rows), 0) == lax.broadcasted_iota(
        jnp.int32, (rows, rows), 1
    )
    for index in range(order // rows):
        here = pl.ds(index * rows, rows)
        flux_diag[:, here] = jnp.sum(
            jnp.where(eye, dot(slabs[here, :], picked[:, here]), 0.0), axis=0, keepdims=True
        )

    leak = leakage[...]
    schur = face * face / (face + leak + flux_diag[...])
    faces[0:1, :] = face
    faces[1:2, :] = schur

    def face_copy(target):
        return pltpu.make_async_remote_copy(
            faces, faces_in, face_send, face_recv, device_id=(target, me), device_id_type=MESH
        )

    @pl.when(plane < planes - 1)
    def _():
        face_copy(plane + 1).start()

    def assemble(index, carry):
        here = pl.ds(pl.multiple_of(index * step_rows, step_rows), step_rows)
        block[here, :] = dot(slabs[here, :], picked[...])
        return carry

    lax.fori_loop(0, steps, assemble, 0)

    @pl.when(plane > 0)
    def _():
        face_copy(plane).wait_recv()

    @pl.when(plane == 0)
    def _():
        faces_in[...] = jnp.zeros_like(faces_in)

    diag = flux_diag[...] + (leak + face + faces_in[0:1, :] - faces_in[1:2, :])
    pivots = 1.0 / diag
    inverse_diag[...] = pivots
    system_diag[...] = diag

    across = lax.broadcasted_iota(jnp.int32, (step_rows, order), 1)
    down = lax.broadcasted_iota(jnp.int32, (step_rows, order), 0)

    def scale(index, carry):
        here = pl.ds(pl.multiple_of(index * step_rows, step_rows), step_rows)
        gain = jnp.where(across == down + index * step_rows, 0.0, block[here, :] * pivots)
        block[here, :] = gain
        gain_high[here, :], gain_low[here, :] = split(gain)
        return carry

    lax.fori_loop(0, steps, scale, 0)

    def squared(index, carry):
        here = pl.ds(pl.multiple_of(index * step_rows, step_rows), step_rows)
        high, low = gain_high[here, :], gain_low[here, :]
        value = dot(high, gain_high[...]) + (dot(high, gain_low[...]) + dot(low, gain_high[...]))
        square[here, :] = value.astype(BF16)
        block[here, :] = value - block[here, :]
        return carry

    lax.fori_loop(0, steps, squared, 0)

    def finish(turn, carry):
        index = lax.rem(chip + turn, steps)
        here = pl.ds(pl.multiple_of(index * step_rows, step_rows), step_rows)
        near = block[here, :] - dot(gain_high[here, :], square[...])
        near_high[here, :], near_low[here, :] = split(near)
        return carry

    def remote(source_ref, target_ref, send, recv, target_plane, target):
        return pltpu.make_async_remote_copy(
            source_ref, target_ref, send, recv,
            device_id=(target_plane, target), device_id_type=MESH,
        )

    def apply(value):
        count = value.shape[0]
        scaled = value * inverse_diag[...]
        high = scaled.astype(BF16).astype(F32)
        both = jnp.concatenate([high, scaled - high], axis=0).astype(BF16)
        by_high = dot(both, near_high[...])
        by_low = dot(both[:count], near_low[...])
        return scaled + (by_high[:count] + (by_high[count:] + by_low)), both[:count], both[count:]

    def two_rows(value):
        row_id = lax.broadcasted_iota(jnp.int32, (8, value.shape[1]), 0)
        high = value.astype(BF16).astype(F32)
        return jnp.where(row_id == 0, high, jnp.where(row_id == 1, value - high, 0.0)).astype(BF16)

    def apply_one(value):
        scaled = value * inverse_diag[...]
        both = two_rows(scaled)
        return scaled + jnp.sum(
            dot(both, near_high[...]) + dot(both, near_low[...]), axis=0, keepdims=True
        )

    def by_panel(value, high, low):
        both = two_rows(value)
        return jnp.sum(dot(both, high[...]) + dot(both, low[...]), axis=0, keepdims=True)

    def take(index):
        return pl.ds(pl.multiple_of(index * depth, depth), depth)

    one_hot_row = lax.broadcasted_iota(jnp.int32, (depth, order), 0)
    one_hot_column = lax.broadcasted_iota(jnp.int32, (depth, order), 1)

    def unit_rows(index):
        return jnp.where(
            one_hot_column == one_hot_row + (chip * width + index * depth), 1.0, 0.0
        )

    def back_copy(index):
        return remote(
            back_out.at[take(index), :], back_in.at[take(index), :],
            back_send.at[index], back_recv.at[index], plane - 1, me,
        )

    def held_copy(index, half):
        ref = back_low if half else back_high
        return remote(
            ref.at[take(index), :], ref.at[take(index), :],
            held_send.at[half, index], held_recv.at[half, index // turns], plane, partner,
        )

    def stream_turns(stream):
        active = spot <= tops[stream]
        if stream == 0:
            active = jnp.logical_and(active, row < spans - 1)
        return jnp.where(active, turns, 0)

    def end_copy(target):
        return remote(
            end_out.at[target], end_pieces.at[chip], end_send.at[target], end_recv.at[chip],
            plane, target,
        )

    def end_from(source_chip):
        return remote(
            end_out.at[0], end_pieces.at[source_chip], end_send.at[0], end_recv.at[source_chip],
            plane, me,
        )

    def panel_copy(index):
        return remote(
            panel_out.at[take(index), :], panel_in.at[take(index), :],
            panel_send.at[index], panel_recv.at[index], plane + 1, me,
        )

    finish(0, 0)

    @pl.when(jnp.logical_and(core == 1, jnp.logical_and(spot == 0, row > 0)))
    def _():
        def first(turn, carry):
            here = pl.ds(pl.multiple_of(first_column + turn * depth, depth), depth)
            unit = unit_rows(turn) * pivots
            near = near_high[here, :].astype(F32) + near_low[here, :].astype(F32)
            panel_out[take(turn), :] = face * (unit + jnp.sum(unit, axis=1, keepdims=True) * near)
            panel_copy(turn).start()
            panel_high[take(turn), :], panel_low[take(turn), :] = split(unit)
            return carry

        lax.fori_loop(0, turns, first, 0)

    lax.fori_loop(1, steps, finish, 0)

    @pl.when(core == 0)
    def _():
        def flow_down(stream, top):
            def flow(turn, carry):
                index = stream * turns + turn

                @pl.when(spot == top)
                def _():
                    back_in[take(index), :] = unit_rows(turn)

                @pl.when(spot < top)
                def _():
                    back_copy(index).wait_recv()

                moved = apply(face * back_in[take(index), :])[0]
                back_out[take(index), :] = moved

                @pl.when(spot > 0)
                def _():
                    back_copy(index).start()

                back_high[take(index), :], back_low[take(index), :] = split(moved)
                held_copy(index, 0).start()
                held_copy(index, 1).start()
                return carry

            return flow

        def drain(stream):
            def wait(turn, carry):
                index = stream * turns + turn

                @pl.when(spot > 0)
                def _():
                    back_copy(index).wait_send()

                held_copy(index, 0).wait_send()
                held_copy(index, 1).wait_send()
                return carry

            return wait

        for stream in range(len(tops) - 1, -1, -1):
            lax.fori_loop(0, stream_turns(stream), flow_down(stream, tops[stream]), 0)
        for stream in range(len(tops) - 1, -1, -1):
            lax.fori_loop(0, stream_turns(stream), drain(stream), 0)
        for target in range(chips):
            end_from(target).wait_recv()
        pressure[...] = (end_pieces[0] + end_pieces[1]) + (end_pieces[2] + end_pieces[3])

    def up_copy(target, part):
        return remote(
            parts_out.at[target], up_pieces.at[chip],
            up_send.at[part, target], up_recv.at[chip],
            row_start + span + tops[part], target * 2 + 1,
        )

    def down_copy(target, place):
        return remote(
            parts_out.at[target], down_pieces.at[chip],
            down_send.at[place, target], down_recv.at[chip],
            row_start - span + place, target * 2 + 1,
        )

    def edge_copy(place):
        return remote(
            edge_up, edge_up, edge_send.at[place], edge_recv, row_start + place, me
        )

    def mid_copy(stream, target, place):
        return remote(
            parts_out.at[target], edge_pieces.at[stream, chip],
            mid_send.at[place, target], mid_recv.at[stream, chip],
            row_start + place, target * 2 + 1,
        )

    sweep_copy = remote(swept, swept_in, sweep_send, sweep_recv, plane - 1, me)

    def cut(value, ref, count, size):
        for index in range(count):
            ref[index] = value[:, index * size : (index + 1) * size]

    @pl.when(core == 1)
    def _():
        def flow(index, carry):
            @pl.when(spot > 0)
            def _():
                panel_copy(index).wait_recv()

            @pl.when(index == turns)
            def _():
                @pl.when(spot == 0)
                def _():
                    panel_in[take(index), :] = jnp.zeros((depth, order), F32)

                panel_in[take(index), :] = panel_in[take(index), :] + jnp.where(
                    one_hot_row == 0, source[...], 0.0
                )

            arrived_rows = panel_in[take(index), :]
            scaled = arrived_rows * inverse_diag[...]
            high = scaled.astype(BF16)
            low = (scaled - high.astype(F32)).astype(BF16)
            both = jnp.concatenate([high, low], axis=0)
            def advance(pass_on):
                size = order // 2
                for block in range(order // size):
                    across = slice(block * size, (block + 1) * size)
                    by_high = dot(both, near_high[:, across])
                    by_low = dot(high, near_low[:, across])
                    panel_out[take(index), across] = face[:, across] * (
                        scaled[:, across] + (by_high[:depth] + (by_high[depth:] + by_low))
                    )
                    if pass_on:
                        remote(
                            panel_out.at[take(index), across], panel_in.at[take(index), across],
                            panel_send.at[index], panel_recv.at[index], plane + 1, me,
                        ).start()

            @pl.when(spot < last)
            def _():
                advance(True)

            @pl.when(spot == last)
            def _():
                advance(False)

            @pl.when(index < turns)
            def _():
                panel_high[take(index), :] = high
                panel_low[take(index), :] = low

                @pl.when(spot == last)
                def _():
                    last_high[take(index), :], last_low[take(index), :] = split(
                        panel_out[take(index), :]
                    )

            return carry

        lax.fori_loop(pass_first, turns + 1, flow, 0)
        level[...] = jnp.where(chip == 0, panel_in[width : width + 1, :], 0.0)

        def gather_pieces(pieces, sems):
            for target in range(chips):
                remote(
                    parts_out.at[target], pieces.at[target], end_send.at[0], sems.at[target],
                    plane, me,
                ).wait_recv()
            return (pieces[0] + pieces[1]) + (pieces[2] + pieces[3])

        @pl.when(jnp.logical_and(row > 0, one_of(tops)))
        def _():
            edge_up[...] = gather_pieces(up_pieces, up_recv)

        @pl.when(jnp.logical_and(spot == last, row < spans - 1))
        def _():
            @pl.when(row == 0)
            def _():
                parts_out[...] = jnp.zeros_like(parts_out)

            @pl.when(row > 0)
            def _():
                cut(by_panel(edge_up[...], last_high, last_low), parts_out, chips, width)

            parts_out[chip] = parts_out[chip] + panel_out[
                width : width + 1, pl.ds(first_column, width)
            ]
            for part in range(len(tops)):
                for target in range(chips):
                    up_copy(target, part).start()

        @pl.when(row > 0)
        def _():
            for top, bottom in zip(tops, bottoms):
                @pl.when(spot == top)
                def _():
                    for place in range(top - 1, bottom - 1, -1):
                        edge_copy(place).start()

            @pl.when(jnp.logical_not(one_of(tops)))
            def _():
                edge_copy(0).wait_recv()

            level[...] = level[...] + system_diag[...] * by_panel(
                edge_up[...], panel_high, panel_low
            )

        @pl.when(jnp.logical_not(one_of(tops)))
        def _():
            sweep_copy.wait_recv()
            level[...] = level[...] + face * swept_in[...]

        swept[...] = apply_one(level[...])

        @pl.when(jnp.logical_not(one_of(bottoms)))
        def _():
            sweep_copy.start()

        for stream in range(1, len(tops)):
            @pl.when(spot == bottoms[stream - 1])
            def _():
                cut(swept[...], parts_out, chips, width)

                def send_mid(place, carry):
                    for target in range(chips):
                        mid_copy(stream, target, place).start()
                    return carry

                lax.fori_loop(0, tops[stream] + 1, send_mid, 0)

        def arrived(stream):
            here = pl.ds(stream * width, width)
            for half, ref in enumerate((back_high, back_low)):
                remote(
                    ref.at[here, :], ref.at[here, :],
                    held_send.at[half, 0], held_recv.at[half, stream], plane, me,
                ).wait_recv()

        def by_stream(stream):
            here = slice(stream * width, (stream + 1) * width)
            return by_panel(edges[stream], back_high.at[here, :], back_low.at[here, :])

        total[...] = swept[...]
        for stream in range(len(tops) - 1, -1, -1):
            @pl.when(stream_turns(stream) > 0)
            def _():
                arrived(stream)

        for stream in range(1, len(tops)):
            @pl.when(spot <= tops[stream])
            def _():
                edges[stream] = gather_pieces(edge_pieces.at[stream], mid_recv.at[stream])
                total[...] = total[...] + by_stream(stream)

        @pl.when(row < spans - 1)
        def _():
            edges[0] = gather_pieces(down_pieces, down_recv)
            total[...] = total[...] + by_stream(0)

        @pl.when(jnp.logical_and(spot == 0, row > 0))
        def _():
            cut(total[...], parts_out, chips, width)

            def send_down(place, carry):
                for target in range(chips):
                    down_copy(target, place).start()
                return carry

            lax.fori_loop(0, span, send_down, 0)

        cut(total[...], end_out, parts, rows)
        for target in others:
            end_copy(target).start()
        end_pieces[chip] = end_out[me]
        for other in other_chips:
            end_from(other).wait_recv()
        pressure[...] = (end_pieces[0] + end_pieces[1]) + (end_pieces[2] + end_pieces[3])

        @pl.when(spot < last)
        def _():
            def drain(index, carry):
                panel_copy(index).wait_send()
                return carry

            lax.fori_loop(up_first, turns + 1, drain, 0)

        @pl.when(jnp.logical_and(spot == last, row < spans - 1))
        def _():
            for part in range(len(tops)):
                for target in range(chips):
                    up_copy(target, part).wait_send()

        @pl.when(row > 0)
        def _():
            for top, bottom in zip(tops, bottoms):
                @pl.when(spot == top)
                def _():
                    for place in range(top - 1, bottom - 1, -1):
                        edge_copy(place).wait_send()

        @pl.when(jnp.logical_and(spot == 0, row > 0))
        def _():
            def sent_down(place, carry):
                for target in range(chips):
                    down_copy(target, place).wait_send()
                return carry

            lax.fori_loop(0, span, sent_down, 0)

        for stream in range(1, len(tops)):
            @pl.when(spot == bottoms[stream - 1])
            def _():
                def sent_mid(place, carry):
                    for target in range(chips):
                        mid_copy(stream, target, place).wait_send()
                    return carry

                lax.fori_loop(0, tops[stream] + 1, sent_mid, 0)

        @pl.when(jnp.logical_not(one_of(bottoms)))
        def _():
            sweep_copy.wait_send()

        for target in others:
            end_copy(target).wait_send()

    for slot, target in enumerate(others):
        pack_copy(me, target, slot).wait_send()
    slab_copy(me, ahead, 0).wait_send()
    slab_copy(me, behind, 1).wait_send()
    slab_copy(me, partner, 2).wait_send()
    slab_copy(behind, ahead, 3).wait_send()
    slab_copy(behind, partner, 4).wait_send()
    slab_copy(ahead, partner, 5).wait_send()
    slab_copy(across_ring, partner, 6).wait_send()

    @pl.when(plane < planes - 1)
    def _():
        face_copy(plane + 1).wait_send()


def per_device(basis_flux, owner_cell, clogged, conductance, live_count, coupling, leakage, source):
    planes = lax.axis_size("flow")
    parts = lax.axis_size("trans")
    chips = parts // 2
    rows, order = basis_flux.shape[1:]
    span, depth = planes // 4, 16
    tops = (15, 10, 7, 4)
    streams = len(tops)
    width = order // chips
    turns = width // depth
    row = (1, order)
    piece = (1, width)
    vmem = pl.BlockSpec(memory_space=pltpu.VMEM)
    dma = pltpu.SemaphoreType.DMA
    half = pltpu.VMEM((order, order), BF16)
    return pl.pallas_call(
        functools.partial(kernel, planes, span, chips, rows, order, depth, tops),
        out_shape=jax.ShapeDtypeStruct((1, rows), F32),
        in_specs=[vmem] * 8,
        out_specs=vmem,
        scratch_shapes=[
            half, half, pltpu.VMEM(row, F32),
            half,
            pltpu.VMEM((parts, 8, rows), F32),
            half,
            pltpu.VMEM((order, order), F32),
            half, half, half,
            pltpu.VMEM((2, order), F32),
            pltpu.VMEM((2, order), F32),
            pltpu.VMEM(row, F32),
            pltpu.VMEM((width + depth, order), F32),
            pltpu.VMEM((width + depth, order), F32),
            pltpu.VMEM((streams * width, order), F32),
            pltpu.VMEM((streams * width, order), F32),
            pltpu.VMEM((streams * width, order), BF16),
            pltpu.VMEM((streams * width, order), BF16),
            *[pltpu.VMEM((width, order), BF16) for _ in range(4)],
            pltpu.VMEM(row, F32),
            *[pltpu.VMEM((chips, *piece), F32) for _ in range(3)],
            pltpu.VMEM((streams, chips, *piece), F32),
            pltpu.VMEM((chips, 1, rows), F32),
            pltpu.VMEM((parts, 1, rows), F32),
            pltpu.VMEM(piece, F32),
            pltpu.VMEM((streams, *piece), F32),
            *[pltpu.VMEM(row, F32) for _ in range(4)],
            dma((parts,)), dma((parts,)), dma((parts,)), dma((parts,)), dma, dma,
            dma((turns + 1,)), dma((turns + 1,)),
            dma((streams * turns,)), dma((streams * turns,)),
            dma((2, streams * turns)), dma((2, streams)),
            dma((streams, chips)), dma((chips,)), dma((span, chips)), dma((chips,)),
            dma((span,)), dma, dma((span, chips)), dma((streams, chips)), dma, dma,
            dma((parts,)), dma((chips,)),
        ],
        compiler_params=pltpu.CompilerParams(
            collective_id=0, has_side_effects=True, vmem_limit_bytes=VMEM_LIMIT
        ),
    )(basis_flux, owner_cell, clogged, conductance, live_count, coupling, leakage, source)


def solution(mesh):
    placed = (
        P("flow", "trans", None),
        P("flow", "trans"),
        P("flow", "trans"),
        P("flow", "trans"),
        P("flow", "trans"),
        P("flow", None),
        P("flow", None),
        P("flow", None),
    )
    return jax.shard_map(
        per_device, mesh=mesh, in_specs=placed, out_specs=P("flow", "trans"), check_vma=False
    )
```

```python
import functools

import jax
import jax.numpy as jnp
from jax import lax
from jax.experimental import pallas as pl
from jax.experimental.pallas import tpu as pltpu
from jax.sharding import PartitionSpec as P

MESH = pl.DeviceIdType.MESH
BF16 = jnp.bfloat16
F32 = jnp.float32
VMEM_LIMIT = 56 * 1024 * 1024


def dot(left, right):
    return jnp.dot(left, right, preferred_element_type=F32)


def split(value):
    high = value.astype(BF16)
    return high, (value - high.astype(F32)).astype(BF16)


def kernel(
    planes, span, chips, rows, order, depth, tops,
    basis, owner, clogged, conductance, live, coupling, leakage, source,
    pressure,
    near_high, near_low, inverse_diag,
    slabs, packs, picked, block, gain_high, gain_low, square, faces, faces_in, flux_diag,
    panel_in, panel_out, back_in, back_out, back_high, back_low,
    panel_high, panel_low, last_high, last_low,
    level, parts_out, up_pieces, down_pieces, edge_pieces, end_pieces, end_out,
    edge_up, edges, total, swept_in, swept, system_diag,
    slab_send, slab_recv, pack_send, pack_recv, face_send, face_recv,
    panel_send, panel_recv, back_send, back_recv, held_send, held_recv,
    up_send, up_recv, down_send, down_recv,
    edge_send, edge_recv, mid_send, mid_recv, sweep_send, sweep_recv, end_send, end_recv,
):
    plane = lax.axis_index("flow")
    me = lax.axis_index("trans")
    parts = 2 * chips
    chip, core = me // 2, lax.rem(me, 2)
    partner = me + 1 - 2 * core
    spans = planes // span
    row, spot = plane // span, lax.rem(plane, span)
    row_start = row * span
    last = span - 1
    width = order // chips
    turns = width // depth
    bottoms = tuple(top + 1 for top in tops[1:]) + (0,)
    up_first = jnp.where(row > 0, 0, turns)
    pass_first = jnp.where(jnp.logical_and(row > 0, spot > 0), 0, turns)

    def one_of(places):
        return functools.reduce(jnp.logical_or, [spot == place for place in places])

    first_column = pl.multiple_of(chip * width, width)
    face = coupling[...]
    other_chips = [lax.rem(chip + turn, chips) for turn in range(1, chips)]
    step_rows = 256
    steps = order // step_rows

    barrier = pltpu.get_barrier_semaphore()

    def greet(target_plane, target):
        pl.semaphore_signal(barrier, inc=1, device_id=(target_plane, target), device_id_type=MESH)

    for turn in range(1, parts):
        greet(plane, lax.rem(me + turn, parts))

    @pl.when(plane > 0)
    def _():
        greet(plane - 1, me)

    @pl.when(plane < planes - 1)
    def _():
        greet(plane + 1, me)

    @pl.when(jnp.logical_and(core == 1, jnp.logical_and(row > 0, one_of(tops))))
    def _():
        for other in range(chips):
            greet(row_start - 1, other * 2 + 1)

    def slab(index):
        return slabs.at[:, pl.ds(pl.multiple_of(index * rows, rows), rows)]

    position = lax.broadcasted_iota(jnp.int32, (1, rows), 1)
    weight = (
        conductance[...]
        * (1 - clogged[...]).astype(F32)
        * (position < live[...]).astype(F32)
    ).astype(BF16).astype(F32)
    row_id = lax.broadcasted_iota(jnp.int32, (8, rows), 0)
    pack = jnp.where(row_id == 0, weight, owner[...].astype(F32))
    packs[me, 0:8, :] = pack
    turned = pack.T
    column = lax.broadcasted_iota(jnp.int32, (rows, order), 1).astype(F32)
    own_share = jnp.sum(
        jnp.where(turned[:, 1:2] == column, turned[:, 0:1], 0.0) * basis[0].astype(F32),
        axis=0, keepdims=True,
    )
    for index in range(order // rows):
        packs[me, 8 + index : 9 + index, :] = own_share[:, index * rows : (index + 1) * rows]
    slabs[:, pl.ds(pl.multiple_of(me * rows, rows), rows)] = basis[0].astype(F32).T.astype(BF16)

    next_to = jnp.where(plane > 0, 1, 0) + jnp.where(plane < planes - 1, 1, 0)
    sends_up = jnp.logical_and(core == 1, jnp.logical_and(spot == last, row < spans - 1))
    extra = jnp.where(sends_up, chips * len(tops), 0)
    pl.semaphore_wait(barrier, parts - 1 + next_to + extra)

    def slab_copy(index, target, slot):
        return pltpu.make_async_remote_copy(
            slab(index), slab(index), slab_send.at[slot], slab_recv.at[index],
            device_id=(plane, target), device_id_type=MESH,
        )

    def pack_copy(index, target, slot):
        return pltpu.make_async_remote_copy(
            packs.at[index], packs.at[index], pack_send.at[slot], pack_recv.at[index],
            device_id=(plane, target), device_id_type=MESH,
        )

    others = [lax.rem(me + turn, parts) for turn in range(1, parts)]
    for slot, target in enumerate(others):
        pack_copy(me, target, slot).start()
    way = 1 - 2 * core
    ahead = lax.rem(chip + way + chips, chips) * 2 + core
    behind = lax.rem(chip - way + chips, chips) * 2 + core
    across_ring = lax.rem(chip + 2, chips) * 2 + core
    slab_copy(me, ahead, 0).start()
    slab_copy(me, behind, 1).start()
    slab_copy(me, partner, 2).start()

    for other in others:
        pack_copy(other, partner, 0).wait_recv()

    shares = packs[0, 8:16, :]
    for index in range(1, parts):
        shares = shares + packs[index, 8:16, :]
    for index in range(order // rows):
        flux_diag[:, index * rows : (index + 1) * rows] = shares[index : index + 1, :]
    leak = leakage[...]
    schur = face * face / (face + leak + flux_diag[...])
    faces[0:1, :] = face
    faces[1:2, :] = schur

    def face_copy(target):
        return pltpu.make_async_remote_copy(
            faces, faces_in, face_send, face_recv, device_id=(target, me), device_id_type=MESH
        )

    @pl.when(plane < planes - 1)
    def _():
        face_copy(plane + 1).start()

    def pick(index, carry):
        turned = packs[index, 0:8, :].T
        picked[pl.ds(pl.multiple_of(index * rows, rows), rows), :] = jnp.where(
            turned[:, 1:2] == column, turned[:, 0:1], 0.0
        ).astype(BF16)
        return carry

    lax.fori_loop(0, parts, pick, 0)

    def chunk(index):
        return pl.ds(pl.multiple_of(index * step_rows, step_rows), step_rows)

    def from_chip(index, source_chip):
        slab_rows = pl.ds(pl.multiple_of(source_chip * 2 * rows, 2 * rows), 2 * rows)
        return dot(slabs[chunk(index), slab_rows], picked[slab_rows, :])

    def begin(index, carry):
        block[chunk(index), :] = from_chip(index, chip)
        return carry

    def add_chip(source_chip):
        def add(index, carry):
            block[chunk(index), :] = block[chunk(index), :] + from_chip(index, source_chip)
            return carry

        return add

    flip = 1 - 2 * core
    slab_copy(partner, partner, 0).wait_recv()
    lax.fori_loop(0, steps, begin, 0)
    slab_copy(behind, partner, 0).wait_recv()
    slab_copy(behind, ahead, 3).start()
    slab_copy(behind, partner, 4).start()
    slab_copy(ahead, partner, 0).wait_recv()
    slab_copy(ahead, partner, 5).start()
    slab_copy(ahead + flip, partner, 0).wait_recv()
    lax.fori_loop(0, steps, add_chip(ahead // 2), 0)
    slab_copy(across_ring, partner, 0).wait_recv()
    slab_copy(across_ring, partner, 6).start()
    slab_copy(behind + flip, partner, 0).wait_recv()
    lax.fori_loop(0, steps, add_chip(behind // 2), 0)

    @pl.when(plane > 0)
    def _():
        face_copy(plane).wait_recv()

    @pl.when(plane == 0)
    def _():
        faces_in[...] = jnp.zeros_like(faces_in)

    diag = flux_diag[...] + (leak + face + faces_in[0:1, :] - faces_in[1:2, :])
    pivots = 1.0 / diag
    inverse_diag[...] = pivots
    system_diag[...] = diag

    across = lax.broadcasted_iota(jnp.int32, (step_rows, order), 1)
    down = lax.broadcasted_iota(jnp.int32, (step_rows, order), 0)

    def scale(index, carry):
        here = chunk(index)
        whole = block[here, :] + from_chip(index, across_ring // 2)
        gain = jnp.where(across == down + index * step_rows, 0.0, whole * pivots)
        block[here, :] = gain
        gain_high[here, :], gain_low[here, :] = split(gain)
        return carry

    slab_copy(across_ring + flip, partner, 0).wait_recv()
    lax.fori_loop(0, steps, scale, 0)

    def squared(index, carry):
        here = pl.ds(pl.multiple_of(index * step_rows, step_rows), step_rows)
        high, low = gain_high[here, :], gain_low[here, :]
        value = dot(high, gain_high[...]) + (dot(high, gain_low[...]) + dot(low, gain_high[...]))
        square[here, :] = value.astype(BF16)
        block[here, :] = value - block[here, :]
        return carry

    lax.fori_loop(0, steps, squared, 0)

    def finish(turn, carry):
        index = lax.rem(chip + turn, steps)
        here = pl.ds(pl.multiple_of(index * step_rows, step_rows), step_rows)
        near = block[here, :] - dot(gain_high[here, :], square[...])
        near_high[here, :], near_low[here, :] = split(near)
        return carry

    def remote(source_ref, target_ref, send, recv, target_plane, target):
        return pltpu.make_async_remote_copy(
            source_ref, target_ref, send, recv,
            device_id=(target_plane, target), device_id_type=MESH,
        )

    def apply(value):
        count = value.shape[0]
        scaled = value * inverse_diag[...]
        high = scaled.astype(BF16).astype(F32)
        both = jnp.concatenate([high, scaled - high], axis=0).astype(BF16)
        by_high = dot(both, near_high[...])
        by_low = dot(both[:count], near_low[...])
        return scaled + (by_high[:count] + (by_high[count:] + by_low)), both[:count], both[count:]

    def two_rows(value):
        row_id = lax.broadcasted_iota(jnp.int32, (8, value.shape[1]), 0)
        high = value.astype(BF16).astype(F32)
        return jnp.where(row_id == 0, high, jnp.where(row_id == 1, value - high, 0.0)).astype(BF16)

    def apply_one(value):
        scaled = value * inverse_diag[...]
        both = two_rows(scaled)
        return scaled + jnp.sum(
            dot(both, near_high[...]) + dot(both, near_low[...]), axis=0, keepdims=True
        )

    def by_panel(value, high, low):
        both = two_rows(value)
        return jnp.sum(dot(both, high[...]) + dot(both, low[...]), axis=0, keepdims=True)

    def take(index):
        return pl.ds(pl.multiple_of(index * depth, depth), depth)

    one_hot_row = lax.broadcasted_iota(jnp.int32, (depth, order), 0)
    one_hot_column = lax.broadcasted_iota(jnp.int32, (depth, order), 1)

    def unit_rows(index):
        return jnp.where(
            one_hot_column == one_hot_row + (chip * width + index * depth), 1.0, 0.0
        )

    def back_copy(index):
        return remote(
            back_out.at[take(index), :], back_in.at[take(index), :],
            back_send.at[index], back_recv.at[index], plane - 1, me,
        )

    def held_copy(index, half):
        ref = back_low if half else back_high
        return remote(
            ref.at[take(index), :], ref.at[take(index), :],
            held_send.at[half, index], held_recv.at[half, index // turns], plane, partner,
        )

    def stream_turns(stream):
        active = spot <= tops[stream]
        if stream == 0:
            active = jnp.logical_and(active, row < spans - 1)
        return jnp.where(active, turns, 0)

    def end_copy(target):
        return remote(
            end_out.at[target], end_pieces.at[chip], end_send.at[target], end_recv.at[chip],
            plane, target,
        )

    def end_from(source_chip):
        return remote(
            end_out.at[0], end_pieces.at[source_chip], end_send.at[0], end_recv.at[source_chip],
            plane, me,
        )

    def panel_copy(index):
        return remote(
            panel_out.at[take(index), :], panel_in.at[take(index), :],
            panel_send.at[index], panel_recv.at[index], plane + 1, me,
        )

    finish(0, 0)

    @pl.when(jnp.logical_and(core == 1, jnp.logical_and(spot == 0, row > 0)))
    def _():
        def first(turn, carry):
            here = pl.ds(pl.multiple_of(first_column + turn * depth, depth), depth)
            unit = unit_rows(turn) * pivots
            near = near_high[here, :].astype(F32) + near_low[here, :].astype(F32)
            panel_out[take(turn), :] = face * (unit + jnp.sum(unit, axis=1, keepdims=True) * near)
            panel_copy(turn).start()
            panel_high[take(turn), :], panel_low[take(turn), :] = split(unit)
            return carry

        lax.fori_loop(0, turns, first, 0)

    lax.fori_loop(1, steps, finish, 0)

    @pl.when(core == 0)
    def _():
        def flow_down(stream, top):
            def flow(turn, carry):
                index = stream * turns + turn

                @pl.when(spot == top)
                def _():
                    back_in[take(index), :] = unit_rows(turn)

                @pl.when(spot < top)
                def _():
                    back_copy(index).wait_recv()

                moved = apply(face * back_in[take(index), :])[0]
                back_out[take(index), :] = moved

                @pl.when(spot > 0)
                def _():
                    back_copy(index).start()

                back_high[take(index), :], back_low[take(index), :] = split(moved)
                held_copy(index, 0).start()
                held_copy(index, 1).start()
                return carry

            return flow

        def drain(stream):
            def wait(turn, carry):
                index = stream * turns + turn

                @pl.when(spot > 0)
                def _():
                    back_copy(index).wait_send()

                held_copy(index, 0).wait_send()
                held_copy(index, 1).wait_send()
                return carry

            return wait

        for stream in range(len(tops) - 1, -1, -1):
            lax.fori_loop(0, stream_turns(stream), flow_down(stream, tops[stream]), 0)
        for stream in range(len(tops) - 1, -1, -1):
            lax.fori_loop(0, stream_turns(stream), drain(stream), 0)
        for target in range(chips):
            end_from(target).wait_recv()
        pressure[...] = (end_pieces[0] + end_pieces[1]) + (end_pieces[2] + end_pieces[3])

    def up_copy(target, part):
        return remote(
            parts_out.at[target], up_pieces.at[chip],
            up_send.at[part, target], up_recv.at[chip],
            row_start + span + tops[part], target * 2 + 1,
        )

    def down_copy(target, place):
        return remote(
            parts_out.at[target], down_pieces.at[chip],
            down_send.at[place, target], down_recv.at[chip],
            row_start - span + place, target * 2 + 1,
        )

    def edge_copy(place):
        return remote(
            edge_up, edge_up, edge_send.at[place], edge_recv, row_start + place, me
        )

    def mid_copy(stream, target, place):
        return remote(
            parts_out.at[target], edge_pieces.at[stream, chip],
            mid_send.at[place, target], mid_recv.at[stream, chip],
            row_start + place, target * 2 + 1,
        )

    sweep_copy = remote(swept, swept_in, sweep_send, sweep_recv, plane - 1, me)

    def cut(value, ref, count, size):
        for index in range(count):
            ref[index] = value[:, index * size : (index + 1) * size]

    @pl.when(core == 1)
    def _():
        def flow(index, carry):
            @pl.when(spot > 0)
            def _():
                panel_copy(index).wait_recv()

            @pl.when(index == turns)
            def _():
                @pl.when(spot == 0)
                def _():
                    panel_in[take(index), :] = jnp.zeros((depth, order), F32)

                panel_in[take(index), :] = panel_in[take(index), :] + jnp.where(
                    one_hot_row == 0, source[...], 0.0
                )

            arrived_rows = panel_in[take(index), :]
            scaled = arrived_rows * inverse_diag[...]
            high = scaled.astype(BF16)
            low = (scaled - high.astype(F32)).astype(BF16)
            both = jnp.concatenate([high, low], axis=0)
            def advance(pass_on):
                size = order // 2
                for block in range(order // size):
                    across = slice(block * size, (block + 1) * size)
                    by_high = dot(both, near_high[:, across])
                    by_low = dot(high, near_low[:, across])
                    panel_out[take(index), across] = face[:, across] * (
                        scaled[:, across] + (by_high[:depth] + (by_high[depth:] + by_low))
                    )
                    if pass_on:
                        remote(
                            panel_out.at[take(index), across], panel_in.at[take(index), across],
                            panel_send.at[index], panel_recv.at[index], plane + 1, me,
                        ).start()

            @pl.when(spot < last)
            def _():
                advance(True)

            @pl.when(spot == last)
            def _():
                advance(False)

            @pl.when(index < turns)
            def _():
                panel_high[take(index), :] = high
                panel_low[take(index), :] = low

                @pl.when(spot == last)
                def _():
                    last_high[take(index), :], last_low[take(index), :] = split(
                        panel_out[take(index), :]
                    )

            return carry

        lax.fori_loop(pass_first, turns + 1, flow, 0)
        level[...] = jnp.where(chip == 0, panel_in[width : width + 1, :], 0.0)

        def gather_pieces(pieces, sems):
            for target in range(chips):
                remote(
                    parts_out.at[target], pieces.at[target], end_send.at[0], sems.at[target],
                    plane, me,
                ).wait_recv()
            return (pieces[0] + pieces[1]) + (pieces[2] + pieces[3])

        @pl.when(jnp.logical_and(row > 0, one_of(tops)))
        def _():
            edge_up[...] = gather_pieces(up_pieces, up_recv)

        @pl.when(jnp.logical_and(spot == last, row < spans - 1))
        def _():
            @pl.when(row == 0)
            def _():
                parts_out[...] = jnp.zeros_like(parts_out)

            @pl.when(row > 0)
            def _():
                cut(by_panel(edge_up[...], last_high, last_low), parts_out, chips, width)

            parts_out[chip] = parts_out[chip] + panel_out[
                width : width + 1, pl.ds(first_column, width)
            ]
            for part in range(len(tops)):
                for target in range(chips):
                    up_copy(target, part).start()

        @pl.when(row > 0)
        def _():
            for top, bottom in zip(tops, bottoms):
                @pl.when(spot == top)
                def _():
                    for place in range(top - 1, bottom - 1, -1):
                        edge_copy(place).start()

            @pl.when(jnp.logical_not(one_of(tops)))
            def _():
                edge_copy(0).wait_recv()

            level[...] = level[...] + system_diag[...] * by_panel(
                edge_up[...], panel_high, panel_low
            )

        @pl.when(jnp.logical_not(one_of(tops)))
        def _():
            sweep_copy.wait_recv()
            level[...] = level[...] + face * swept_in[...]

        swept[...] = apply_one(level[...])

        @pl.when(jnp.logical_not(one_of(bottoms)))
        def _():
            sweep_copy.start()

        for stream in range(1, len(tops)):
            @pl.when(spot == bottoms[stream - 1])
            def _():
                cut(swept[...], parts_out, chips, width)

                def send_mid(place, carry):
                    for target in range(chips):
                        mid_copy(stream, target, place).start()
                    return carry

                lax.fori_loop(0, tops[stream] + 1, send_mid, 0)

        def arrived(stream):
            here = pl.ds(stream * width, width)
            for half, ref in enumerate((back_high, back_low)):
                remote(
                    ref.at[here, :], ref.at[here, :],
                    held_send.at[half, 0], held_recv.at[half, stream], plane, me,
                ).wait_recv()

        def by_stream(stream):
            here = slice(stream * width, (stream + 1) * width)
            return by_panel(edges[stream], back_high.at[here, :], back_low.at[here, :])

        total[...] = swept[...]
        for stream in range(len(tops) - 1, -1, -1):
            @pl.when(stream_turns(stream) > 0)
            def _():
                arrived(stream)

        for stream in range(1, len(tops)):
            @pl.when(spot <= tops[stream])
            def _():
                edges[stream] = gather_pieces(edge_pieces.at[stream], mid_recv.at[stream])
                total[...] = total[...] + by_stream(stream)

        @pl.when(row < spans - 1)
        def _():
            edges[0] = gather_pieces(down_pieces, down_recv)
            total[...] = total[...] + by_stream(0)

        @pl.when(jnp.logical_and(spot == 0, row > 0))
        def _():
            cut(total[...], parts_out, chips, width)

            def send_down(place, carry):
                for target in range(chips):
                    down_copy(target, place).start()
                return carry

            lax.fori_loop(0, span, send_down, 0)

        cut(total[...], end_out, parts, rows)
        for target in others:
            end_copy(target).start()
        end_pieces[chip] = end_out[me]
        for other in other_chips:
            end_from(other).wait_recv()
        pressure[...] = (end_pieces[0] + end_pieces[1]) + (end_pieces[2] + end_pieces[3])

        @pl.when(spot < last)
        def _():
            def drain(index, carry):
                panel_copy(index).wait_send()
                return carry

            lax.fori_loop(up_first, turns + 1, drain, 0)

        @pl.when(jnp.logical_and(spot == last, row < spans - 1))
        def _():
            for part in range(len(tops)):
                for target in range(chips):
                    up_copy(target, part).wait_send()

        @pl.when(row > 0)
        def _():
            for top, bottom in zip(tops, bottoms):
                @pl.when(spot == top)
                def _():
                    for place in range(top - 1, bottom - 1, -1):
                        edge_copy(place).wait_send()

        @pl.when(jnp.logical_and(spot == 0, row > 0))
        def _():
            def sent_down(place, carry):
                for target in range(chips):
                    down_copy(target, place).wait_send()
                return carry

            lax.fori_loop(0, span, sent_down, 0)

        for stream in range(1, len(tops)):
            @pl.when(spot == bottoms[stream - 1])
            def _():
                def sent_mid(place, carry):
                    for target in range(chips):
                        mid_copy(stream, target, place).wait_send()
                    return carry

                lax.fori_loop(0, tops[stream] + 1, sent_mid, 0)

        @pl.when(jnp.logical_not(one_of(bottoms)))
        def _():
            sweep_copy.wait_send()

        for target in others:
            end_copy(target).wait_send()

    for slot, target in enumerate(others):
        pack_copy(me, target, slot).wait_send()
    slab_copy(me, ahead, 0).wait_send()
    slab_copy(me, behind, 1).wait_send()
    slab_copy(me, partner, 2).wait_send()
    slab_copy(behind, ahead, 3).wait_send()
    slab_copy(behind, partner, 4).wait_send()
    slab_copy(ahead, partner, 5).wait_send()
    slab_copy(across_ring, partner, 6).wait_send()

    @pl.when(plane < planes - 1)
    def _():
        face_copy(plane + 1).wait_send()


def per_device(basis_flux, owner_cell, clogged, conductance, live_count, coupling, leakage, source):
    planes = lax.axis_size("flow")
    parts = lax.axis_size("trans")
    chips = parts // 2
    rows, order = basis_flux.shape[1:]
    span, depth = planes // 4, 16
    tops = (15, 10, 7, 4)
    streams = len(tops)
    width = order // chips
    turns = width // depth
    row = (1, order)
    piece = (1, width)
    vmem = pl.BlockSpec(memory_space=pltpu.VMEM)
    dma = pltpu.SemaphoreType.DMA
    half = pltpu.VMEM((order, order), BF16)
    return pl.pallas_call(
        functools.partial(kernel, planes, span, chips, rows, order, depth, tops),
        out_shape=jax.ShapeDtypeStruct((1, rows), F32),
        in_specs=[vmem] * 8,
        out_specs=vmem,
        scratch_shapes=[
            half, half, pltpu.VMEM(row, F32),
            half,
            pltpu.VMEM((parts, 16, rows), F32),
            half,
            pltpu.VMEM((order, order), F32),
            half, half, half,
            pltpu.VMEM((2, order), F32),
            pltpu.VMEM((2, order), F32),
            pltpu.VMEM(row, F32),
            pltpu.VMEM((width + depth, order), F32),
            pltpu.VMEM((width + depth, order), F32),
            pltpu.VMEM((streams * width, order), F32),
            pltpu.VMEM((streams * width, order), F32),
            pltpu.VMEM((streams * width, order), BF16),
            pltpu.VMEM((streams * width, order), BF16),
            *[pltpu.VMEM((width, order), BF16) for _ in range(4)],
            pltpu.VMEM(row, F32),
            *[pltpu.VMEM((chips, *piece), F32) for _ in range(3)],
            pltpu.VMEM((streams, chips, *piece), F32),
            pltpu.VMEM((chips, 1, rows), F32),
            pltpu.VMEM((parts, 1, rows), F32),
            pltpu.VMEM(piece, F32),
            pltpu.VMEM((streams, *piece), F32),
            *[pltpu.VMEM(row, F32) for _ in range(4)],
            dma((parts,)), dma((parts,)), dma((parts,)), dma((parts,)), dma, dma,
            dma((turns + 1,)), dma((turns + 1,)),
            dma((streams * turns,)), dma((streams * turns,)),
            dma((2, streams * turns)), dma((2, streams)),
            dma((streams, chips)), dma((chips,)), dma((span, chips)), dma((chips,)),
            dma((span,)), dma, dma((span, chips)), dma((streams, chips)), dma, dma,
            dma((parts,)), dma((chips,)),
        ],
        compiler_params=pltpu.CompilerParams(
            collective_id=0, has_side_effects=True, vmem_limit_bytes=VMEM_LIMIT
        ),
    )(basis_flux, owner_cell, clogged, conductance, live_count, coupling, leakage, source)


def solution(mesh):
    placed = (
        P("flow", "trans", None),
        P("flow", "trans"),
        P("flow", "trans"),
        P("flow", "trans"),
        P("flow", "trans"),
        P("flow", None),
        P("flow", None),
        P("flow", None),
    )
    return jax.shard_map(
        per_device, mesh=mesh, in_specs=placed, out_specs=P("flow", "trans"), check_vma=False
    )
```

```python
import functools

import jax
import jax.numpy as jnp
from jax import lax
from jax.experimental import pallas as pl
from jax.experimental.pallas import tpu as pltpu
from jax.sharding import PartitionSpec as P

MESH = pl.DeviceIdType.MESH
BF16 = jnp.bfloat16
F32 = jnp.float32
VMEM_LIMIT = 56 * 1024 * 1024


def dot(left, right):
    return jnp.dot(left, right, preferred_element_type=F32)


def split(value):
    high = value.astype(BF16)
    return high, (value - high.astype(F32)).astype(BF16)


def kernel(
    planes, span, chips, rows, order, depth, tops,
    basis, owner, clogged, conductance, live, coupling, leakage, source,
    pressure,
    near_high, near_low, inverse_diag,
    slabs, packs, picked, block, gain_high, gain_low, square, square_low, faces, faces_in, flux_diag,
    panel_in, panel_out, back_in, back_out, back_high, back_low,
    panel_high, panel_low, last_high, last_low,
    level, parts_out, up_pieces, down_pieces, edge_pieces, end_pieces, end_out,
    edge_up, edges, total, swept_in, swept, system_diag,
    slab_send, slab_recv, pack_send, pack_recv, face_send, face_recv, square_send, square_recv,
    panel_send, panel_recv, back_send, back_recv, held_send, held_recv,
    up_send, up_recv, down_send, down_recv,
    edge_send, edge_recv, mid_send, mid_recv, sweep_send, sweep_recv, end_send, end_recv,
):
    plane = lax.axis_index("flow")
    me = lax.axis_index("trans")
    parts = 2 * chips
    chip, core = me // 2, lax.rem(me, 2)
    partner = me + 1 - 2 * core
    spans = planes // span
    row, spot = plane // span, lax.rem(plane, span)
    row_start = row * span
    last = span - 1
    width = order // chips
    turns = width // depth
    bottoms = tuple(top + 1 for top in tops[1:]) + (0,)
    up_first = jnp.where(row > 0, 0, turns)
    pass_first = jnp.where(jnp.logical_and(row > 0, spot > 0), 0, turns)

    def one_of(places):
        return functools.reduce(jnp.logical_or, [spot == place for place in places])

    first_column = pl.multiple_of(chip * width, width)
    face = coupling[...]
    other_chips = [lax.rem(chip + turn, chips) for turn in range(1, chips)]
    step_rows = 256
    steps = order // step_rows

    barrier = pltpu.get_barrier_semaphore()

    def greet(target_plane, target):
        pl.semaphore_signal(barrier, inc=1, device_id=(target_plane, target), device_id_type=MESH)

    for turn in range(1, parts):
        greet(plane, lax.rem(me + turn, parts))

    @pl.when(plane > 0)
    def _():
        greet(plane - 1, me)

    @pl.when(plane < planes - 1)
    def _():
        greet(plane + 1, me)

    @pl.when(jnp.logical_and(core == 1, jnp.logical_and(row > 0, one_of(tops))))
    def _():
        for other in range(chips):
            greet(row_start - 1, other * 2 + 1)

    def slab(index):
        return slabs.at[:, pl.ds(pl.multiple_of(index * rows, rows), rows)]

    position = lax.broadcasted_iota(jnp.int32, (1, rows), 1)
    weight = (
        conductance[...]
        * (1 - clogged[...]).astype(F32)
        * (position < live[...]).astype(F32)
    ).astype(BF16).astype(F32)
    row_id = lax.broadcasted_iota(jnp.int32, (8, rows), 0)
    pack = jnp.where(row_id == 0, weight, owner[...].astype(F32))
    packs[me, 0:8, :] = pack
    turned = pack.T
    column = lax.broadcasted_iota(jnp.int32, (rows, order), 1).astype(F32)
    own_share = jnp.sum(
        jnp.where(turned[:, 1:2] == column, turned[:, 0:1], 0.0) * basis[0].astype(F32),
        axis=0, keepdims=True,
    )
    for index in range(order // rows):
        packs[me, 8 + index : 9 + index, :] = own_share[:, index * rows : (index + 1) * rows]
    slabs[:, pl.ds(pl.multiple_of(me * rows, rows), rows)] = basis[0].astype(F32).T.astype(BF16)

    next_to = jnp.where(plane > 0, 1, 0) + jnp.where(plane < planes - 1, 1, 0)
    sends_up = jnp.logical_and(core == 1, jnp.logical_and(spot == last, row < spans - 1))
    extra = jnp.where(sends_up, chips * len(tops), 0)
    pl.semaphore_wait(barrier, parts - 1 + next_to + extra)

    def slab_copy(index, target, slot):
        return pltpu.make_async_remote_copy(
            slab(index), slab(index), slab_send.at[slot], slab_recv.at[index],
            device_id=(plane, target), device_id_type=MESH,
        )

    def pack_copy(index, target, slot):
        return pltpu.make_async_remote_copy(
            packs.at[index], packs.at[index], pack_send.at[slot], pack_recv.at[index],
            device_id=(plane, target), device_id_type=MESH,
        )

    others = [lax.rem(me + turn, parts) for turn in range(1, parts)]
    for slot, target in enumerate(others):
        pack_copy(me, target, slot).start()
    way = 1 - 2 * core
    ahead = lax.rem(chip + way + chips, chips) * 2 + core
    behind = lax.rem(chip - way + chips, chips) * 2 + core
    across_ring = lax.rem(chip + 2, chips) * 2 + core
    slab_copy(me, ahead, 0).start()
    slab_copy(me, behind, 1).start()
    slab_copy(me, partner, 2).start()

    for other in others:
        pack_copy(other, partner, 0).wait_recv()

    shares = packs[0, 8:16, :]
    for index in range(1, parts):
        shares = shares + packs[index, 8:16, :]
    for index in range(order // rows):
        flux_diag[:, index * rows : (index + 1) * rows] = shares[index : index + 1, :]
    leak = leakage[...]
    schur = face * face / (face + leak + flux_diag[...])
    faces[0:1, :] = face
    faces[1:2, :] = schur

    def face_copy(target):
        return pltpu.make_async_remote_copy(
            faces, faces_in, face_send, face_recv, device_id=(target, me), device_id_type=MESH
        )

    @pl.when(plane < planes - 1)
    def _():
        face_copy(plane + 1).start()

    def pick(index, carry):
        turned = packs[index, 0:8, :].T
        picked[pl.ds(pl.multiple_of(index * rows, rows), rows), :] = jnp.where(
            turned[:, 1:2] == column, turned[:, 0:1], 0.0
        ).astype(BF16)
        return carry

    lax.fori_loop(0, parts, pick, 0)

    def chunk(index):
        return pl.ds(pl.multiple_of(index * step_rows, step_rows), step_rows)

    def from_chip(index, source_chip):
        slab_rows = pl.ds(pl.multiple_of(source_chip * 2 * rows, 2 * rows), 2 * rows)
        return dot(slabs[chunk(index), slab_rows], picked[slab_rows, :])

    def begin(index, carry):
        block[chunk(index), :] = from_chip(index, chip)
        return carry

    def add_chip(source_chip):
        def add(index, carry):
            block[chunk(index), :] = block[chunk(index), :] + from_chip(index, source_chip)
            return carry

        return add

    flip = 1 - 2 * core
    slab_copy(partner, partner, 0).wait_recv()
    lax.fori_loop(0, steps, begin, 0)
    slab_copy(behind, partner, 0).wait_recv()
    slab_copy(behind, ahead, 3).start()
    slab_copy(behind, partner, 4).start()
    slab_copy(ahead, partner, 0).wait_recv()
    slab_copy(ahead, partner, 5).start()
    slab_copy(ahead + flip, partner, 0).wait_recv()
    lax.fori_loop(0, steps, add_chip(ahead // 2), 0)
    slab_copy(across_ring, partner, 0).wait_recv()
    slab_copy(across_ring, partner, 6).start()
    slab_copy(behind + flip, partner, 0).wait_recv()
    lax.fori_loop(0, steps, add_chip(behind // 2), 0)

    @pl.when(plane > 0)
    def _():
        face_copy(plane).wait_recv()

    @pl.when(plane == 0)
    def _():
        faces_in[...] = jnp.zeros_like(faces_in)

    diag = flux_diag[...] + (leak + face + faces_in[0:1, :] - faces_in[1:2, :])
    pivots = 1.0 / diag
    inverse_diag[...] = pivots
    system_diag[...] = diag

    across = lax.broadcasted_iota(jnp.int32, (step_rows, order), 1)
    down = lax.broadcasted_iota(jnp.int32, (step_rows, order), 0)

    def scale(index, carry):
        here = chunk(index)
        whole = block[here, :] + from_chip(index, across_ring // 2)
        gain = jnp.where(across == down + index * step_rows, 0.0, whole * pivots)
        block[here, :] = gain
        gain_high[here, :], gain_low[here, :] = split(gain)
        return carry

    slab_copy(across_ring + flip, partner, 0).wait_recv()
    lax.fori_loop(0, steps, scale, 0)

    square_rows = 256
    half_rows = order // 2
    square_turns = half_rows // square_rows
    own_half = pl.ds(pl.multiple_of(core * half_rows, half_rows), half_rows)
    other_half = pl.ds(pl.multiple_of((1 - core) * half_rows, half_rows), half_rows)

    def square_copy(part, turn):
        ref = square_low if part else square
        here = pl.ds(pl.multiple_of(core * half_rows + turn * square_rows, square_rows), square_rows)
        return pltpu.make_async_remote_copy(
            ref.at[here, :], ref.at[here, :], square_send.at[part, turn], square_recv.at[part],
            device_id=(plane, partner), device_id_type=MESH,
        )

    def squared(turn, carry):
        first_row = turn * square_rows
        here = pl.ds(pl.multiple_of(core * half_rows + first_row, square_rows), square_rows)
        there = pl.ds(pl.multiple_of((1 - core) * half_rows + first_row, square_rows), square_rows)
        high, low = gain_high[here, :], gain_low[here, :]
        value = dot(high, gain_high[...]) + (dot(high, gain_low[...]) + dot(low, gain_high[...]))
        square[here, :], square_low[here, :] = split(value)
        square_copy(0, turn).start()
        square_copy(1, turn).start()
        block[here, :] = value - block[here, :]
        block[there, :] = -block[there, :]
        return carry

    lax.fori_loop(0, square_turns, squared, 0)

    def own_cubic(turn, carry):
        here = chunk(lax.rem(chip + turn, steps))
        block[here, :] = block[here, :] - dot(gain_high[here, own_half], square[own_half, :])
        return carry

    lax.fori_loop(0, steps, own_cubic, 0)
    for part, ref in enumerate((square, square_low)):
        pltpu.make_async_remote_copy(
            ref.at[other_half, :], ref.at[other_half, :],
            square_send.at[part, 0], square_recv.at[part],
            device_id=(plane, partner), device_id_type=MESH,
        ).wait_recv()

    def finish(turn, carry):
        index = lax.rem(chip + turn, steps)
        here = chunk(index)
        add = jnp.where(index // (steps // 2) == core, 0.0, 1.0)
        near = (
            block[here, :]
            - dot(gain_high[here, other_half], square[other_half, :])
            + add * (square[here, :].astype(F32) + square_low[here, :].astype(F32))
        )
        near_high[here, :], near_low[here, :] = split(near)
        return carry

    def remote(source_ref, target_ref, send, recv, target_plane, target):
        return pltpu.make_async_remote_copy(
            source_ref, target_ref, send, recv,
            device_id=(target_plane, target), device_id_type=MESH,
        )

    def apply(value):
        count = value.shape[0]
        scaled = value * inverse_diag[...]
        high = scaled.astype(BF16).astype(F32)
        both = jnp.concatenate([high, scaled - high], axis=0).astype(BF16)
        by_high = dot(both, near_high[...])
        by_low = dot(both[:count], near_low[...])
        return scaled + (by_high[:count] + (by_high[count:] + by_low)), both[:count], both[count:]

    def two_rows(value):
        row_id = lax.broadcasted_iota(jnp.int32, (8, value.shape[1]), 0)
        high = value.astype(BF16).astype(F32)
        return jnp.where(row_id == 0, high, jnp.where(row_id == 1, value - high, 0.0)).astype(BF16)

    def apply_one(value):
        scaled = value * inverse_diag[...]
        both = two_rows(scaled)
        return scaled + jnp.sum(
            dot(both, near_high[...]) + dot(both, near_low[...]), axis=0, keepdims=True
        )

    def by_panel(value, high, low):
        both = two_rows(value)
        return jnp.sum(dot(both, high[...]) + dot(both, low[...]), axis=0, keepdims=True)

    def take(index):
        return pl.ds(pl.multiple_of(index * depth, depth), depth)

    one_hot_row = lax.broadcasted_iota(jnp.int32, (depth, order), 0)
    one_hot_column = lax.broadcasted_iota(jnp.int32, (depth, order), 1)

    def unit_rows(index):
        return jnp.where(
            one_hot_column == one_hot_row + (chip * width + index * depth), 1.0, 0.0
        )

    def back_copy(index):
        return remote(
            back_out.at[take(index), :], back_in.at[take(index), :],
            back_send.at[index], back_recv.at[index], plane - 1, me,
        )

    def held_copy(index, half):
        ref = back_low if half else back_high
        return remote(
            ref.at[take(index), :], ref.at[take(index), :],
            held_send.at[half, index], held_recv.at[half, index // turns], plane, partner,
        )

    def stream_turns(stream):
        active = spot <= tops[stream]
        if stream == 0:
            active = jnp.logical_and(active, row < spans - 1)
        return jnp.where(active, turns, 0)

    def end_copy(target):
        return remote(
            end_out.at[target], end_pieces.at[chip], end_send.at[target], end_recv.at[chip],
            plane, target,
        )

    def end_from(source_chip):
        return remote(
            end_out.at[0], end_pieces.at[source_chip], end_send.at[0], end_recv.at[source_chip],
            plane, me,
        )

    def panel_copy(index):
        return remote(
            panel_out.at[take(index), :], panel_in.at[take(index), :],
            panel_send.at[index], panel_recv.at[index], plane + 1, me,
        )

    finish(0, 0)

    @pl.when(jnp.logical_and(core == 1, jnp.logical_and(spot == 0, row > 0)))
    def _():
        def first(turn, carry):
            here = pl.ds(pl.multiple_of(first_column + turn * depth, depth), depth)
            unit = unit_rows(turn) * pivots
            near = near_high[here, :].astype(F32) + near_low[here, :].astype(F32)
            panel_out[take(turn), :] = face * (unit + jnp.sum(unit, axis=1, keepdims=True) * near)
            panel_copy(turn).start()
            panel_high[take(turn), :], panel_low[take(turn), :] = split(unit)
            return carry

        lax.fori_loop(0, turns, first, 0)

    lax.fori_loop(1, steps, finish, 0)

    @pl.when(core == 0)
    def _():
        def flow_down(stream, top):
            def flow(turn, carry):
                index = stream * turns + turn

                @pl.when(spot == top)
                def _():
                    back_in[take(index), :] = unit_rows(turn)

                @pl.when(spot < top)
                def _():
                    back_copy(index).wait_recv()

                moved = apply(face * back_in[take(index), :])[0]
                back_out[take(index), :] = moved

                @pl.when(spot > 0)
                def _():
                    back_copy(index).start()

                back_high[take(index), :], back_low[take(index), :] = split(moved)
                held_copy(index, 0).start()
                held_copy(index, 1).start()
                return carry

            return flow

        def drain(stream):
            def wait(turn, carry):
                index = stream * turns + turn

                @pl.when(spot > 0)
                def _():
                    back_copy(index).wait_send()

                held_copy(index, 0).wait_send()
                held_copy(index, 1).wait_send()
                return carry

            return wait

        for stream in range(len(tops) - 1, -1, -1):
            lax.fori_loop(0, stream_turns(stream), flow_down(stream, tops[stream]), 0)
        for stream in range(len(tops) - 1, -1, -1):
            lax.fori_loop(0, stream_turns(stream), drain(stream), 0)
        for target in range(chips):
            end_from(target).wait_recv()
        pressure[...] = (end_pieces[0] + end_pieces[1]) + (end_pieces[2] + end_pieces[3])

    def up_copy(target, part):
        return remote(
            parts_out.at[target], up_pieces.at[chip],
            up_send.at[part, target], up_recv.at[chip],
            row_start + span + tops[part], target * 2 + 1,
        )

    def down_copy(target, place):
        return remote(
            parts_out.at[target], down_pieces.at[chip],
            down_send.at[place, target], down_recv.at[chip],
            row_start - span + place, target * 2 + 1,
        )

    def edge_copy(place):
        return remote(
            edge_up, edge_up, edge_send.at[place], edge_recv, row_start + place, me
        )

    def mid_copy(stream, target, place):
        return remote(
            parts_out.at[target], edge_pieces.at[stream, chip],
            mid_send.at[place, target], mid_recv.at[stream, chip],
            row_start + place, target * 2 + 1,
        )

    sweep_copy = remote(swept, swept_in, sweep_send, sweep_recv, plane - 1, me)

    def cut(value, ref, count, size):
        for index in range(count):
            ref[index] = value[:, index * size : (index + 1) * size]

    @pl.when(core == 1)
    def _():
        def flow(index, carry):
            @pl.when(spot > 0)
            def _():
                panel_copy(index).wait_recv()

            @pl.when(index == turns)
            def _():
                @pl.when(spot == 0)
                def _():
                    panel_in[take(index), :] = jnp.zeros((depth, order), F32)

                panel_in[take(index), :] = panel_in[take(index), :] + jnp.where(
                    one_hot_row == 0, source[...], 0.0
                )

            arrived_rows = panel_in[take(index), :]
            scaled = arrived_rows * inverse_diag[...]
            high = scaled.astype(BF16)
            low = (scaled - high.astype(F32)).astype(BF16)
            both = jnp.concatenate([high, low], axis=0)
            def advance(pass_on):
                size = order // 2
                for block in range(order // size):
                    across = slice(block * size, (block + 1) * size)
                    by_high = dot(both, near_high[:, across])
                    by_low = dot(high, near_low[:, across])
                    panel_out[take(index), across] = face[:, across] * (
                        scaled[:, across] + (by_high[:depth] + (by_high[depth:] + by_low))
                    )
                    if pass_on:
                        remote(
                            panel_out.at[take(index), across], panel_in.at[take(index), across],
                            panel_send.at[index], panel_recv.at[index], plane + 1, me,
                        ).start()

            @pl.when(spot < last)
            def _():
                advance(True)

            @pl.when(spot == last)
            def _():
                advance(False)

            @pl.when(index < turns)
            def _():
                panel_high[take(index), :] = high
                panel_low[take(index), :] = low

                @pl.when(spot == last)
                def _():
                    last_high[take(index), :], last_low[take(index), :] = split(
                        panel_out[take(index), :]
                    )

            return carry

        lax.fori_loop(pass_first, turns + 1, flow, 0)
        level[...] = jnp.where(chip == 0, panel_in[width : width + 1, :], 0.0)

        def gather_pieces(pieces, sems):
            for target in range(chips):
                remote(
                    parts_out.at[target], pieces.at[target], end_send.at[0], sems.at[target],
                    plane, me,
                ).wait_recv()
            return (pieces[0] + pieces[1]) + (pieces[2] + pieces[3])

        @pl.when(jnp.logical_and(row > 0, one_of(tops)))
        def _():
            edge_up[...] = gather_pieces(up_pieces, up_recv)

        @pl.when(jnp.logical_and(spot == last, row < spans - 1))
        def _():
            @pl.when(row == 0)
            def _():
                parts_out[...] = jnp.zeros_like(parts_out)

            @pl.when(row > 0)
            def _():
                cut(by_panel(edge_up[...], last_high, last_low), parts_out, chips, width)

            parts_out[chip] = parts_out[chip] + panel_out[
                width : width + 1, pl.ds(first_column, width)
            ]
            for part in range(len(tops)):
                for target in range(chips):
                    up_copy(target, part).start()

        @pl.when(row > 0)
        def _():
            for top, bottom in zip(tops, bottoms):
                @pl.when(spot == top)
                def _():
                    for place in range(top - 1, bottom - 1, -1):
                        edge_copy(place).start()

            @pl.when(jnp.logical_not(one_of(tops)))
            def _():
                edge_copy(0).wait_recv()

            level[...] = level[...] + system_diag[...] * by_panel(
                edge_up[...], panel_high, panel_low
            )

        @pl.when(jnp.logical_not(one_of(tops)))
        def _():
            sweep_copy.wait_recv()
            level[...] = level[...] + face * swept_in[...]

        swept[...] = apply_one(level[...])

        @pl.when(jnp.logical_not(one_of(bottoms)))
        def _():
            sweep_copy.start()

        for stream in range(1, len(tops)):
            @pl.when(spot == bottoms[stream - 1])
            def _():
                cut(swept[...], parts_out, chips, width)

                def send_mid(place, carry):
                    for target in range(chips):
                        mid_copy(stream, target, place).start()
                    return carry

                lax.fori_loop(0, tops[stream] + 1, send_mid, 0)

        def arrived(stream):
            here = pl.ds(stream * width, width)
            for half, ref in enumerate((back_high, back_low)):
                remote(
                    ref.at[here, :], ref.at[here, :],
                    held_send.at[half, 0], held_recv.at[half, stream], plane, me,
                ).wait_recv()

        def by_stream(stream):
            here = slice(stream * width, (stream + 1) * width)
            return by_panel(edges[stream], back_high.at[here, :], back_low.at[here, :])

        total[...] = swept[...]
        for stream in range(len(tops) - 1, -1, -1):
            @pl.when(stream_turns(stream) > 0)
            def _():
                arrived(stream)

        for stream in range(1, len(tops)):
            @pl.when(spot <= tops[stream])
            def _():
                edges[stream] = gather_pieces(edge_pieces.at[stream], mid_recv.at[stream])
                total[...] = total[...] + by_stream(stream)

        @pl.when(row < spans - 1)
        def _():
            edges[0] = gather_pieces(down_pieces, down_recv)
            total[...] = total[...] + by_stream(0)

        @pl.when(jnp.logical_and(spot == 0, row > 0))
        def _():
            cut(total[...], parts_out, chips, width)

            def send_down(place, carry):
                for target in range(chips):
                    down_copy(target, place).start()
                return carry

            lax.fori_loop(0, span, send_down, 0)

        cut(total[...], end_out, parts, rows)
        for target in others:
            end_copy(target).start()
        end_pieces[chip] = end_out[me]
        for other in other_chips:
            end_from(other).wait_recv()
        pressure[...] = (end_pieces[0] + end_pieces[1]) + (end_pieces[2] + end_pieces[3])

        @pl.when(spot < last)
        def _():
            def drain(index, carry):
                panel_copy(index).wait_send()
                return carry

            lax.fori_loop(up_first, turns + 1, drain, 0)

        @pl.when(jnp.logical_and(spot == last, row < spans - 1))
        def _():
            for part in range(len(tops)):
                for target in range(chips):
                    up_copy(target, part).wait_send()

        @pl.when(row > 0)
        def _():
            for top, bottom in zip(tops, bottoms):
                @pl.when(spot == top)
                def _():
                    for place in range(top - 1, bottom - 1, -1):
                        edge_copy(place).wait_send()

        @pl.when(jnp.logical_and(spot == 0, row > 0))
        def _():
            def sent_down(place, carry):
                for target in range(chips):
                    down_copy(target, place).wait_send()
                return carry

            lax.fori_loop(0, span, sent_down, 0)

        for stream in range(1, len(tops)):
            @pl.when(spot == bottoms[stream - 1])
            def _():
                def sent_mid(place, carry):
                    for target in range(chips):
                        mid_copy(stream, target, place).wait_send()
                    return carry

                lax.fori_loop(0, tops[stream] + 1, sent_mid, 0)

        @pl.when(jnp.logical_not(one_of(bottoms)))
        def _():
            sweep_copy.wait_send()

        for target in others:
            end_copy(target).wait_send()

    for slot, target in enumerate(others):
        pack_copy(me, target, slot).wait_send()
    for turn in range(square_turns):
        square_copy(0, turn).wait_send()
        square_copy(1, turn).wait_send()
    slab_copy(me, ahead, 0).wait_send()
    slab_copy(me, behind, 1).wait_send()
    slab_copy(me, partner, 2).wait_send()
    slab_copy(behind, ahead, 3).wait_send()
    slab_copy(behind, partner, 4).wait_send()
    slab_copy(ahead, partner, 5).wait_send()
    slab_copy(across_ring, partner, 6).wait_send()

    @pl.when(plane < planes - 1)
    def _():
        face_copy(plane + 1).wait_send()


def per_device(basis_flux, owner_cell, clogged, conductance, live_count, coupling, leakage, source):
    planes = lax.axis_size("flow")
    parts = lax.axis_size("trans")
    chips = parts // 2
    rows, order = basis_flux.shape[1:]
    span, depth = planes // 4, 16
    tops = (15, 11, 8, 6, 4)
    streams = len(tops)
    width = order // chips
    turns = width // depth
    row = (1, order)
    piece = (1, width)
    vmem = pl.BlockSpec(memory_space=pltpu.VMEM)
    dma = pltpu.SemaphoreType.DMA
    half = pltpu.VMEM((order, order), BF16)
    return pl.pallas_call(
        functools.partial(kernel, planes, span, chips, rows, order, depth, tops),
        out_shape=jax.ShapeDtypeStruct((1, rows), F32),
        in_specs=[vmem] * 8,
        out_specs=vmem,
        scratch_shapes=[
            half, half, pltpu.VMEM(row, F32),
            half,
            pltpu.VMEM((parts, 16, rows), F32),
            half,
            pltpu.VMEM((order, order), F32),
            half, half, half, half,
            pltpu.VMEM((2, order), F32),
            pltpu.VMEM((2, order), F32),
            pltpu.VMEM(row, F32),
            pltpu.VMEM((width + depth, order), F32),
            pltpu.VMEM((width + depth, order), F32),
            pltpu.VMEM((streams * width, order), F32),
            pltpu.VMEM((streams * width, order), F32),
            pltpu.VMEM((streams * width, order), BF16),
            pltpu.VMEM((streams * width, order), BF16),
            *[pltpu.VMEM((width, order), BF16) for _ in range(4)],
            pltpu.VMEM(row, F32),
            *[pltpu.VMEM((chips, *piece), F32) for _ in range(3)],
            pltpu.VMEM((streams, chips, *piece), F32),
            pltpu.VMEM((chips, 1, rows), F32),
            pltpu.VMEM((parts, 1, rows), F32),
            pltpu.VMEM(piece, F32),
            pltpu.VMEM((streams, *piece), F32),
            *[pltpu.VMEM(row, F32) for _ in range(4)],
            dma((parts,)), dma((parts,)), dma((parts,)), dma((parts,)), dma, dma,
            dma((2, 4)), dma((2,)),
            dma((turns + 1,)), dma((turns + 1,)),
            dma((streams * turns,)), dma((streams * turns,)),
            dma((2, streams * turns)), dma((2, streams)),
            dma((streams, chips)), dma((chips,)), dma((span, chips)), dma((chips,)),
            dma((span,)), dma, dma((span, chips)), dma((streams, chips)), dma, dma,
            dma((parts,)), dma((chips,)),
        ],
        compiler_params=pltpu.CompilerParams(
            collective_id=0, has_side_effects=True, vmem_limit_bytes=VMEM_LIMIT
        ),
    )(basis_flux, owner_cell, clogged, conductance, live_count, coupling, leakage, source)


def solution(mesh):
    placed = (
        P("flow", "trans", None),
        P("flow", "trans"),
        P("flow", "trans"),
        P("flow", "trans"),
        P("flow", "trans"),
        P("flow", None),
        P("flow", None),
        P("flow", None),
    )
    return jax.shard_map(
        per_device, mesh=mesh, in_specs=placed, out_specs=P("flow", "trans"), check_vma=False
    )
```

```python
import functools

import jax
import jax.numpy as jnp
from jax import lax
from jax.experimental import pallas as pl
from jax.experimental.pallas import tpu as pltpu
from jax.sharding import PartitionSpec as P

MESH = pl.DeviceIdType.MESH
BF16 = jnp.bfloat16
F32 = jnp.float32
VMEM_LIMIT = 56 * 1024 * 1024


def dot(left, right):
    return jnp.dot(left, right, preferred_element_type=F32)


def split(value):
    high = value.astype(BF16)
    return high, (value - high.astype(F32)).astype(BF16)


def kernel(
    planes, span, chips, rows, order, depth, tops,
    basis_in, owner_in, clogged_in, conductance_in, live_in, coupling_in, leakage_in, source_in,
    pressure,
    basis, owner, clogged, conductance, live, coupling, leakage, source, fetched,
    near_high, near_low, inverse_diag,
    slabs, packs, picked, block, gain_high, gain_low, square, square_low, faces, faces_in, flux_diag,
    panel_in, panel_out, back_in, back_out, back_high, back_low,
    panel_high, panel_low, last_high, last_low,
    level, parts_out, up_pieces, down_pieces, edge_pieces, end_pieces, end_out,
    edge_up, edges, total, swept_in, swept, system_diag,
    slab_send, slab_recv, pack_send, pack_recv, face_send, face_recv, square_send, square_recv,
    panel_send, panel_recv, back_send, back_recv, held_send, held_recv,
    up_send, up_recv, down_send, down_recv,
    edge_send, edge_recv, mid_send, mid_recv, sweep_send, sweep_recv, end_send, end_recv,
):
    plane = lax.axis_index("flow")
    me = lax.axis_index("trans")
    parts = 2 * chips
    chip, core = me // 2, lax.rem(me, 2)
    partner = me + 1 - 2 * core
    spans = planes // span
    row, spot = plane // span, lax.rem(plane, span)
    row_start = row * span
    last = span - 1
    width = order // chips
    turns = width // depth
    bottoms = tuple(top + 1 for top in tops[1:]) + (0,)
    up_first = jnp.where(row > 0, 0, turns)
    pass_first = jnp.where(jnp.logical_and(row > 0, spot > 0), 0, turns)

    def one_of(places):
        return functools.reduce(jnp.logical_or, [spot == place for place in places])

    first_column = pl.multiple_of(chip * width, width)
    other_chips = [lax.rem(chip + turn, chips) for turn in range(1, chips)]
    step_rows = 256
    steps = order // step_rows

    given = (
        basis_in, owner_in, clogged_in, conductance_in, live_in, coupling_in, leakage_in, source_in
    )
    held = (basis, owner, clogged, conductance, live, coupling, leakage, source)
    fetches = [
        pltpu.make_async_copy(given[index], held[index], fetched.at[index])
        for index in range(len(given))
    ]
    for fetch in fetches:
        fetch.start()

    barrier = pltpu.get_barrier_semaphore()

    def greet(target_plane, target):
        pl.semaphore_signal(barrier, inc=1, device_id=(target_plane, target), device_id_type=MESH)

    for turn in range(1, parts):
        greet(plane, lax.rem(me + turn, parts))

    @pl.when(plane > 0)
    def _():
        greet(plane - 1, me)

    @pl.when(plane < planes - 1)
    def _():
        greet(plane + 1, me)

    @pl.when(jnp.logical_and(core == 1, jnp.logical_and(row > 0, one_of(tops))))
    def _():
        for other in range(chips):
            greet(row_start - 1, other * 2 + 1)

    def slab(index):
        return slabs.at[:, pl.ds(pl.multiple_of(index * rows, rows), rows)]

    for fetch in fetches:
        fetch.wait()
    face = coupling[...]
    position = lax.broadcasted_iota(jnp.int32, (1, rows), 1)
    weight = (
        conductance[...]
        * (1 - clogged[...]).astype(F32)
        * (position < live[...]).astype(F32)
    ).astype(BF16).astype(F32)
    row_id = lax.broadcasted_iota(jnp.int32, (8, rows), 0)
    pack = jnp.where(row_id == 0, weight, owner[...].astype(F32))
    packs[me, 0:8, :] = pack
    turned = pack.T
    column = lax.broadcasted_iota(jnp.int32, (rows, order), 1).astype(F32)
    own_share = jnp.sum(
        jnp.where(turned[:, 1:2] == column, turned[:, 0:1], 0.0) * basis[0].astype(F32),
        axis=0, keepdims=True,
    )
    for index in range(order // rows):
        packs[me, 8 + index : 9 + index, :] = own_share[:, index * rows : (index + 1) * rows]
    slabs[:, pl.ds(pl.multiple_of(me * rows, rows), rows)] = basis[0].astype(F32).T.astype(BF16)

    next_to = jnp.where(plane > 0, 1, 0) + jnp.where(plane < planes - 1, 1, 0)
    sends_up = jnp.logical_and(core == 1, jnp.logical_and(spot == last, row < spans - 1))
    extra = jnp.where(sends_up, chips * len(tops), 0)
    pl.semaphore_wait(barrier, parts - 1 + next_to + extra)

    def slab_copy(index, target, slot):
        return pltpu.make_async_remote_copy(
            slab(index), slab(index), slab_send.at[slot], slab_recv.at[index],
            device_id=(plane, target), device_id_type=MESH,
        )

    def pack_copy(index, target, slot):
        return pltpu.make_async_remote_copy(
            packs.at[index], packs.at[index], pack_send.at[slot], pack_recv.at[index],
            device_id=(plane, target), device_id_type=MESH,
        )

    others = [lax.rem(me + turn, parts) for turn in range(1, parts)]
    for slot, target in enumerate(others):
        pack_copy(me, target, slot).start()
    way = 1 - 2 * core
    ahead = lax.rem(chip + way + chips, chips) * 2 + core
    behind = lax.rem(chip - way + chips, chips) * 2 + core
    across_ring = lax.rem(chip + 2, chips) * 2 + core
    slab_copy(me, ahead, 0).start()
    slab_copy(me, behind, 1).start()
    slab_copy(me, partner, 2).start()

    for other in others:
        pack_copy(other, partner, 0).wait_recv()

    shares = packs[0, 8:16, :]
    for index in range(1, parts):
        shares = shares + packs[index, 8:16, :]
    for index in range(order // rows):
        flux_diag[:, index * rows : (index + 1) * rows] = shares[index : index + 1, :]
    leak = leakage[...]
    schur = face * face / (face + leak + flux_diag[...])
    faces[0:1, :] = face
    faces[1:2, :] = schur

    def face_copy(target):
        return pltpu.make_async_remote_copy(
            faces, faces_in, face_send, face_recv, device_id=(target, me), device_id_type=MESH
        )

    @pl.when(plane < planes - 1)
    def _():
        face_copy(plane + 1).start()

    def pick(index, carry):
        turned = packs[index, 0:8, :].T
        picked[pl.ds(pl.multiple_of(index * rows, rows), rows), :] = jnp.where(
            turned[:, 1:2] == column, turned[:, 0:1], 0.0
        ).astype(BF16)
        return carry

    lax.fori_loop(0, parts, pick, 0)

    def chunk(index):
        return pl.ds(pl.multiple_of(index * step_rows, step_rows), step_rows)

    def from_chip(index, source_chip):
        slab_rows = pl.ds(pl.multiple_of(source_chip * 2 * rows, 2 * rows), 2 * rows)
        return dot(slabs[chunk(index), slab_rows], picked[slab_rows, :])

    def begin(index, carry):
        block[chunk(index), :] = from_chip(index, chip)
        return carry

    def add_chip(source_chip):
        def add(index, carry):
            block[chunk(index), :] = block[chunk(index), :] + from_chip(index, source_chip)
            return carry

        return add

    flip = 1 - 2 * core
    slab_copy(partner, partner, 0).wait_recv()
    lax.fori_loop(0, steps, begin, 0)
    slab_copy(behind, partner, 0).wait_recv()
    slab_copy(behind, ahead, 3).start()
    slab_copy(behind, partner, 4).start()
    slab_copy(ahead, partner, 0).wait_recv()
    slab_copy(ahead, partner, 5).start()
    slab_copy(ahead + flip, partner, 0).wait_recv()
    lax.fori_loop(0, steps, add_chip(ahead // 2), 0)
    slab_copy(across_ring, partner, 0).wait_recv()
    slab_copy(across_ring, partner, 6).start()
    slab_copy(behind + flip, partner, 0).wait_recv()
    lax.fori_loop(0, steps, add_chip(behind // 2), 0)

    @pl.when(plane > 0)
    def _():
        face_copy(plane).wait_recv()

    @pl.when(plane == 0)
    def _():
        faces_in[...] = jnp.zeros_like(faces_in)

    diag = flux_diag[...] + (leak + face + faces_in[0:1, :] - faces_in[1:2, :])
    pivots = 1.0 / diag
    inverse_diag[...] = pivots
    system_diag[...] = diag

    across = lax.broadcasted_iota(jnp.int32, (step_rows, order), 1)
    down = lax.broadcasted_iota(jnp.int32, (step_rows, order), 0)

    def scale(index, carry):
        here = chunk(index)
        whole = block[here, :] + from_chip(index, across_ring // 2)
        gain = jnp.where(across == down + index * step_rows, 0.0, whole * pivots)
        block[here, :] = gain
        gain_high[here, :], gain_low[here, :] = split(gain)
        return carry

    slab_copy(across_ring + flip, partner, 0).wait_recv()
    lax.fori_loop(0, steps, scale, 0)

    square_rows = 256
    half_rows = order // 2
    square_turns = half_rows // square_rows
    own_half = pl.ds(pl.multiple_of(core * half_rows, half_rows), half_rows)
    other_half = pl.ds(pl.multiple_of((1 - core) * half_rows, half_rows), half_rows)

    def square_copy(part, turn):
        ref = square_low if part else square
        here = pl.ds(pl.multiple_of(core * half_rows + turn * square_rows, square_rows), square_rows)
        return pltpu.make_async_remote_copy(
            ref.at[here, :], ref.at[here, :], square_send.at[part, turn], square_recv.at[part],
            device_id=(plane, partner), device_id_type=MESH,
        )

    def squared(turn, carry):
        first_row = turn * square_rows
        here = pl.ds(pl.multiple_of(core * half_rows + first_row, square_rows), square_rows)
        there = pl.ds(pl.multiple_of((1 - core) * half_rows + first_row, square_rows), square_rows)
        high, low = gain_high[here, :], gain_low[here, :]
        value = dot(high, gain_high[...]) + (dot(high, gain_low[...]) + dot(low, gain_high[...]))
        square[here, :], square_low[here, :] = split(value)
        square_copy(0, turn).start()
        square_copy(1, turn).start()
        block[here, :] = value - block[here, :]
        block[there, :] = -block[there, :]
        return carry

    lax.fori_loop(0, square_turns, squared, 0)

    def own_cubic(turn, carry):
        here = chunk(lax.rem(chip + turn, steps))
        block[here, :] = block[here, :] - dot(gain_high[here, own_half], square[own_half, :])
        return carry

    lax.fori_loop(0, steps, own_cubic, 0)
    for part, ref in enumerate((square, square_low)):
        pltpu.make_async_remote_copy(
            ref.at[other_half, :], ref.at[other_half, :],
            square_send.at[part, 0], square_recv.at[part],
            device_id=(plane, partner), device_id_type=MESH,
        ).wait_recv()

    def finish(turn, carry):
        index = lax.rem(chip + turn, steps)
        here = chunk(index)
        add = jnp.where(index // (steps // 2) == core, 0.0, 1.0)
        near = (
            block[here, :]
            - dot(gain_high[here, other_half], square[other_half, :])
            + add * (square[here, :].astype(F32) + square_low[here, :].astype(F32))
        )
        near_high[here, :], near_low[here, :] = split(near)
        return carry

    def remote(source_ref, target_ref, send, recv, target_plane, target):
        return pltpu.make_async_remote_copy(
            source_ref, target_ref, send, recv,
            device_id=(target_plane, target), device_id_type=MESH,
        )

    def apply(value):
        count = value.shape[0]
        scaled = value * inverse_diag[...]
        high = scaled.astype(BF16).astype(F32)
        both = jnp.concatenate([high, scaled - high], axis=0).astype(BF16)
        by_high = dot(both, near_high[...])
        by_low = dot(both[:count], near_low[...])
        return scaled + (by_high[:count] + (by_high[count:] + by_low)), both[:count], both[count:]

    def two_rows(value):
        row_id = lax.broadcasted_iota(jnp.int32, (8, value.shape[1]), 0)
        high = value.astype(BF16).astype(F32)
        return jnp.where(row_id == 0, high, jnp.where(row_id == 1, value - high, 0.0)).astype(BF16)

    def apply_one(value):
        scaled = value * inverse_diag[...]
        both = two_rows(scaled)
        return scaled + jnp.sum(
            dot(both, near_high[...]) + dot(both, near_low[...]), axis=0, keepdims=True
        )

    def by_panel(value, high, low):
        both = two_rows(value)
        return jnp.sum(dot(both, high[...]) + dot(both, low[...]), axis=0, keepdims=True)

    def take(index):
        return pl.ds(pl.multiple_of(index * depth, depth), depth)

    one_hot_row = lax.broadcasted_iota(jnp.int32, (depth, order), 0)
    one_hot_column = lax.broadcasted_iota(jnp.int32, (depth, order), 1)

    def unit_rows(index):
        return jnp.where(
            one_hot_column == one_hot_row + (chip * width + index * depth), 1.0, 0.0
        )

    def back_copy(index):
        return remote(
            back_out.at[take(index), :], back_in.at[take(index), :],
            back_send.at[index], back_recv.at[index], plane - 1, me,
        )

    def held_copy(index, half):
        ref = back_low if half else back_high
        return remote(
            ref.at[take(index), :], ref.at[take(index), :],
            held_send.at[half, index], held_recv.at[half, index // turns], plane, partner,
        )

    def stream_turns(stream):
        active = spot <= tops[stream]
        if stream == 0:
            active = jnp.logical_and(active, row < spans - 1)
        return jnp.where(active, turns, 0)

    def end_copy(target):
        return remote(
            end_out.at[target], end_pieces.at[chip], end_send.at[target], end_recv.at[chip],
            plane, target,
        )

    def end_from(source_chip):
        return remote(
            end_out.at[0], end_pieces.at[source_chip], end_send.at[0], end_recv.at[source_chip],
            plane, me,
        )

    def panel_copy(index):
        return remote(
            panel_out.at[take(index), :], panel_in.at[take(index), :],
            panel_send.at[index], panel_recv.at[index], plane + 1, me,
        )

    finish(0, 0)

    @pl.when(jnp.logical_and(core == 1, jnp.logical_and(spot == 0, row > 0)))
    def _():
        def first(turn, carry):
            here = pl.ds(pl.multiple_of(first_column + turn * depth, depth), depth)
            unit = unit_rows(turn) * pivots
            near = near_high[here, :].astype(F32) + near_low[here, :].astype(F32)
            panel_out[take(turn), :] = face * (unit + jnp.sum(unit, axis=1, keepdims=True) * near)
            panel_copy(turn).start()
            panel_high[take(turn), :], panel_low[take(turn), :] = split(unit)
            return carry

        lax.fori_loop(0, turns, first, 0)

    lax.fori_loop(1, steps, finish, 0)

    @pl.when(core == 0)
    def _():
        def flow_down(stream, top):
            def flow(turn, carry):
                index = stream * turns + turn

                @pl.when(spot == top)
                def _():
                    back_in[take(index), :] = unit_rows(turn)

                @pl.when(spot < top)
                def _():
                    back_copy(index).wait_recv()

                moved = apply(face * back_in[take(index), :])[0]
                back_out[take(index), :] = moved

                @pl.when(spot > 0)
                def _():
                    back_copy(index).start()

                back_high[take(index), :], back_low[take(index), :] = split(moved)
                held_copy(index, 0).start()
                held_copy(index, 1).start()
                return carry

            return flow

        def drain(stream):
            def wait(turn, carry):
                index = stream * turns + turn

                @pl.when(spot > 0)
                def _():
                    back_copy(index).wait_send()

                held_copy(index, 0).wait_send()
                held_copy(index, 1).wait_send()
                return carry

            return wait

        for stream in range(len(tops) - 1, -1, -1):
            lax.fori_loop(0, stream_turns(stream), flow_down(stream, tops[stream]), 0)
        for stream in range(len(tops) - 1, -1, -1):
            lax.fori_loop(0, stream_turns(stream), drain(stream), 0)
        for target in range(chips):
            end_from(target).wait_recv()
        pressure[...] = (end_pieces[0] + end_pieces[1]) + (end_pieces[2] + end_pieces[3])

    def up_copy(target, part):
        return remote(
            parts_out.at[target], up_pieces.at[chip],
            up_send.at[part, target], up_recv.at[chip],
            row_start + span + tops[part], target * 2 + 1,
        )

    def down_copy(target, place):
        return remote(
            parts_out.at[target], down_pieces.at[chip],
            down_send.at[place, target], down_recv.at[chip],
            row_start - span + place, target * 2 + 1,
        )

    def edge_copy(place):
        return remote(
            edge_up, edge_up, edge_send.at[place], edge_recv, row_start + place, me
        )

    def mid_copy(stream, target, place):
        return remote(
            parts_out.at[target], edge_pieces.at[stream, chip],
            mid_send.at[place, target], mid_recv.at[stream, chip],
            row_start + place, target * 2 + 1,
        )

    sweep_copy = remote(swept, swept_in, sweep_send, sweep_recv, plane - 1, me)

    def cut(value, ref, count, size):
        for index in range(count):
            ref[index] = value[:, index * size : (index + 1) * size]

    @pl.when(core == 1)
    def _():
        def flow(index, carry):
            @pl.when(spot > 0)
            def _():
                panel_copy(index).wait_recv()

            @pl.when(index == turns)
            def _():
                @pl.when(spot == 0)
                def _():
                    panel_in[take(index), :] = jnp.zeros((depth, order), F32)

                panel_in[take(index), :] = panel_in[take(index), :] + jnp.where(
                    one_hot_row == 0, source[...], 0.0
                )

            arrived_rows = panel_in[take(index), :]
            scaled = arrived_rows * inverse_diag[...]
            high = scaled.astype(BF16)
            low = (scaled - high.astype(F32)).astype(BF16)
            both = jnp.concatenate([high, low], axis=0)
            def advance(pass_on):
                size = order // 2
                for block in range(order // size):
                    across = slice(block * size, (block + 1) * size)
                    by_high = dot(both, near_high[:, across])
                    by_low = dot(high, near_low[:, across])
                    panel_out[take(index), across] = face[:, across] * (
                        scaled[:, across] + (by_high[:depth] + (by_high[depth:] + by_low))
                    )
                    if pass_on:
                        remote(
                            panel_out.at[take(index), across], panel_in.at[take(index), across],
                            panel_send.at[index], panel_recv.at[index], plane + 1, me,
                        ).start()

            @pl.when(spot < last)
            def _():
                advance(True)

            @pl.when(spot == last)
            def _():
                advance(False)

            @pl.when(index < turns)
            def _():
                panel_high[take(index), :] = high
                panel_low[take(index), :] = low

                @pl.when(spot == last)
                def _():
                    last_high[take(index), :], last_low[take(index), :] = split(
                        panel_out[take(index), :]
                    )

            return carry

        lax.fori_loop(pass_first, turns + 1, flow, 0)
        level[...] = jnp.where(chip == 0, panel_in[width : width + 1, :], 0.0)

        def gather_pieces(pieces, sems):
            for target in range(chips):
                remote(
                    parts_out.at[target], pieces.at[target], end_send.at[0], sems.at[target],
                    plane, me,
                ).wait_recv()
            return (pieces[0] + pieces[1]) + (pieces[2] + pieces[3])

        @pl.when(jnp.logical_and(row > 0, one_of(tops)))
        def _():
            edge_up[...] = gather_pieces(up_pieces, up_recv)

        @pl.when(jnp.logical_and(spot == last, row < spans - 1))
        def _():
            @pl.when(row == 0)
            def _():
                parts_out[...] = jnp.zeros_like(parts_out)

            @pl.when(row > 0)
            def _():
                cut(by_panel(edge_up[...], last_high, last_low), parts_out, chips, width)

            parts_out[chip] = parts_out[chip] + panel_out[
                width : width + 1, pl.ds(first_column, width)
            ]
            for part in range(len(tops)):
                for target in range(chips):
                    up_copy(target, part).start()

        @pl.when(row > 0)
        def _():
            for top, bottom in zip(tops, bottoms):
                @pl.when(spot == top)
                def _():
                    for place in range(top - 1, bottom - 1, -1):
                        edge_copy(place).start()

            @pl.when(jnp.logical_not(one_of(tops)))
            def _():
                edge_copy(0).wait_recv()

            level[...] = level[...] + system_diag[...] * by_panel(
                edge_up[...], panel_high, panel_low
            )

        @pl.when(jnp.logical_not(one_of(tops)))
        def _():
            sweep_copy.wait_recv()
            level[...] = level[...] + face * swept_in[...]

        swept[...] = apply_one(level[...])

        @pl.when(jnp.logical_not(one_of(bottoms)))
        def _():
            sweep_copy.start()

        for stream in range(1, len(tops)):
            @pl.when(spot == bottoms[stream - 1])
            def _():
                cut(swept[...], parts_out, chips, width)

                def send_mid(place, carry):
                    for target in range(chips):
                        mid_copy(stream, target, place).start()
                    return carry

                lax.fori_loop(0, tops[stream] + 1, send_mid, 0)

        def arrived(stream):
            here = pl.ds(stream * width, width)
            for half, ref in enumerate((back_high, back_low)):
                remote(
                    ref.at[here, :], ref.at[here, :],
                    held_send.at[half, 0], held_recv.at[half, stream], plane, me,
                ).wait_recv()

        def by_stream(stream):
            here = slice(stream * width, (stream + 1) * width)
            return by_panel(edges[stream], back_high.at[here, :], back_low.at[here, :])

        total[...] = swept[...]
        for stream in range(len(tops) - 1, -1, -1):
            @pl.when(stream_turns(stream) > 0)
            def _():
                arrived(stream)

        for stream in range(1, len(tops)):
            @pl.when(spot <= tops[stream])
            def _():
                edges[stream] = gather_pieces(edge_pieces.at[stream], mid_recv.at[stream])
                total[...] = total[...] + by_stream(stream)

        @pl.when(row < spans - 1)
        def _():
            edges[0] = gather_pieces(down_pieces, down_recv)
            total[...] = total[...] + by_stream(0)

        @pl.when(jnp.logical_and(spot == 0, row > 0))
        def _():
            cut(total[...], parts_out, chips, width)

            def send_down(place, carry):
                for target in range(chips):
                    down_copy(target, place).start()
                return carry

            lax.fori_loop(0, span, send_down, 0)

        cut(total[...], end_out, parts, rows)
        for target in others:
            end_copy(target).start()
        end_pieces[chip] = end_out[me]
        for other in other_chips:
            end_from(other).wait_recv()
        pressure[...] = (end_pieces[0] + end_pieces[1]) + (end_pieces[2] + end_pieces[3])

        @pl.when(spot < last)
        def _():
            def drain(index, carry):
                panel_copy(index).wait_send()
                return carry

            lax.fori_loop(up_first, turns + 1, drain, 0)

        @pl.when(jnp.logical_and(spot == last, row < spans - 1))
        def _():
            for part in range(len(tops)):
                for target in range(chips):
                    up_copy(target, part).wait_send()

        @pl.when(row > 0)
        def _():
            for top, bottom in zip(tops, bottoms):
                @pl.when(spot == top)
                def _():
                    for place in range(top - 1, bottom - 1, -1):
                        edge_copy(place).wait_send()

        @pl.when(jnp.logical_and(spot == 0, row > 0))
        def _():
            def sent_down(place, carry):
                for target in range(chips):
                    down_copy(target, place).wait_send()
                return carry

            lax.fori_loop(0, span, sent_down, 0)

        for stream in range(1, len(tops)):
            @pl.when(spot == bottoms[stream - 1])
            def _():
                def sent_mid(place, carry):
                    for target in range(chips):
                        mid_copy(stream, target, place).wait_send()
                    return carry

                lax.fori_loop(0, tops[stream] + 1, sent_mid, 0)

        @pl.when(jnp.logical_not(one_of(bottoms)))
        def _():
            sweep_copy.wait_send()

        for target in others:
            end_copy(target).wait_send()

    for slot, target in enumerate(others):
        pack_copy(me, target, slot).wait_send()
    for turn in range(square_turns):
        square_copy(0, turn).wait_send()
        square_copy(1, turn).wait_send()
    slab_copy(me, ahead, 0).wait_send()
    slab_copy(me, behind, 1).wait_send()
    slab_copy(me, partner, 2).wait_send()
    slab_copy(behind, ahead, 3).wait_send()
    slab_copy(behind, partner, 4).wait_send()
    slab_copy(ahead, partner, 5).wait_send()
    slab_copy(across_ring, partner, 6).wait_send()

    @pl.when(plane < planes - 1)
    def _():
        face_copy(plane + 1).wait_send()


def per_device(basis_flux, owner_cell, clogged, conductance, live_count, coupling, leakage, source):
    arguments = (
        basis_flux, owner_cell, clogged, conductance, live_count, coupling, leakage, source
    )
    planes = lax.axis_size("flow")
    parts = lax.axis_size("trans")
    chips = parts // 2
    rows, order = basis_flux.shape[1:]
    span, depth = planes // 4, 16
    tops = (15, 11, 8, 6, 4)
    streams = len(tops)
    width = order // chips
    turns = width // depth
    row = (1, order)
    piece = (1, width)
    vmem = pl.BlockSpec(memory_space=pltpu.VMEM)
    dma = pltpu.SemaphoreType.DMA
    half = pltpu.VMEM((order, order), BF16)
    return pl.pallas_call(
        functools.partial(kernel, planes, span, chips, rows, order, depth, tops),
        out_shape=jax.ShapeDtypeStruct((1, rows), F32),
        in_specs=[pl.BlockSpec(memory_space=pl.ANY)] * 8,
        out_specs=vmem,
        scratch_shapes=[
            *[pltpu.VMEM(array.shape, array.dtype) for array in arguments],
            dma((len(arguments),)),
            half, half, pltpu.VMEM(row, F32),
            half,
            pltpu.VMEM((parts, 16, rows), F32),
            half,
            pltpu.VMEM((order, order), F32),
            half, half, half, half,
            pltpu.VMEM((2, order), F32),
            pltpu.VMEM((2, order), F32),
            pltpu.VMEM(row, F32),
            pltpu.VMEM((width + depth, order), F32),
            pltpu.VMEM((width + depth, order), F32),
            pltpu.VMEM((streams * width, order), F32),
            pltpu.VMEM((streams * width, order), F32),
            pltpu.VMEM((streams * width, order), BF16),
            pltpu.VMEM((streams * width, order), BF16),
            *[pltpu.VMEM((width, order), BF16) for _ in range(4)],
            pltpu.VMEM(row, F32),
            *[pltpu.VMEM((chips, *piece), F32) for _ in range(3)],
            pltpu.VMEM((streams, chips, *piece), F32),
            pltpu.VMEM((chips, 1, rows), F32),
            pltpu.VMEM((parts, 1, rows), F32),
            pltpu.VMEM(piece, F32),
            pltpu.VMEM((streams, *piece), F32),
            *[pltpu.VMEM(row, F32) for _ in range(4)],
            dma((parts,)), dma((parts,)), dma((parts,)), dma((parts,)), dma, dma,
            dma((2, 4)), dma((2,)),
            dma((turns + 1,)), dma((turns + 1,)),
            dma((streams * turns,)), dma((streams * turns,)),
            dma((2, streams * turns)), dma((2, streams)),
            dma((streams, chips)), dma((chips,)), dma((span, chips)), dma((chips,)),
            dma((span,)), dma, dma((span, chips)), dma((streams, chips)), dma, dma,
            dma((parts,)), dma((chips,)),
        ],
        compiler_params=pltpu.CompilerParams(
            collective_id=0, has_side_effects=True, vmem_limit_bytes=VMEM_LIMIT
        ),
    )(*arguments)


def solution(mesh):
    placed = (
        P("flow", "trans", None),
        P("flow", "trans"),
        P("flow", "trans"),
        P("flow", "trans"),
        P("flow", "trans"),
        P("flow", None),
        P("flow", None),
        P("flow", None),
    )
    return jax.shard_map(
        per_device, mesh=mesh, in_specs=placed, out_specs=P("flow", "trans"), check_vma=False
    )
```

```python
import functools

import jax
import jax.numpy as jnp
from jax import lax
from jax.experimental import pallas as pl
from jax.experimental.pallas import tpu as pltpu
from jax.sharding import PartitionSpec as P

MESH = pl.DeviceIdType.MESH
BF16 = jnp.bfloat16
F32 = jnp.float32
VMEM_LIMIT = 56 * 1024 * 1024


def dot(left, right):
    return jnp.dot(left, right, preferred_element_type=F32)


def split(value):
    high = value.astype(BF16)
    return high, (value - high.astype(F32)).astype(BF16)


def kernel(
    planes, span, chips, rows, order, depth, tops,
    basis_in, owner_in, clogged_in, conductance_in, live_in, coupling_in, leakage_in, source_in,
    pressure,
    basis, owner, clogged, conductance, live, coupling, leakage, source, fetched,
    near_high, near_low, inverse_diag,
    slabs, packs, picked, block, gain_high, gain_low, square, square_low, faces, faces_in, flux_diag,
    panel_in, panel_out, back_in, back_out, back_high, back_low,
    panel_high, panel_low, last_high, last_low,
    level, parts_out, up_pieces, down_pieces, edge_pieces, end_pieces, end_out,
    edge_up, edges, total, swept_in, swept, system_diag,
    slab_send, slab_recv, pack_send, pack_recv, face_send, face_recv, square_send, square_recv,
    panel_send, panel_recv, back_send, back_recv, held_send, held_recv,
    up_send, up_recv, down_send, down_recv,
    edge_send, edge_recv, mid_send, mid_recv, sweep_send, sweep_recv, end_send, end_recv,
):
    plane = lax.axis_index("flow")
    me = lax.axis_index("trans")
    parts = 2 * chips
    chip, core = me // 2, lax.rem(me, 2)
    partner = me + 1 - 2 * core
    before, after = jnp.maximum(plane - 1, 0), jnp.minimum(plane + 1, planes - 1)
    spans = planes // span
    row, spot = plane // span, lax.rem(plane, span)
    row_start = row * span
    last = span - 1
    width = order // chips
    turns = width // depth
    bottoms = tuple(top + 1 for top in tops[1:]) + (0,)
    up_first = jnp.where(row > 0, 0, turns)
    pass_first = jnp.where(jnp.logical_and(row > 0, spot > 0), 0, turns)

    def one_of(places):
        return functools.reduce(jnp.logical_or, [spot == place for place in places])

    first_column = pl.multiple_of(chip * width, width)
    other_chips = [lax.rem(chip + turn, chips) for turn in range(1, chips)]
    step_rows = 256
    steps = order // step_rows

    given = (
        basis_in, owner_in, clogged_in, conductance_in, live_in, coupling_in, leakage_in, source_in
    )
    held = (basis, owner, clogged, conductance, live, coupling, leakage, source)
    fetches = [
        pltpu.make_async_copy(given[index], held[index], fetched.at[index])
        for index in range(len(given))
    ]
    for fetch in fetches:
        fetch.start()

    barrier = pltpu.get_barrier_semaphore()

    def greet(target_plane, target):
        pl.semaphore_signal(barrier, inc=1, device_id=(target_plane, target), device_id_type=MESH)

    for turn in range(1, parts):
        greet(plane, lax.rem(me + turn, parts))

    @pl.when(plane > 0)
    def _():
        greet(plane - 1, me)

    @pl.when(plane < planes - 1)
    def _():
        greet(plane + 1, me)

    @pl.when(jnp.logical_and(core == 1, jnp.logical_and(row > 0, one_of(tops))))
    def _():
        for other in range(chips):
            greet(row_start - 1, other * 2 + 1)

    def slab(index):
        return slabs.at[:, pl.ds(pl.multiple_of(index * rows, rows), rows)]

    for fetch in fetches:
        fetch.wait()
    face = coupling[...]
    position = lax.broadcasted_iota(jnp.int32, (1, rows), 1)
    weight = (
        conductance[...]
        * (1 - clogged[...]).astype(F32)
        * (position < live[...]).astype(F32)
    ).astype(BF16).astype(F32)
    row_id = lax.broadcasted_iota(jnp.int32, (8, rows), 0)
    pack = jnp.where(row_id == 0, weight, owner[...].astype(F32))
    packs[me, 0:8, :] = pack
    turned = pack.T
    column = lax.broadcasted_iota(jnp.int32, (rows, order), 1).astype(F32)
    own_share = jnp.sum(
        jnp.where(turned[:, 1:2] == column, turned[:, 0:1], 0.0) * basis[0].astype(F32),
        axis=0, keepdims=True,
    )
    for index in range(order // rows):
        packs[me, 8 + index : 9 + index, :] = own_share[:, index * rows : (index + 1) * rows]
    slabs[:, pl.ds(pl.multiple_of(me * rows, rows), rows)] = basis[0].astype(F32).T.astype(BF16)

    next_to = jnp.where(plane > 0, 1, 0) + jnp.where(plane < planes - 1, 1, 0)
    sends_up = jnp.logical_and(core == 1, jnp.logical_and(spot == last, row < spans - 1))
    extra = jnp.where(sends_up, chips * len(tops), 0)
    pl.semaphore_wait(barrier, parts - 1 + next_to + extra)

    def slab_copy(index, target, slot):
        return pltpu.make_async_remote_copy(
            slab(index), slab(index), slab_send.at[slot], slab_recv.at[index],
            device_id=(plane, target), device_id_type=MESH,
        )

    def pack_copy(index, target, slot):
        return pltpu.make_async_remote_copy(
            packs.at[index], packs.at[index], pack_send.at[slot], pack_recv.at[index],
            device_id=(plane, target), device_id_type=MESH,
        )

    others = [lax.rem(me + turn, parts) for turn in range(1, parts)]
    for slot, target in enumerate(others):
        pack_copy(me, target, slot).start()
    way = 1 - 2 * core
    ahead = lax.rem(chip + way + chips, chips) * 2 + core
    behind = lax.rem(chip - way + chips, chips) * 2 + core
    across_ring = lax.rem(chip + 2, chips) * 2 + core
    slab_copy(me, ahead, 0).start()
    slab_copy(me, behind, 1).start()
    slab_copy(me, partner, 2).start()

    for other in others:
        pack_copy(other, partner, 0).wait_recv()

    shares = packs[0, 8:16, :]
    for index in range(1, parts):
        shares = shares + packs[index, 8:16, :]
    for index in range(order // rows):
        flux_diag[:, index * rows : (index + 1) * rows] = shares[index : index + 1, :]
    leak = leakage[...]
    schur = face * face / (face + leak + flux_diag[...])
    faces[0:1, :] = face
    faces[1:2, :] = schur

    def face_copy(target):
        return pltpu.make_async_remote_copy(
            faces, faces_in, face_send, face_recv, device_id=(target, me), device_id_type=MESH
        )

    @pl.when(plane < planes - 1)
    def _():
        face_copy(plane + 1).start()

    def pick(index, carry):
        turned = packs[index, 0:8, :].T
        picked[pl.ds(pl.multiple_of(index * rows, rows), rows), :] = jnp.where(
            turned[:, 1:2] == column, turned[:, 0:1], 0.0
        ).astype(BF16)
        return carry

    lax.fori_loop(0, parts, pick, 0)

    def chunk(index):
        return pl.ds(pl.multiple_of(index * step_rows, step_rows), step_rows)

    def from_chip(index, source_chip):
        slab_rows = pl.ds(pl.multiple_of(source_chip * 2 * rows, 2 * rows), 2 * rows)
        return dot(slabs[chunk(index), slab_rows], picked[slab_rows, :])

    def begin(index, carry):
        block[chunk(index), :] = from_chip(index, chip)
        return carry

    def add_chip(source_chip):
        def add(index, carry):
            block[chunk(index), :] = block[chunk(index), :] + from_chip(index, source_chip)
            return carry

        return add

    flip = 1 - 2 * core
    slab_copy(partner, partner, 0).wait_recv()
    lax.fori_loop(0, steps, begin, 0)
    slab_copy(behind, partner, 0).wait_recv()
    slab_copy(behind, ahead, 3).start()
    slab_copy(behind, partner, 4).start()
    slab_copy(ahead, partner, 0).wait_recv()
    slab_copy(ahead, partner, 5).start()
    slab_copy(ahead + flip, partner, 0).wait_recv()
    lax.fori_loop(0, steps, add_chip(ahead // 2), 0)
    slab_copy(across_ring, partner, 0).wait_recv()
    slab_copy(across_ring, partner, 6).start()
    slab_copy(behind + flip, partner, 0).wait_recv()
    lax.fori_loop(0, steps, add_chip(behind // 2), 0)

    @pl.when(plane > 0)
    def _():
        face_copy(plane).wait_recv()

    @pl.when(plane == 0)
    def _():
        faces_in[...] = jnp.zeros_like(faces_in)

    diag = flux_diag[...] + (leak + face + faces_in[0:1, :] - faces_in[1:2, :])
    pivots = 1.0 / diag
    inverse_diag[...] = pivots
    system_diag[...] = diag

    across = lax.broadcasted_iota(jnp.int32, (step_rows, order), 1)
    down = lax.broadcasted_iota(jnp.int32, (step_rows, order), 0)

    def scale(index, carry):
        here = chunk(index)
        whole = block[here, :] + from_chip(index, across_ring // 2)
        gain = jnp.where(across == down + index * step_rows, 0.0, whole * pivots)
        block[here, :] = gain
        gain_high[here, :], gain_low[here, :] = split(gain)
        return carry

    slab_copy(across_ring + flip, partner, 0).wait_recv()
    lax.fori_loop(0, steps, scale, 0)

    square_rows = 256
    half_rows = order // 2
    square_turns = half_rows // square_rows
    own_half = pl.ds(pl.multiple_of(core * half_rows, half_rows), half_rows)
    other_half = pl.ds(pl.multiple_of((1 - core) * half_rows, half_rows), half_rows)

    def square_copy(part, turn):
        ref = square_low if part else square
        here = pl.ds(pl.multiple_of(core * half_rows + turn * square_rows, square_rows), square_rows)
        return pltpu.make_async_remote_copy(
            ref.at[here, :], ref.at[here, :], square_send.at[part, turn], square_recv.at[part],
            device_id=(plane, partner), device_id_type=MESH,
        )

    def squared(turn, carry):
        first_row = turn * square_rows
        here = pl.ds(pl.multiple_of(core * half_rows + first_row, square_rows), square_rows)
        there = pl.ds(pl.multiple_of((1 - core) * half_rows + first_row, square_rows), square_rows)
        high, low = gain_high[here, :], gain_low[here, :]
        value = dot(high, gain_high[...]) + (dot(high, gain_low[...]) + dot(low, gain_high[...]))
        square[here, :], square_low[here, :] = split(value)
        square_copy(0, turn).start()
        square_copy(1, turn).start()
        block[here, :] = value - block[here, :]
        block[there, :] = -block[there, :]
        return carry

    lax.fori_loop(0, square_turns, squared, 0)

    def own_cubic(turn, carry):
        here = chunk(lax.rem(chip + turn, steps))
        block[here, :] = block[here, :] - dot(gain_high[here, own_half], square[own_half, :])
        return carry

    lax.fori_loop(0, steps, own_cubic, 0)
    for part, ref in enumerate((square, square_low)):
        pltpu.make_async_remote_copy(
            ref.at[other_half, :], ref.at[other_half, :],
            square_send.at[part, 0], square_recv.at[part],
            device_id=(plane, partner), device_id_type=MESH,
        ).wait_recv()

    def finish(turn, carry):
        index = lax.rem(chip + turn, steps)
        here = chunk(index)
        add = jnp.where(index // (steps // 2) == core, 0.0, 1.0)
        near = (
            block[here, :]
            - dot(gain_high[here, other_half], square[other_half, :])
            + add * (square[here, :].astype(F32) + square_low[here, :].astype(F32))
        )
        near_high[here, :], near_low[here, :] = split(near)
        return carry

    def remote(source_ref, target_ref, send, recv, target_plane, target):
        return pltpu.make_async_remote_copy(
            source_ref, target_ref, send, recv,
            device_id=(target_plane, target), device_id_type=MESH,
        )

    def apply(value):
        count = value.shape[0]
        scaled = value * inverse_diag[...]
        high = scaled.astype(BF16).astype(F32)
        both = jnp.concatenate([high, scaled - high], axis=0).astype(BF16)
        by_high = dot(both, near_high[...])
        by_low = dot(both[:count], near_low[...])
        return scaled + (by_high[:count] + (by_high[count:] + by_low)), both[:count], both[count:]

    def two_rows(value):
        row_id = lax.broadcasted_iota(jnp.int32, (8, value.shape[1]), 0)
        high = value.astype(BF16).astype(F32)
        return jnp.where(row_id == 0, high, jnp.where(row_id == 1, value - high, 0.0)).astype(BF16)

    def apply_one(value):
        scaled = value * inverse_diag[...]
        both = two_rows(scaled)
        return scaled + jnp.sum(
            dot(both, near_high[...]) + dot(both, near_low[...]), axis=0, keepdims=True
        )

    def by_panel(value, high, low):
        both = two_rows(value)
        return jnp.sum(dot(both, high[...]) + dot(both, low[...]), axis=0, keepdims=True)

    def take(index):
        return pl.ds(pl.multiple_of(index * depth, depth), depth)

    one_hot_row = lax.broadcasted_iota(jnp.int32, (depth, order), 0)
    one_hot_column = lax.broadcasted_iota(jnp.int32, (depth, order), 1)

    def unit_rows(index):
        return jnp.where(
            one_hot_column == one_hot_row + (chip * width + index * depth), 1.0, 0.0
        )

    def back_copy(index):
        return remote(
            back_out.at[take(index), :], back_in.at[take(index), :],
            back_send.at[index], back_recv.at[index], before, me,
        )

    def held_copy(index, half):
        ref = back_low if half else back_high
        return remote(
            ref.at[take(index), :], ref.at[take(index), :],
            held_send.at[half, index], held_recv.at[half, index // turns], plane, partner,
        )

    def stream_turns(stream):
        active = spot <= tops[stream]
        if stream == 0:
            active = jnp.logical_and(active, row < spans - 1)
        return jnp.where(active, turns, 0)

    def end_copy(target):
        return remote(
            end_out.at[target], end_pieces.at[chip], end_send.at[target], end_recv.at[chip],
            plane, target,
        )

    def end_from(source_chip):
        return remote(
            end_out.at[0], end_pieces.at[source_chip], end_send.at[0], end_recv.at[source_chip],
            plane, me,
        )

    def panel_copy(index):
        return remote(
            panel_out.at[take(index), :], panel_in.at[take(index), :],
            panel_send.at[index], panel_recv.at[index], after, me,
        )

    finish(0, 0)

    @pl.when(jnp.logical_and(core == 1, jnp.logical_and(spot == 0, row > 0)))
    def _():
        def first(turn, carry):
            here = pl.ds(pl.multiple_of(first_column + turn * depth, depth), depth)
            unit = unit_rows(turn) * pivots
            near = near_high[here, :].astype(F32) + near_low[here, :].astype(F32)
            panel_out[take(turn), :] = face * (unit + jnp.sum(unit, axis=1, keepdims=True) * near)
            panel_copy(turn).start()
            panel_high[take(turn), :], panel_low[take(turn), :] = split(unit)
            return carry

        lax.fori_loop(0, turns, first, 0)

    lax.fori_loop(1, steps, finish, 0)

    @pl.when(core == 0)
    def _():
        def flow_down(stream, top):
            def flow(turn, carry):
                index = stream * turns + turn

                @pl.when(spot == top)
                def _():
                    back_in[take(index), :] = unit_rows(turn)

                @pl.when(spot < top)
                def _():
                    back_copy(index).wait_recv()

                moved = apply(face * back_in[take(index), :])[0]
                back_out[take(index), :] = moved

                @pl.when(spot > 0)
                def _():
                    back_copy(index).start()

                back_high[take(index), :], back_low[take(index), :] = split(moved)
                held_copy(index, 0).start()
                held_copy(index, 1).start()
                return carry

            return flow

        def drain(stream):
            def wait(turn, carry):
                index = stream * turns + turn

                @pl.when(spot > 0)
                def _():
                    back_copy(index).wait_send()

                held_copy(index, 0).wait_send()
                held_copy(index, 1).wait_send()
                return carry

            return wait

        for stream in range(len(tops) - 1, -1, -1):
            lax.fori_loop(0, stream_turns(stream), flow_down(stream, tops[stream]), 0)
        for stream in range(len(tops) - 1, -1, -1):
            lax.fori_loop(0, stream_turns(stream), drain(stream), 0)
        for target in range(chips):
            end_from(target).wait_recv()
        pressure[...] = (end_pieces[0] + end_pieces[1]) + (end_pieces[2] + end_pieces[3])

    def up_copy(target, part):
        return remote(
            parts_out.at[target], up_pieces.at[chip],
            up_send.at[part, target], up_recv.at[chip],
            row_start + span + tops[part], target * 2 + 1,
        )

    def down_copy(target, place):
        return remote(
            parts_out.at[target], down_pieces.at[chip],
            down_send.at[place, target], down_recv.at[chip],
            row_start - span + place, target * 2 + 1,
        )

    def edge_copy(place):
        return remote(
            edge_up, edge_up, edge_send.at[place], edge_recv, row_start + place, me
        )

    def mid_copy(stream, target, place):
        return remote(
            parts_out.at[target], edge_pieces.at[stream, chip],
            mid_send.at[place, target], mid_recv.at[stream, chip],
            row_start + place, target * 2 + 1,
        )

    sweep_copy = remote(swept, swept_in, sweep_send, sweep_recv, before, me)

    def cut(value, ref, count, size):
        for index in range(count):
            ref[index] = value[:, index * size : (index + 1) * size]

    @pl.when(core == 1)
    def _():
        def flow(index, carry):
            @pl.when(spot > 0)
            def _():
                panel_copy(index).wait_recv()

            @pl.when(index == turns)
            def _():
                @pl.when(spot == 0)
                def _():
                    panel_in[take(index), :] = jnp.zeros((depth, order), F32)

                panel_in[take(index), :] = panel_in[take(index), :] + jnp.where(
                    one_hot_row == 0, source[...], 0.0
                )

            arrived_rows = panel_in[take(index), :]
            scaled = arrived_rows * inverse_diag[...]
            high = scaled.astype(BF16)
            low = (scaled - high.astype(F32)).astype(BF16)
            both = jnp.concatenate([high, low], axis=0)
            def advance(pass_on):
                size = order // 2
                for block in range(order // size):
                    across = slice(block * size, (block + 1) * size)
                    by_high = dot(both, near_high[:, across])
                    by_low = dot(high, near_low[:, across])
                    panel_out[take(index), across] = face[:, across] * (
                        scaled[:, across] + (by_high[:depth] + (by_high[depth:] + by_low))
                    )
                    if pass_on:
                        remote(
                            panel_out.at[take(index), across], panel_in.at[take(index), across],
                            panel_send.at[index], panel_recv.at[index], after, me,
                        ).start()

            @pl.when(spot < last)
            def _():
                advance(True)

            @pl.when(spot == last)
            def _():
                advance(False)

            @pl.when(index < turns)
            def _():
                panel_high[take(index), :] = high
                panel_low[take(index), :] = low

                @pl.when(spot == last)
                def _():
                    last_high[take(index), :], last_low[take(index), :] = split(
                        panel_out[take(index), :]
                    )

            return carry

        lax.fori_loop(pass_first, turns + 1, flow, 0)
        level[...] = jnp.where(chip == 0, panel_in[width : width + 1, :], 0.0)

        def gather_pieces(pieces, sems):
            for target in range(chips):
                remote(
                    parts_out.at[target], pieces.at[target], end_send.at[0], sems.at[target],
                    plane, me,
                ).wait_recv()
            return (pieces[0] + pieces[1]) + (pieces[2] + pieces[3])

        @pl.when(jnp.logical_and(row > 0, one_of(tops)))
        def _():
            edge_up[...] = gather_pieces(up_pieces, up_recv)

        @pl.when(jnp.logical_and(spot == last, row < spans - 1))
        def _():
            @pl.when(row == 0)
            def _():
                parts_out[...] = jnp.zeros_like(parts_out)

            @pl.when(row > 0)
            def _():
                cut(by_panel(edge_up[...], last_high, last_low), parts_out, chips, width)

            parts_out[chip] = parts_out[chip] + panel_out[
                width : width + 1, pl.ds(first_column, width)
            ]
            for part in range(len(tops)):
                for target in range(chips):
                    up_copy(target, part).start()

        @pl.when(row > 0)
        def _():
            for top, bottom in zip(tops, bottoms):
                @pl.when(spot == top)
                def _():
                    for place in range(top - 1, bottom - 1, -1):
                        edge_copy(place).start()

            @pl.when(jnp.logical_not(one_of(tops)))
            def _():
                edge_copy(0).wait_recv()

            level[...] = level[...] + system_diag[...] * by_panel(
                edge_up[...], panel_high, panel_low
            )

        @pl.when(jnp.logical_not(one_of(tops)))
        def _():
            sweep_copy.wait_recv()
            level[...] = level[...] + face * swept_in[...]

        swept[...] = apply_one(level[...])

        @pl.when(jnp.logical_not(one_of(bottoms)))
        def _():
            sweep_copy.start()

        for stream in range(1, len(tops)):
            @pl.when(spot == bottoms[stream - 1])
            def _():
                cut(swept[...], parts_out, chips, width)

                def send_mid(place, carry):
                    for target in range(chips):
                        mid_copy(stream, target, place).start()
                    return carry

                lax.fori_loop(0, tops[stream] + 1, send_mid, 0)

        def arrived(stream):
            here = pl.ds(stream * width, width)
            for half, ref in enumerate((back_high, back_low)):
                remote(
                    ref.at[here, :], ref.at[here, :],
                    held_send.at[half, 0], held_recv.at[half, stream], plane, me,
                ).wait_recv()

        def by_stream(stream):
            here = slice(stream * width, (stream + 1) * width)
            return by_panel(edges[stream], back_high.at[here, :], back_low.at[here, :])

        total[...] = swept[...]
        for stream in range(len(tops) - 1, -1, -1):
            @pl.when(stream_turns(stream) > 0)
            def _():
                arrived(stream)

        for stream in range(1, len(tops)):
            @pl.when(spot <= tops[stream])
            def _():
                edges[stream] = gather_pieces(edge_pieces.at[stream], mid_recv.at[stream])
                total[...] = total[...] + by_stream(stream)

        @pl.when(row < spans - 1)
        def _():
            edges[0] = gather_pieces(down_pieces, down_recv)
            total[...] = total[...] + by_stream(0)

        @pl.when(jnp.logical_and(spot == 0, row > 0))
        def _():
            cut(total[...], parts_out, chips, width)

            def send_down(place, carry):
                for target in range(chips):
                    down_copy(target, place).start()
                return carry

            lax.fori_loop(0, span, send_down, 0)

        cut(total[...], end_out, parts, rows)
        for target in others:
            end_copy(target).start()
        end_pieces[chip] = end_out[me]
        for other in other_chips:
            end_from(other).wait_recv()
        pressure[...] = (end_pieces[0] + end_pieces[1]) + (end_pieces[2] + end_pieces[3])

        @pl.when(spot < last)
        def _():
            def drain(index, carry):
                panel_copy(index).wait_send()
                return carry

            lax.fori_loop(up_first, turns + 1, drain, 0)

        @pl.when(jnp.logical_and(spot == last, row < spans - 1))
        def _():
            for part in range(len(tops)):
                for target in range(chips):
                    up_copy(target, part).wait_send()

        @pl.when(row > 0)
        def _():
            for top, bottom in zip(tops, bottoms):
                @pl.when(spot == top)
                def _():
                    for place in range(top - 1, bottom - 1, -1):
                        edge_copy(place).wait_send()

        @pl.when(jnp.logical_and(spot == 0, row > 0))
        def _():
            def sent_down(place, carry):
                for target in range(chips):
                    down_copy(target, place).wait_send()
                return carry

            lax.fori_loop(0, span, sent_down, 0)

        for stream in range(1, len(tops)):
            @pl.when(spot == bottoms[stream - 1])
            def _():
                def sent_mid(place, carry):
                    for target in range(chips):
                        mid_copy(stream, target, place).wait_send()
                    return carry

                lax.fori_loop(0, tops[stream] + 1, sent_mid, 0)

        @pl.when(jnp.logical_not(one_of(bottoms)))
        def _():
            sweep_copy.wait_send()

        for target in others:
            end_copy(target).wait_send()

    for slot, target in enumerate(others):
        pack_copy(me, target, slot).wait_send()
    for turn in range(square_turns):
        square_copy(0, turn).wait_send()
        square_copy(1, turn).wait_send()
    slab_copy(me, ahead, 0).wait_send()
    slab_copy(me, behind, 1).wait_send()
    slab_copy(me, partner, 2).wait_send()
    slab_copy(behind, ahead, 3).wait_send()
    slab_copy(behind, partner, 4).wait_send()
    slab_copy(ahead, partner, 5).wait_send()
    slab_copy(across_ring, partner, 6).wait_send()

    @pl.when(plane < planes - 1)
    def _():
        face_copy(plane + 1).wait_send()


def per_device(basis_flux, owner_cell, clogged, conductance, live_count, coupling, leakage, source):
    arguments = (
        basis_flux, owner_cell, clogged, conductance, live_count, coupling, leakage, source
    )
    planes = lax.axis_size("flow")
    parts = lax.axis_size("trans")
    chips = parts // 2
    rows, order = basis_flux.shape[1:]
    span, depth = planes // 4, 16
    tops = (15, 11, 8, 6, 4)
    streams = len(tops)
    width = order // chips
    turns = width // depth
    row = (1, order)
    piece = (1, width)
    vmem = pl.BlockSpec(memory_space=pltpu.VMEM)
    dma = pltpu.SemaphoreType.DMA
    half = pltpu.VMEM((order, order), BF16)
    return pl.pallas_call(
        functools.partial(kernel, planes, span, chips, rows, order, depth, tops),
        out_shape=jax.ShapeDtypeStruct((1, rows), F32),
        in_specs=[pl.BlockSpec(memory_space=pl.ANY)] * 8,
        out_specs=vmem,
        scratch_shapes=[
            *[pltpu.VMEM(array.shape, array.dtype) for array in arguments],
            dma((len(arguments),)),
            half, half, pltpu.VMEM(row, F32),
            half,
            pltpu.VMEM((parts, 16, rows), F32),
            half,
            pltpu.VMEM((order, order), F32),
            half, half, half, half,
            pltpu.VMEM((2, order), F32),
            pltpu.VMEM((2, order), F32),
            pltpu.VMEM(row, F32),
            pltpu.VMEM((width + depth, order), F32),
            pltpu.VMEM((width + depth, order), F32),
            pltpu.VMEM((streams * width, order), F32),
            pltpu.VMEM((streams * width, order), F32),
            pltpu.VMEM((streams * width, order), BF16),
            pltpu.VMEM((streams * width, order), BF16),
            *[pltpu.VMEM((width, order), BF16) for _ in range(4)],
            pltpu.VMEM(row, F32),
            *[pltpu.VMEM((chips, *piece), F32) for _ in range(3)],
            pltpu.VMEM((streams, chips, *piece), F32),
            pltpu.VMEM((chips, 1, rows), F32),
            pltpu.VMEM((parts, 1, rows), F32),
            pltpu.VMEM(piece, F32),
            pltpu.VMEM((streams, *piece), F32),
            *[pltpu.VMEM(row, F32) for _ in range(4)],
            dma((parts,)), dma((parts,)), dma((parts,)), dma((parts,)), dma, dma,
            dma((2, 4)), dma((2,)),
            dma((turns + 1,)), dma((turns + 1,)),
            dma((streams * turns,)), dma((streams * turns,)),
            dma((2, streams * turns)), dma((2, streams)),
            dma((streams, chips)), dma((chips,)), dma((span, chips)), dma((chips,)),
            dma((span,)), dma, dma((span, chips)), dma((streams, chips)), dma, dma,
            dma((parts,)), dma((chips,)),
        ],
        compiler_params=pltpu.CompilerParams(
            collective_id=0, has_side_effects=True, vmem_limit_bytes=VMEM_LIMIT
        ),
    )(*arguments)


def solution(mesh):
    placed = (
        P("flow", "trans", None),
        P("flow", "trans"),
        P("flow", "trans"),
        P("flow", "trans"),
        P("flow", "trans"),
        P("flow", None),
        P("flow", None),
        P("flow", None),
    )
    return jax.shard_map(
        per_device, mesh=mesh, in_specs=placed, out_specs=P("flow", "trans"), check_vma=False
    )
```
